32 devices in a mesh: shard: 4 (over x, core), ctx: 4 (over z), tp: 2 (over y).
Axes of the slice: x: 2, y: 2, z: 4, core: 2. Of those that a mesh axis runs over, the one named last changes fastest.
Arguments:
- tokens: bfloat16 [8, 2048, 1280], P('shard', 'ctx'), may hold values from -6 to 6
- cotangent: bfloat16 [8, 2048, 1280], P('shard', 'ctx'), may hold values from -6 to 6
- doc_lengths: int32 [8, 4], P('shard'), may hold values from 1 to 2045, as said below
- norm_gains: bfloat16 [2, 2, 1280], P(None, None, 'shard'), may hold values from 0.099609375 to 1.8984375
- norm_biases: bfloat16 [2, 4, 1280], P(None, None, 'shard'), may hold values from -1.796875 to 1.796875
- qkv_weight: bfloat16 [2, 3, 1280, 1280], P(None, None, 'shard', 'tp'), may hold values from -0.15625 to 0.15625
- qv_bias: bfloat16 [2, 2, 1280], P(None, None, 'tp'), may hold values from -1.796875 to 1.796875
- proj_weight: bfloat16 [2, 1280, 1280], P(None, 'tp', 'shard'), may hold values from -0.625 to 0.625
- fc_weight: bfloat16 [2, 1280, 5120], P(None, 'shard', 'tp'), may hold values from -0.15625 to 0.15625
- fc_bias: bfloat16 [2, 5120], P(None, 'tp'), may hold values from -1.796875 to 1.796875
- out_weight: bfloat16 [2, 5120, 1280], P(None, 'tp', 'shard'), may hold values from -0.078125 to 0.078125
Outputs:
- output: bfloat16 [8, 2048, 1280], P('shard', 'ctx')
- token_grad: float32 [8, 2048, 1280], P('shard', 'ctx')
- norm_gains_grad: float32 [2, 2, 1280], P(None, None, 'shard')
- norm_biases_grad: float32 [2, 4, 1280], P(None, None, 'shard')
- qkv_weight_grad: float32 [2, 3, 1280, 1280], P(None, None, 'shard', 'tp')
- qv_bias_grad: float32 [2, 2, 1280], P(None, None, 'tp')
- proj_weight_grad: float32 [2, 1280, 1280], P(None, 'tp', 'shard')
- fc_weight_grad: float32 [2, 1280, 5120], P(None, 'shard', 'tp')
- fc_bias_grad: float32 [2, 5120], P(None, 'tp')
- out_weight_grad: float32 [2, 5120, 1280], P(None, 'tp', 'shard')
The draws below stay inside these ranges and needn't reach their ends.
Inputs may be any that keep to these rules, and one draw needn't show every extreme that they name: `doc_lengths`: each row sums to 2048. Among the 2 sequences of each index of shard, one document starts within the first 512 positions of its sequence and ends within the last 512.
All inputs are finite; a program needn't handle non-finite values.
Results may differ from the reference program's by a relative error of at most 0.018.
Values may be sent and summed in bfloat16 or wider, within the bound.
No kernel may reach another device: no remote copies, remote signals or barrier semaphores. Data moves between devices by JAX's collectives and lax.ppermute only.
A program may use at most 320 MiB of HBM per device.

```python
import math
import jax
import jax.numpy as jnp
from jax import lax

D = 1280
HEADS = 20
HD = 64
FF = 5120
LAYERS = 2
SEQ_LEN = 2048
WINDOW = 1024
DOCS = 4
SEQ_DEV = 2
BLOCK_LEN = 512
SEQS = 8


def draw_doc_lengths(key, part):
    key = jax.random.fold_in(key, 7)
    seq_keys = jax.random.split(jax.random.fold_in(key, 1), SEQS)
    group_pick = jax.random.randint(jax.random.fold_in(key, 2), (SEQS // SEQ_DEV,), 0, SEQ_DEV)
    row_ids = jnp.arange(SEQS, dtype=jnp.int32)
    chosen = row_ids % SEQ_DEV == jnp.repeat(group_pick, SEQ_DEV)
    extreme = row_ids == group_pick[0]

    def one_row(row_key, long_doc, widest):
        free_key, head_key, tail_key = jax.random.split(row_key, 3)
        free_cuts = jax.random.permutation(free_key, SEQ_LEN - 1)[:DOCS - 1].astype(jnp.int32) + 1
        head_cuts = jax.random.permutation(head_key, BLOCK_LEN - 1)[:DOCS - 2].astype(jnp.int32) + 1
        tail_cut = SEQ_LEN - BLOCK_LEN + 1 + jax.random.randint(tail_key, (1,), 0, BLOCK_LEN - 1).astype(jnp.int32)
        forced = jnp.concatenate([head_cuts, tail_cut])
        packed_cuts = jnp.arange(1, DOCS, dtype=jnp.int32)
        cuts = jnp.sort(jnp.where(long_doc, forced, free_cuts))
        cuts = jnp.where(widest, packed_cuts, cuts)
        bounds = jnp.concatenate([jnp.zeros((1,), jnp.int32), cuts, jnp.full((1,), SEQ_LEN, jnp.int32)])
        return bounds[1:] - bounds[:-1]
    return jax.vmap(one_row)(seq_keys, chosen, extreme).astype(jnp.int32)


def block_levels(rng, extent, cuts, low, high):
    def one(position, blocks):
        draws = jax.random.uniform(jax.random.fold_in(jax.random.fold_in(rng, 6), position), (blocks,), jnp.float32, low / len(cuts), high / len(cuts))
        return jnp.repeat(jnp.exp(draws), extent[position] // blocks).reshape((-1,) + (1,) * (len(extent) - position - 1))

    level = one(*cuts[0])
    for cut in cuts[1:]:
        level = level * one(*cut)
    return level


def noise(rng, extent, deviation, bound, shards=(), kind=jnp.bfloat16):
    values = jax.random.normal(rng, extent, jnp.float32) * deviation
    if len(shards) > 0:
        values = block_levels(rng, extent, shards, -0.22, 0.18) * values
    return jnp.clip(values, min=-bound, max=bound).astype(kind)


def setup_inputs(seed: int = 0) -> dict:
    keys = jax.random.split(jax.random.key(seed), 12)
    return {
        "tokens": noise(keys[0], (SEQS, SEQ_LEN, D), 1.0, 6.0, ((0, 4), (1, 4))),
        "cotangent": noise(keys[1], (SEQS, SEQ_LEN, D), 1.0, 6.0, ((0, 4), (1, 4))),
        "doc_lengths": draw_doc_lengths(jax.random.fold_in(keys[11], 71), 0),
        "norm_gains": jnp.clip(1.0 + 0.18 * jax.random.normal(keys[3], (LAYERS, 2, D), jnp.float32), 0.099609375, 1.8984375).astype(jnp.bfloat16),
        "norm_biases": noise(keys[4], (LAYERS, 4, D), 0.3, 1.796875, ((2, 4),)),
        "qkv_weight": noise(keys[5], (LAYERS, 3, D, D), D ** -0.5, 0.15625, ((2, 4), (3, 2))),
        "qv_bias": noise(keys[6], (LAYERS, 2, D), 0.3, 1.796875, ((2, 2),)),
        "proj_weight": noise(keys[7], (LAYERS, D, D), (D // 16) ** -0.5, 0.625, ((1, 2), (2, 4))),
        "fc_weight": noise(keys[8], (LAYERS, D, FF), D ** -0.5, 0.15625, ((1, 4), (2, 2))),
        "fc_bias": noise(keys[9], (LAYERS, FF), 0.3, 1.796875, ((1, 2),)),
        "out_weight": noise(keys[10], (LAYERS, FF, D), FF ** -0.5, 0.078125, ((1, 2), (2, 4))),
    }


@jax.custom_vjp
def low(v):
    return lax.optimization_barrier(v.astype(jnp.bfloat16)).astype(jnp.float32)

@jax.custom_vjp
def low_back(v):
    return v

def low_keep(v):
    return (low(v), None)

def low_pass(kept, grad):
    return (grad,)

def back_keep(v):
    return (v, None)

def back_low(kept, grad):
    return (low(grad),)
low.defvjp(low_keep, low_pass)
low_back.defvjp(back_keep, back_low)
norm_eps = 1e-05
masked_score = -1e+30

def product(left_side, right_side):
    return jnp.dot(left_side, right_side, preferred_element_type=jnp.float32, precision=lax.Precision.HIGHEST)

def layer_norm(hidden, norm_gain, norm_shift):
    row_mean = lax.optimization_barrier(jnp.mean(hidden, axis=-1, keepdims=True))
    centred = hidden - row_mean
    variance = lax.optimization_barrier(jnp.mean(centred * centred, axis=-1, keepdims=True))
    return centred * lax.rsqrt(variance + norm_eps) * norm_gain + norm_shift

def head_attention(allowed):
    score_scale = HD ** (-0.5)

    def run_head(pieces):
        q_head, k_head, v_head = pieces
        scores = low_back(jnp.einsum('gqd,gkd->gqk', q_head, k_head, precision=lax.Precision.HIGHEST) * score_scale)
        scores = jnp.where(allowed, scores, masked_score)
        top_score = lax.optimization_barrier(jnp.max(scores, axis=-1, keepdims=True))
        weights = jnp.exp(scores - top_score)
        attn_probs = low(weights / lax.optimization_barrier(jnp.sum(weights, axis=-1, keepdims=True)))
        return jnp.einsum('gqk,gkd->gqd', attn_probs, v_head, precision=lax.Precision.HIGHEST)
    return jax.checkpoint(run_head)

def one_layer(hidden, params, layer_index, allowed):
    norm_gains, norm_biases, qkv_weight, qv_bias, proj_weight, fc_weight, fc_bias, out_weight = params
    row_count = hidden.shape[0]
    group_size = allowed.shape[0]
    attn_in = low(layer_norm(hidden, norm_gains[layer_index, 0], norm_biases[layer_index, 0]))
    query_rows = low(low_back(product(attn_in, qkv_weight[layer_index, 0]) + qv_bias[layer_index, 0]))
    key_rows = low(low_back(product(attn_in, qkv_weight[layer_index, 1])))
    value_rows = low(low_back(product(attn_in, qkv_weight[layer_index, 2]) + qv_bias[layer_index, 1]))

    def split_heads(tensor):
        return tensor.reshape(group_size, SEQ_LEN, HEADS, HD).transpose(2, 0, 1, 3)
    attn_mixed = lax.map(head_attention(allowed), (split_heads(query_rows), split_heads(key_rows), split_heads(value_rows)))
    attn_mixed = low(low_back(attn_mixed.transpose(1, 2, 0, 3).reshape(row_count, HEADS * HD)))
    middle = hidden + low_back(product(attn_mixed, proj_weight[layer_index])) + norm_biases[layer_index, 1]
    mlp_in = low(layer_norm(middle, norm_gains[layer_index, 1], norm_biases[layer_index, 2]))
    pre_act = low_back(product(mlp_in, fc_weight[layer_index]) + fc_bias[layer_index])
    activated = low(jax.nn.gelu(pre_act, approximate=True))
    return middle + low_back(product(activated, out_weight[layer_index])) + norm_biases[layer_index, 3]

def run_group(params, pieces):
    hidden, visible_mask = pieces
    for layer_index in range(LAYERS):
        hidden = one_layer(hidden, params, layer_index, visible_mask)
    return hidden

def reference(tokens, cotangent, doc_lengths, norm_gains, norm_biases, qkv_weight, qv_bias, proj_weight, fc_weight, fc_bias, out_weight):
    group_size = math.gcd(SEQS, max(1, 4096 // SEQ_LEN))
    group_count = SEQS // group_size
    doc_ends = jnp.cumsum(doc_lengths, axis=1).astype(jnp.int32)
    positions = jnp.arange(SEQ_LEN, dtype=jnp.int32)
    doc_of = lax.optimization_barrier(jnp.sum((doc_ends[:, None, :] <= positions[None, :, None]).astype(jnp.int32), axis=-1))
    distance = positions[:, None] - positions[None, :]
    allowed = (doc_of[:, :, None] == doc_of[:, None, :]) & ((distance >= 0) & (distance < WINDOW))[None, :, :]
    allowed = allowed.reshape(group_count, group_size, SEQ_LEN, SEQ_LEN)
    params = tuple((array.astype(jnp.float32) for array in (norm_gains, norm_biases, qkv_weight, qv_bias, proj_weight, fc_weight, fc_bias, out_weight)))
    checked = jax.checkpoint(run_group)

    def forward(inputs, weights):
        blocks = inputs.reshape(group_count, group_size * SEQ_LEN, D)
        result = lax.map(lambda pieces: checked(weights, pieces), (blocks, allowed))
        return result.reshape(SEQS, SEQ_LEN, D)
    output, pullback = jax.vjp(forward, tokens.astype(jnp.float32), params)
    token_grad, grads = pullback(cotangent.astype(jnp.float32))
    return (output.astype(jnp.bfloat16), token_grad, grads[0], grads[1], grads[2], grads[3], grads[4], grads[5], grads[6], grads[7])
```

```python
import jax
import jax.numpy as jnp
from jax import lax
from jax.experimental import pallas as pl
from jax.experimental.pallas import tpu as pltpu
from jax.sharding import PartitionSpec as P

HD = 64
WINDOW = 1024
TILE = 256
masked_score = -1e30


def contract(left_side, right_side, left_dim, right_dim):
    return lax.dot_general(
        left_side, right_side, (((left_dim,), (right_dim,)), ((), ())),
        preferred_element_type=jnp.float32,
    )


def half_mask(shape, half):
    lane = lax.broadcasted_iota(jnp.int32, shape, 1)
    return (lane < HD) if half == 0 else (lane >= HD)


def forward_kernel(q_ref, k_ref, v_ref, low_ref, mixed_ref, total_ref):
    block_len = q_ref.shape[1]
    span = WINDOW + TILE
    eye = lax.broadcasted_iota(jnp.int32, (TILE, TILE), 0) == lax.broadcasted_iota(
        jnp.int32, (TILE, TILE), 1
    )
    for block in range(block_len // TILE):
        rows = pl.ds(block * TILE, TILE)
        window = pl.ds(block * TILE, span)
        queries = q_ref[0, rows, :] * jnp.asarray(HD ** (-0.5), jnp.bfloat16)
        keys = k_ref[0, window, :]
        values = v_ref[0, window, :]
        low_pos = low_ref[0, rows, :] - block * TILE
        key_pos = lax.broadcasted_iota(jnp.int32, (TILE, span), 1)
        query_pos = lax.broadcasted_iota(jnp.int32, (TILE, TILE), 0) + WINDOW
        allowed = key_pos >= low_pos
        causal = key_pos[:, WINDOW:] <= query_pos
        mixed = jnp.zeros((TILE, 2 * HD), jnp.float32)
        for half in range(2):
            scores = contract(
                jnp.where(half_mask(queries.shape, half), queries, 0), keys, 1, 1
            )
            early = jnp.where(allowed[:, :WINDOW], scores[:, :WINDOW], masked_score)
            late = jnp.where(allowed[:, WINDOW:] & causal, scores[:, WINDOW:], masked_score)
            top_score = jnp.maximum(
                jnp.max(early, axis=1, keepdims=True), jnp.max(late, axis=1, keepdims=True)
            )
            early = jnp.exp(early - top_score)
            late = jnp.exp(late - top_score)
            row_total = jnp.sum(early, axis=1, keepdims=True) + jnp.sum(
                late, axis=1, keepdims=True
            )
            part = contract(early.astype(jnp.bfloat16), values[:WINDOW], 1, 0) + contract(
                late.astype(jnp.bfloat16), values[WINDOW:], 1, 0
            )
            part = part * (1.0 / row_total)
            mixed = jnp.where(half_mask(mixed.shape, half), part, mixed)
            log_total = top_score + jnp.log(row_total)
            total_ref[0, 0, half : half + 1, rows] = jnp.sum(
                jnp.where(eye, log_total, 0.0), axis=0, keepdims=True
            )
        mixed_ref[0, rows, :] = mixed.astype(jnp.bfloat16)


def attention_forward(queries, keys, values, low_pos):
    groups, block_len, width = queries.shape
    key_len = keys.shape[1]
    pairs = width // (2 * HD)
    pick = lambda seq, pair: (seq, 0, pair)
    return pl.pallas_call(
        forward_kernel,
        grid=(groups, pairs),
        in_specs=[
            pl.BlockSpec((1, block_len, 2 * HD), pick),
            pl.BlockSpec((1, key_len, 2 * HD), pick),
            pl.BlockSpec((1, key_len, 2 * HD), pick),
            pl.BlockSpec((1, block_len, 1), lambda seq, pair: (seq, 0, 0)),
        ],
        out_specs=[
            pl.BlockSpec((1, block_len, 2 * HD), pick),
            pl.BlockSpec((1, 1, 2, block_len), lambda seq, pair: (seq, pair, 0, 0)),
        ],
        out_shape=[
            jax.ShapeDtypeStruct((groups, block_len, width), jnp.bfloat16),
            jax.ShapeDtypeStruct((groups, pairs, 2, block_len), jnp.float32),
        ],
        compiler_params=pltpu.CompilerParams(vmem_limit_bytes=40 << 20),
        cost_estimate=pl.CostEstimate(
            flops=16 * groups * pairs * block_len * (WINDOW + TILE) * HD,
            bytes_accessed=4 * groups * width * (block_len + key_len),
            transcendentals=2 * groups * pairs * block_len * (WINDOW + TILE),
        ),
    )(queries, keys, values, low_pos[:, :, None])


def backward_kernel(
    q_ref, k_ref, v_ref, mixed_ref, grad_ref, total_ref, low_ref,
    gq_ref, gk_ref, gv_ref, gk_sum, gv_sum,
):
    block_len = q_ref.shape[1]
    span = WINDOW + TILE
    scale = HD ** (-0.5)
    gk_sum[...] = jnp.zeros_like(gk_sum)
    gv_sum[...] = jnp.zeros_like(gv_sum)
    eye = lax.broadcasted_iota(jnp.int32, (TILE, TILE), 0) == lax.broadcasted_iota(
        jnp.int32, (TILE, TILE), 1
    )
    for block in range(block_len // TILE):
        rows = pl.ds(block * TILE, TILE)
        window = pl.ds(block * TILE, span)
        queries = q_ref[0, rows, :] * jnp.asarray(scale, jnp.bfloat16)
        keys = k_ref[0, window, :]
        values = v_ref[0, window, :]
        grads = grad_ref[0, rows, :]
        product = grads.astype(jnp.float32) * mixed_ref[0, rows, :].astype(jnp.float32)
        low_pos = low_ref[0, :, rows] - block * TILE
        key_pos = lax.broadcasted_iota(jnp.int32, (span, TILE), 0)
        query_pos = lax.broadcasted_iota(jnp.int32, (TILE, TILE), 1) + WINDOW
        allowed = key_pos >= low_pos
        late_allowed = allowed[WINDOW:] & (key_pos[WINDOW:] <= query_pos)
        keys_t = jnp.transpose(keys)
        gq_parts = []
        for half in range(2):
            mask = half_mask(queries.shape, half)
            q_half = jnp.where(mask, queries, 0)
            g_half = jnp.where(mask, grads, 0)
            delta = jnp.sum(jnp.where(mask, product, 0.0), axis=1, keepdims=True)
            delta = jnp.sum(jnp.where(eye, delta, 0.0), axis=0, keepdims=True)
            log_total = total_ref[0, 0, half : half + 1, rows]
            scores = contract(keys, q_half, 1, 1)
            probs = jnp.concatenate(
                [
                    jnp.where(allowed[:WINDOW], jnp.exp(scores[:WINDOW] - log_total), 0.0),
                    jnp.where(late_allowed, jnp.exp(scores[WINDOW:] - log_total), 0.0),
                ]
            )
            grad_probs = contract(values, g_half, 1, 1)
            grad_scores = (probs * (grad_probs - delta)).astype(jnp.bfloat16)
            gv_sum[window, :] += contract(probs.astype(jnp.bfloat16), g_half, 1, 0)
            gk_sum[window, :] += contract(grad_scores, q_half, 1, 0)
            gq_parts.append(contract(keys_t[half * HD : (half + 1) * HD], grad_scores, 1, 0))
        gq = jnp.transpose(jnp.concatenate(gq_parts)) * scale
        gq_ref[0, rows, :] = gq.astype(jnp.bfloat16)
    gk_ref[0] = gk_sum[...].astype(jnp.bfloat16)
    gv_ref[0] = gv_sum[...].astype(jnp.bfloat16)


def attention_backward(queries, keys, values, mixed, grads, log_total, low_pos):
    groups, block_len, width = queries.shape
    key_len = keys.shape[1]
    pairs = width // (2 * HD)
    pick = lambda seq, pair: (seq, 0, pair)
    q_spec = pl.BlockSpec((1, block_len, 2 * HD), pick)
    k_spec = pl.BlockSpec((1, key_len, 2 * HD), pick)
    return pl.pallas_call(
        backward_kernel,
        grid=(groups, pairs),
        in_specs=[
            q_spec, k_spec, k_spec, q_spec, q_spec,
            pl.BlockSpec((1, 1, 2, block_len), lambda seq, pair: (seq, pair, 0, 0)),
            pl.BlockSpec((1, 1, block_len), lambda seq, pair: (seq, 0, 0)),
        ],
        out_specs=[q_spec, k_spec, k_spec],
        out_shape=[
            jax.ShapeDtypeStruct(queries.shape, jnp.bfloat16),
            jax.ShapeDtypeStruct(keys.shape, jnp.bfloat16),
            jax.ShapeDtypeStruct(keys.shape, jnp.bfloat16),
        ],
        scratch_shapes=[
            pltpu.VMEM((key_len, 2 * HD), jnp.float32),
            pltpu.VMEM((key_len, 2 * HD), jnp.float32),
        ],
        compiler_params=pltpu.CompilerParams(vmem_limit_bytes=40 << 20),
        cost_estimate=pl.CostEstimate(
            flops=40 * groups * pairs * block_len * (WINDOW + TILE) * HD,
            bytes_accessed=8 * groups * width * (block_len + key_len),
            transcendentals=2 * groups * pairs * block_len * (WINDOW + TILE),
        ),
    )(queries, keys, values, mixed, grads, log_total, low_pos[:, None, :])


norm_eps = 1e-05


def mate(value):
    count = lax.axis_size("shard")
    return lax.ppermute(value, "shard", [(i, i ^ 1) for i in range(count)])


def chip_shift(value, steps, half_only=False):
    count = lax.axis_size("shard")
    if not half_only:
        return lax.ppermute(value, "shard", [(i, (i + 2 * steps) % count) for i in range(count)])
    tp_count = lax.axis_size("tp")
    pairs = [
        (i * tp_count + i % 2, ((i + 2 * steps) % count) * tp_count + i % 2) for i in range(count)
    ]
    return lax.ppermute(value, ("shard", "tp"), pairs)


def cross_out(value):
    pairs = [(i * 2 + i % 2, i * 2 + 1 - i % 2) for i in range(lax.axis_size("shard"))]
    return lax.ppermute(value, ("shard", "tp"), pairs)


def cross_home(value):
    pairs = [(i * 2 + 1 - i % 2, i * 2 + i % 2) for i in range(lax.axis_size("shard"))]
    return lax.ppermute(value, ("shard", "tp"), pairs)


def other_tp(value):
    return lax.ppermute(value, "tp", [(0, 1), (1, 0)])


def onward(value):
    count = lax.axis_size("ctx")
    return lax.ppermute(value, "ctx", [(i, i + 1) for i in range(count - 1)])


def backward_step(value):
    count = lax.axis_size("ctx")
    return lax.ppermute(value, "ctx", [(i + 1, i) for i in range(count - 1)])


def tie(first, second):
    return lax.optimization_barrier((first, second))


def ordered(own, others, chip):
    if len(others) == 1:
        return jnp.where(
            chip == 0, jnp.stack([own, others[0]]), jnp.stack([others[0], own])
        )
    count = len(others) + 1
    whole = jnp.stack([own] + others)
    return jnp.take(whole, (chip - jnp.arange(count)) % count, axis=0)


class Place:
    def __init__(self):
        shard = lax.axis_index("shard")
        self.chips = lax.axis_size("shard") // 2
        self.chip = shard // 2
        self.core = shard % 2
        self.tp = lax.axis_index("tp")
        self.ctx = lax.axis_index("ctx")
        self.home = self.core == self.tp


def gather_core_first(piece, place):
    both = ordered(piece, [mate(piece)], place.core)
    across = cross_out(both)
    yield across
    pair = jnp.where(place.home, both, across)
    others = [chip_shift(pair, steps) for steps in range(1, place.chips)]
    yield tuple(others)
    whole = ordered(pair, others, place.chip)
    yield whole.reshape(-1, piece.shape[1])


def gather_chip_first(piece, place):
    others = [chip_shift(piece, steps) for steps in range(1, place.chips)]
    yield tuple(others)
    own = ordered(piece, others, place.chip)
    both = ordered(own, [mate(own)], place.core)
    across = cross_out(both)
    yield across
    whole = jnp.where(place.home, both, across)
    yield jnp.swapaxes(whole, 0, 1).reshape(-1, piece.shape[1])


def dot_f32(left_side, right_side):
    return jnp.dot(left_side, right_side, preferred_element_type=jnp.float32)


def dot_first(left_side, right_side):
    return contract(left_side, right_side, 0, 0)


def dot_second(left_side, right_side):
    return contract(left_side, right_side, 1, 1)


def norm_forward(hidden, norm_gain, norm_shift):
    row_mean = jnp.mean(hidden, axis=-1, keepdims=True)
    centred = hidden - row_mean
    variance = jnp.mean(centred * centred, axis=-1, keepdims=True)
    inv_std = lax.rsqrt(variance + norm_eps)
    norm_hat = centred * inv_std
    return ((norm_hat * norm_gain + norm_shift).astype(jnp.bfloat16), norm_hat, inv_std)


def norm_backward(grad_out, norm_hat, inv_std, norm_gain):
    scaled = grad_out * norm_gain
    mean_one = jnp.mean(scaled, axis=-1, keepdims=True)
    mean_two = jnp.mean(scaled * norm_hat, axis=-1, keepdims=True)
    grad_input = inv_std * (scaled - mean_one - norm_hat * mean_two)
    return (grad_input, jnp.sum(grad_out * norm_hat, axis=0), jnp.sum(grad_out, axis=0))


def scatter_chip_first(left_side, right_side, place):
    features = left_side.shape[1] // place.chips

    def part(steps):
        start = ((place.chip + steps) % place.chips) * features
        columns = lax.dynamic_slice_in_dim(left_side, start, features, 1)
        return dot_first(columns, right_side).astype(jnp.bfloat16)

    total = None
    sent = [chip_shift(part(steps), steps) for steps in range(1, place.chips)]
    own = part(0)
    total = own.astype(jnp.float32)
    for piece in sent:
        total = total + piece.astype(jnp.float32)
    total = total.astype(jnp.bfloat16)
    total = add_low(total, cross_home(total))
    return share_rows(total, place)


def scatter_tp_first(left_side, right_side, place):
    whole = dot_first(left_side, right_side).astype(jnp.bfloat16)
    whole = add_low(whole, cross_home(whole))
    whole = whole.reshape(place.chips, -1, whole.shape[1])

    def part(steps):
        return lax.dynamic_index_in_dim(whole, (place.chip + steps) % place.chips, 0, False)

    sent = [chip_shift(part(steps), steps, True) for steps in range(1, place.chips)]
    total = part(0)
    for piece in sent:
        total = add_low(total, piece)
    return share_rows(total, place)


def add_low(first, second):
    return (first.astype(jnp.float32) + second.astype(jnp.float32)).astype(jnp.bfloat16)


def share_rows(total, place):
    total = total.reshape(2, -1, total.shape[1])
    own = lax.dynamic_index_in_dim(total, place.core, 0, False)
    other = lax.dynamic_index_in_dim(total, 1 - place.core, 0, False)
    share = jnp.where(place.home, own, mate(other))
    return ctx_total(share, place)


def ctx_total(share, place):
    if lax.axis_size("ctx") != 4:
        return lax.psum(share, "ctx")
    outer = (place.ctx == 0) | (place.ctx == 3)
    inner = add_low(share, lax.ppermute(share, "ctx", [(0, 1), (3, 2)]))
    total = add_low(inner, lax.ppermute(inner, "ctx", [(1, 2), (2, 1)]))
    back = lax.ppermute(total, "ctx", [(1, 0), (2, 3)])
    return jnp.where(outer, back, total)


def core_sum(own_part, mate_part):
    return own_part + mate(mate_part.astype(jnp.bfloat16)).astype(jnp.float32)


def gelu_slope(pre_act, grad_act):
    pullback = jax.vjp(lambda values: jax.nn.gelu(values, approximate=True), pre_act)[1]
    return pullback(grad_act)[0]


def per_device(
    tokens,
    cotangent,
    doc_lengths,
    norm_gains,
    norm_biases,
    qkv_weight,
    qv_bias,
    proj_weight,
    fc_weight,
    fc_bias,
    out_weight,
):
    place = Place()
    block_len, model_width = tokens.shape[1:]
    shard_rows = qkv_weight.shape[2]
    half_width = qkv_weight.shape[3]
    half_hidden = fc_weight.shape[2]
    layer_count = qkv_weight.shape[0]
    reach = WINDOW // block_len
    key_len = (reach + 1) * block_len

    def my_seq(value):
        return lax.dynamic_index_in_dim(value, place.tp, 0, False)

    own_tokens = my_seq(tokens)
    halo = []
    step_value = own_tokens
    for _ in range(reach):
        step_value = onward(step_value)
        halo.insert(0, step_value)
    vectors = jnp.concatenate([norm_gains, norm_biases], axis=1)
    vectors = lax.all_gather(
        vectors.reshape(-1, vectors.shape[2]), "shard", axis=1, tiled=True
    ).astype(jnp.float32)
    vectors = vectors.reshape(layer_count, 6, model_width)

    def half_of(value, axis):
        other = other_tp(value)
        return jnp.where(place.home, value, other).astype(jnp.float32)

    qv_half = half_of(qv_bias, 2)
    fc_half = half_of(fc_bias, 1)

    def packed(layer):
        return (
            jnp.concatenate([qkv_weight[layer, 0], qkv_weight[layer, 1]], axis=1),
            jnp.concatenate(
                [qkv_weight[layer, 2], jnp.transpose(proj_weight[layer])], axis=1
            ),
            fc_weight[layer],
            jnp.transpose(out_weight[layer]),
        )

    weights = []
    gate = None
    for layer in range(layer_count):
        row = []
        pieces = packed(layer)
        for pair in range(2):
            first, second = pieces[2 * pair], pieces[2 * pair + 1]
            if gate is not None:
                (first, second), _ = tie((first, second), gate)
            one = gather_core_first(first, place)
            two = gather_chip_first(second, place)
            next(one), next(two)
            gate = (next(one), next(two))
            row += [next(one), next(two)]
        weights.append(row)

    lengths = my_seq(doc_lengths)
    lengths = jnp.stack([lengths, mate(lengths)])
    doc_ends = jnp.cumsum(lengths, axis=1)
    first_pos = place.ctx * block_len
    query_pos = first_pos + jnp.arange(block_len, dtype=jnp.int32)
    started = doc_ends[:, None, :] <= query_pos[None, :, None]
    doc_start = jnp.max(jnp.where(started, doc_ends[:, None, :], 0), axis=-1)
    low_pos = jnp.maximum(doc_start, query_pos[None, :] - (WINDOW - 1))
    low_pos = (low_pos - first_pos + reach * block_len).astype(jnp.int32)

    hidden = own_tokens.astype(jnp.float32)
    stash = []
    for layer in range(layer_count):
        gains, shifts = vectors[layer, :2], vectors[layer, 2:]
        w_qk, w_vp, w_fc, w_out_t = weights[layer]
        w_q, w_k = w_qk[:, :half_width], w_qk[:, half_width:]
        w_v, w_proj_t = w_vp[:, :half_width], w_vp[:, half_width:]
        attn_in, hat_attn, inv_attn = norm_forward(hidden, gains[0], shifts[0])
        own_near = [attn_in]
        if layer == 0:
            for part in reversed(halo):
                own_near.insert(
                    0, norm_forward(part.astype(jnp.float32), gains[0], shifts[0])[0]
                )
        else:
            step_value = attn_in
            for _ in range(reach):
                step_value = onward(step_value)
                own_near.insert(0, step_value)
        mate_near = [mate(part) for part in own_near]
        near = jnp.concatenate(own_near + mate_near)
        pair_in = jnp.concatenate([own_near[-1], mate_near[-1]])
        queries = (dot_f32(pair_in, w_q) + qv_half[layer, 0]).astype(jnp.bfloat16)
        keys = dot_f32(near, w_k).astype(jnp.bfloat16)
        values = (dot_f32(near, w_v) + qv_half[layer, 1]).astype(jnp.bfloat16)
        queries = queries.reshape(2, block_len, half_width)
        keys = keys.reshape(2, key_len, half_width)
        values = values.reshape(2, key_len, half_width)
        mixed, log_total = attention_forward(queries, keys, values, low_pos)
        mate_part = dot_second(mixed[1], w_proj_t)
        own_part = dot_second(mixed[0], w_proj_t)
        middle = hidden + core_sum(own_part, mate_part) + shifts[1]
        mlp_own, hat_mlp, inv_mlp = norm_forward(middle, gains[1], shifts[2])
        mlp_in = jnp.concatenate([mlp_own, mate(mlp_own)])
        pre_act = dot_f32(mlp_in, w_fc) + fc_half[layer]
        activated = jax.nn.gelu(pre_act, approximate=True).astype(jnp.bfloat16)
        mate_part = dot_second(activated[block_len:], w_out_t)
        own_part = dot_second(activated[:block_len], w_out_t)
        hidden = middle + core_sum(own_part, mate_part) + shifts[3]
        stash.append(
            (
                near, pair_in, hat_attn, inv_attn, queries, keys, values, mixed, log_total,
                hat_mlp, inv_mlp, mlp_in, pre_act, activated,
            )
        )

    own_output = hidden.astype(jnp.bfloat16)
    far_output = other_tp(own_output)

    def both_seqs(own, other):
        return jnp.where(place.tp == 0, jnp.stack([own, other]), jnp.stack([other, own]))

    output = both_seqs(own_output, far_output)

    grad_hidden = my_seq(cotangent).astype(jnp.float32)
    layer_grads = [None] * layer_count
    for layer in reversed(range(layer_count)):
        (
            near, pair_in, hat_attn, inv_attn, queries, keys, values, mixed, log_total,
            hat_mlp, inv_mlp, mlp_in, pre_act, activated,
        ) = stash[layer]
        gains = vectors[layer, :2]
        w_qk, w_vp, w_fc, w_out_t = weights[layer]
        w_q, w_k = w_qk[:, :half_width], w_qk[:, half_width:]
        w_v, w_proj_t = w_vp[:, :half_width], w_vp[:, half_width:]
        grad_out_bias = jnp.sum(grad_hidden, axis=0)
        grad_low = grad_hidden.astype(jnp.bfloat16)
        grad_low = jnp.concatenate([grad_low, mate(grad_low)])
        out_share = scatter_tp_first(grad_low, activated, place)
        grad_pre = gelu_slope(pre_act, dot_f32(grad_low, w_out_t)).astype(jnp.bfloat16)
        grad_fc_bias = jnp.sum(grad_pre.astype(jnp.float32), axis=0)
        fc_share = scatter_chip_first(mlp_in, grad_pre, place)
        mate_part = dot_second(grad_pre[block_len:], w_fc)
        own_part = dot_second(grad_pre[:block_len], w_fc)
        grad_norm_in = core_sum(own_part, mate_part)
        grad_from_mlp, grad_gain_mlp, grad_shift_mlp = norm_backward(
            grad_norm_in, hat_mlp, inv_mlp, gains[1]
        )
        grad_middle = grad_hidden + grad_from_mlp
        grad_proj_bias = jnp.sum(grad_middle, axis=0)
        grad_low = grad_middle.astype(jnp.bfloat16)
        grad_low = jnp.concatenate([grad_low, mate(grad_low)])
        mixed_rows = mixed.reshape(2 * block_len, half_width)
        grad_mixed = dot_f32(grad_low, w_proj_t).astype(jnp.bfloat16)
        grad_q, grad_k, grad_v = attention_backward(
            queries, keys, values, mixed, grad_mixed.reshape(queries.shape), log_total, low_pos
        )
        grad_qv_bias = jnp.stack(
            [
                jnp.sum(grad_q.astype(jnp.float32), axis=(0, 1)),
                jnp.sum(grad_v.astype(jnp.float32), axis=(0, 1)),
            ]
        )
        near_part = [
            dot_second(grad_k[seq], w_k) + dot_second(grad_v[seq], w_v) for seq in range(2)
        ]
        query_part = [dot_second(grad_q[seq], w_q) for seq in range(2)]
        last = reach * block_len
        far_total = core_sum(near_part[0][:last], near_part[1][:last])
        grad_attn_in = core_sum(
            near_part[0][last:] + query_part[0], near_part[1][last:] + query_part[1]
        )
        carried = far_total[:block_len].astype(jnp.bfloat16)
        for step in range(1, reach + 1):
            arrived = backward_step(carried).astype(jnp.float32)
            if step < reach:
                section = far_total[step * block_len : (step + 1) * block_len]
                carried = (arrived + section).astype(jnp.bfloat16)
            else:
                grad_attn_in = grad_attn_in + arrived
        grad_k = grad_k.reshape(2 * key_len, half_width)
        grad_v = grad_v.reshape(2 * key_len, half_width)
        grad_q = grad_q.reshape(2 * block_len, half_width)
        grad_from_attn, grad_gain_attn, grad_shift_attn = norm_backward(
            grad_attn_in, hat_attn, inv_attn, gains[0]
        )
        proj_share = scatter_tp_first(grad_low, mixed_rows, place)
        v_share = scatter_tp_first(near, grad_v, place)
        q_share = scatter_chip_first(pair_in, grad_q, place)
        k_share = scatter_chip_first(near, grad_k, place)
        grad_hidden = grad_middle + grad_from_attn
        halves = jnp.concatenate([grad_qv_bias.reshape(-1), grad_fc_bias])
        empty = jnp.zeros_like(halves)
        small = jnp.concatenate(
            [
                grad_gain_attn, grad_gain_mlp,
                grad_shift_attn, grad_proj_bias, grad_shift_mlp, grad_out_bias,
                jnp.where(place.core == 0, halves, empty),
                jnp.where(place.core == 1, halves, empty),
            ]
        )
        small = lax.psum(small, ("shard", "ctx", "tp"))
        layer_grads[layer] = (q_share, k_share, v_share, proj_share, fc_share, out_share, small)

    own_grad = grad_hidden.astype(jnp.bfloat16)
    far_grad = other_tp(own_grad).astype(jnp.float32)
    token_grad = both_seqs(grad_hidden, far_grad)

    def entries(pick):
        return jnp.stack([pick(entry) for entry in layer_grads])

    def full(value):
        return value.astype(jnp.float32)

    small = entries(lambda entry: entry[6])
    split = 6 * model_width
    norms = small[:, :split].reshape(layer_count, 6, model_width)
    shard = lax.axis_index("shard")
    norms = lax.dynamic_slice_in_dim(norms, shard * shard_rows, shard_rows, 2)
    halves = small[:, split:].reshape(layer_count, 2, -1)
    halves = lax.dynamic_index_in_dim(halves, place.tp, 1, False)
    return (
        output,
        token_grad,
        norms[:, :2],
        norms[:, 2:],
        entries(lambda entry: jnp.stack([full(entry[0]), full(entry[1]), full(entry[2])])),
        halves[:, : 2 * half_width].reshape(layer_count, 2, half_width),
        entries(lambda entry: jnp.transpose(full(entry[3]))),
        entries(lambda entry: full(entry[4])),
        halves[:, 2 * half_width :],
        entries(lambda entry: jnp.transpose(full(entry[5]))),
    )


def solution(mesh):
    placed = (
        P("shard", "ctx", None),
        P("shard", "ctx", None),
        P("shard", None),
        P(None, None, "shard"),
        P(None, None, "shard"),
        P(None, None, "shard", "tp"),
        P(None, None, "tp"),
        P(None, "tp", "shard"),
        P(None, "shard", "tp"),
        P(None, "tp"),
        P(None, "tp", "shard"),
    )
    return jax.shard_map(
        per_device,
        mesh=mesh,
        in_specs=placed,
        out_specs=(
            P("shard", "ctx", None),
            P("shard", "ctx", None),
            P(None, None, "shard"),
            P(None, None, "shard"),
            P(None, None, "shard", "tp"),
            P(None, None, "tp"),
            P(None, "tp", "shard"),
            P(None, "shard", "tp"),
            P(None, "tp"),
            P(None, "tp", "shard"),
        ),
        check_vma=False,
    )
```

```python
import jax
import jax.numpy as jnp
from jax import lax
from jax.experimental import pallas as pl
from jax.experimental.pallas import tpu as pltpu
from jax.sharding import PartitionSpec as P

HD = 64
WINDOW = 1024
TILE = 256
masked_score = -1e30


def contract(left_side, right_side, left_dim, right_dim):
    return lax.dot_general(
        left_side, right_side, (((left_dim,), (right_dim,)), ((), ())),
        preferred_element_type=jnp.float32,
    )


def half_mask(shape, half):
    lane = lax.broadcasted_iota(jnp.int32, shape, 1)
    return (lane < HD) if half == 0 else (lane >= HD)


PAIR = 2 * HD


def forward_kernel(qkv_ref, low_ref, mixed_ref, total_ref):
    block_len = mixed_ref.shape[1]
    first = qkv_ref.shape[1] - block_len
    span = WINDOW + TILE
    eye = lax.broadcasted_iota(jnp.int32, (TILE, TILE), 0) == lax.broadcasted_iota(
        jnp.int32, (TILE, TILE), 1
    )
    for block in range(block_len // TILE):
        rows = pl.ds(block * TILE, TILE)
        window = pl.ds(block * TILE, span)
        queries = qkv_ref[0, pl.ds(first + block * TILE, TILE), :PAIR]
        queries = queries * jnp.asarray(HD ** (-0.5), jnp.bfloat16)
        keys = qkv_ref[0, window, PAIR : 2 * PAIR]
        values = qkv_ref[0, window, 2 * PAIR :]
        low_pos = low_ref[0, rows, :] - block * TILE
        key_pos = lax.broadcasted_iota(jnp.int32, (TILE, span), 1)
        query_pos = lax.broadcasted_iota(jnp.int32, (TILE, TILE), 0) + WINDOW
        allowed = key_pos >= low_pos
        causal = key_pos[:, WINDOW:] <= query_pos
        mixed = jnp.zeros((TILE, 2 * HD), jnp.float32)
        for half in range(2):
            scores = contract(
                jnp.where(half_mask(queries.shape, half), queries, 0), keys, 1, 1
            )
            early = jnp.where(allowed[:, :WINDOW], scores[:, :WINDOW], masked_score)
            late = jnp.where(allowed[:, WINDOW:] & causal, scores[:, WINDOW:], masked_score)
            top_score = jnp.maximum(
                jnp.max(early, axis=1, keepdims=True), jnp.max(late, axis=1, keepdims=True)
            )
            early = jnp.exp(early - top_score)
            late = jnp.exp(late - top_score)
            row_total = jnp.sum(early, axis=1, keepdims=True) + jnp.sum(
                late, axis=1, keepdims=True
            )
            part = contract(early.astype(jnp.bfloat16), values[:WINDOW], 1, 0) + contract(
                late.astype(jnp.bfloat16), values[WINDOW:], 1, 0
            )
            part = part * (1.0 / row_total)
            mixed = jnp.where(half_mask(mixed.shape, half), part, mixed)
            log_total = top_score + jnp.log(row_total)
            total_ref[0, 0, half : half + 1, rows] = jnp.sum(
                jnp.where(eye, log_total, 0.0), axis=0, keepdims=True
            )
        mixed_ref[0, rows, :] = mixed.astype(jnp.bfloat16)


def attention_forward(packed, low_pos):
    groups, key_len, width = packed.shape
    block_len = low_pos.shape[1]
    pairs = width // (3 * PAIR)
    pick = lambda seq, pair: (seq, 0, pair)
    return pl.pallas_call(
        forward_kernel,
        grid=(groups, pairs),
        in_specs=[
            pl.BlockSpec((1, key_len, 3 * PAIR), pick),
            pl.BlockSpec((1, block_len, 1), lambda seq, pair: (seq, 0, 0)),
        ],
        out_specs=[
            pl.BlockSpec((1, block_len, PAIR), pick),
            pl.BlockSpec((1, 1, 2, block_len), lambda seq, pair: (seq, pair, 0, 0)),
        ],
        out_shape=[
            jax.ShapeDtypeStruct((groups, block_len, pairs * PAIR), jnp.bfloat16),
            jax.ShapeDtypeStruct((groups, pairs, 2, block_len), jnp.float32),
        ],
        compiler_params=pltpu.CompilerParams(vmem_limit_bytes=40 << 20),
        cost_estimate=pl.CostEstimate(
            flops=16 * groups * pairs * block_len * (WINDOW + TILE) * HD,
            bytes_accessed=2 * groups * width * key_len,
            transcendentals=2 * groups * pairs * block_len * (WINDOW + TILE),
        ),
    )(packed, low_pos[:, :, None])


def backward_kernel(qkv_ref, mixed_ref, grad_ref, total_ref, low_ref, out_ref, gk_sum, gv_sum):
    block_len = mixed_ref.shape[1]
    first = qkv_ref.shape[1] - block_len
    span = WINDOW + TILE
    scale = HD ** (-0.5)
    gk_sum[...] = jnp.zeros_like(gk_sum)
    gv_sum[...] = jnp.zeros_like(gv_sum)
    eye = lax.broadcasted_iota(jnp.int32, (TILE, TILE), 0) == lax.broadcasted_iota(
        jnp.int32, (TILE, TILE), 1
    )
    for block in range(block_len // TILE):
        rows = pl.ds(block * TILE, TILE)
        window = pl.ds(block * TILE, span)
        queries = qkv_ref[0, pl.ds(first + block * TILE, TILE), :PAIR]
        queries = queries * jnp.asarray(scale, jnp.bfloat16)
        keys = qkv_ref[0, window, PAIR : 2 * PAIR]
        values = qkv_ref[0, window, 2 * PAIR :]
        grads = grad_ref[0, rows, :]
        product = grads.astype(jnp.float32) * mixed_ref[0, rows, :].astype(jnp.float32)
        low_pos = low_ref[0, :, rows] - block * TILE
        key_pos = lax.broadcasted_iota(jnp.int32, (span, TILE), 0)
        query_pos = lax.broadcasted_iota(jnp.int32, (TILE, TILE), 1) + WINDOW
        allowed = key_pos >= low_pos
        late_allowed = allowed[WINDOW:] & (key_pos[WINDOW:] <= query_pos)
        keys_t = jnp.transpose(keys)
        gq_parts = []
        for half in range(2):
            mask = half_mask(queries.shape, half)
            q_half = jnp.where(mask, queries, 0)
            g_half = jnp.where(mask, grads, 0)
            delta = jnp.sum(jnp.where(mask, product, 0.0), axis=1, keepdims=True)
            delta = jnp.sum(jnp.where(eye, delta, 0.0), axis=0, keepdims=True)
            log_total = total_ref[0, 0, half : half + 1, rows]
            scores = contract(keys, q_half, 1, 1)
            probs = jnp.concatenate(
                [
                    jnp.where(allowed[:WINDOW], jnp.exp(scores[:WINDOW] - log_total), 0.0),
                    jnp.where(late_allowed, jnp.exp(scores[WINDOW:] - log_total), 0.0),
                ]
            )
            grad_probs = contract(values, g_half, 1, 1)
            grad_scores = (probs * (grad_probs - delta)).astype(jnp.bfloat16)
            gv_sum[window, :] += contract(probs.astype(jnp.bfloat16), g_half, 1, 0)
            gk_sum[window, :] += contract(grad_scores, q_half, 1, 0)
            gq_parts.append(contract(keys_t[half * HD : (half + 1) * HD], grad_scores, 1, 0))
        gq = jnp.transpose(jnp.concatenate(gq_parts)) * scale
        out_ref[0, pl.ds(first + block * TILE, TILE), :PAIR] = gq.astype(jnp.bfloat16)
    out_ref[0, :first, :PAIR] = jnp.zeros((first, PAIR), jnp.bfloat16)
    out_ref[0, :, PAIR : 2 * PAIR] = gk_sum[...].astype(jnp.bfloat16)
    out_ref[0, :, 2 * PAIR :] = gv_sum[...].astype(jnp.bfloat16)


def attention_backward(packed, mixed, grads, log_total, low_pos):
    groups, key_len, width = packed.shape
    block_len = mixed.shape[1]
    pairs = width // (3 * PAIR)
    pick = lambda seq, pair: (seq, 0, pair)
    row_spec = pl.BlockSpec((1, block_len, PAIR), pick)
    packed_spec = pl.BlockSpec((1, key_len, 3 * PAIR), pick)
    return pl.pallas_call(
        backward_kernel,
        grid=(groups, pairs),
        in_specs=[
            packed_spec, row_spec, row_spec,
            pl.BlockSpec((1, 1, 2, block_len), lambda seq, pair: (seq, pair, 0, 0)),
            pl.BlockSpec((1, 1, block_len), lambda seq, pair: (seq, 0, 0)),
        ],
        out_specs=packed_spec,
        out_shape=jax.ShapeDtypeStruct(packed.shape, jnp.bfloat16),
        scratch_shapes=[
            pltpu.VMEM((key_len, PAIR), jnp.float32),
            pltpu.VMEM((key_len, PAIR), jnp.float32),
        ],
        compiler_params=pltpu.CompilerParams(vmem_limit_bytes=40 << 20),
        cost_estimate=pl.CostEstimate(
            flops=40 * groups * pairs * block_len * (WINDOW + TILE) * HD,
            bytes_accessed=4 * groups * width * key_len,
            transcendentals=2 * groups * pairs * block_len * (WINDOW + TILE),
        ),
    )(packed, mixed, grads, log_total, low_pos[:, None, :])


norm_eps = 1e-05


def mate(value):
    count = lax.axis_size("shard")
    return lax.ppermute(value, "shard", [(i, i ^ 1) for i in range(count)])


def chip_shift(value, steps, half_only=False):
    count = lax.axis_size("shard")
    if not half_only:
        return lax.ppermute(value, "shard", [(i, (i + 2 * steps) % count) for i in range(count)])
    pairs = [(i * 2 + i % 2, ((i + 2 * steps) % count) * 2 + i % 2) for i in range(count)]
    return lax.ppermute(value, ("shard", "tp"), pairs)


def cross_out(value):
    pairs = [(i * 2 + i % 2, i * 2 + 1 - i % 2) for i in range(lax.axis_size("shard"))]
    return lax.ppermute(value, ("shard", "tp"), pairs)


def cross_home(value):
    pairs = [(i * 2 + 1 - i % 2, i * 2 + i % 2) for i in range(lax.axis_size("shard"))]
    return lax.ppermute(value, ("shard", "tp"), pairs)


def other_tp(value):
    return lax.ppermute(value, "tp", [(0, 1), (1, 0)])


def onward(value):
    count = lax.axis_size("ctx")
    return lax.ppermute(value, "ctx", [(i, i + 1) for i in range(count - 1)])


def backward_step(value):
    count = lax.axis_size("ctx")
    return lax.ppermute(value, "ctx", [(i + 1, i) for i in range(count - 1)])


class Place:
    def __init__(self):
        shard = lax.axis_index("shard")
        self.shard = shard
        self.chips = lax.axis_size("shard") // 2
        self.chip = shard // 2
        self.core = shard % 2
        self.tp = lax.axis_index("tp")
        self.ctx = lax.axis_index("ctx")
        self.home = self.core == self.tp


class Flow:
    def __init__(self, steps):
        self.steps = steps
        self.result = None
        self.pending = next(steps)

    def go_on(self, arrived):
        try:
            self.pending = self.steps.send(arrived)
        except StopIteration as stop:
            self.pending, self.result = None, stop.value


def drain(*flows):
    while any(flow.pending is not None for flow in flows):
        for flow in flows:
            if flow.pending is not None:
                flow.go_on(flow.pending)
    return [flow.result for flow in flows]


def pump(value, *flows):
    flows = [flow for flow in flows if flow is not None and flow.pending is not None]
    value, arrived = lax.optimization_barrier((value, [flow.pending for flow in flows]))
    for flow, piece in zip(flows, arrived):
        flow.go_on(piece)
    return value


def ordered(own, others, position, axis=0):
    if len(others) == 1:
        return jnp.where(
            position == 0,
            jnp.stack([own, others[0]], axis=axis),
            jnp.stack([others[0], own], axis=axis),
        )
    count = len(others) + 1
    whole = jnp.stack([own] + others, axis=axis)
    return jnp.take(whole, (position - jnp.arange(count)) % count, axis=axis)


def gather_core_first(piece, place):
    other = yield mate(piece)
    both = ordered(piece, [other], place.core)
    across = yield cross_out(both)
    pair = jnp.where(place.home, both, across)
    others = yield [chip_shift(pair, steps) for steps in range(1, place.chips)]
    return ordered(pair, others, place.chip).reshape(-1, piece.shape[1])


def gather_chip_first(piece, place):
    others = yield [chip_shift(piece, steps) for steps in range(1, place.chips)]
    own = ordered(piece, others, place.chip)
    other = yield mate(own)
    both = ordered(own, [other], place.core, 1)
    across = yield cross_out(both)
    return jnp.where(place.home, both, across).reshape(-1, piece.shape[1])


def gather_small(value, place):
    if place.chips != 2:
        return lax.all_gather(value, "shard", axis=1, tiled=True)
    near, far, last = [
        lax.ppermute(value, "shard", [(i, i ^ flip) for i in range(4)]) for flip in (1, 2, 3)
    ]
    pair = ordered(value, [near], place.core, 1)
    far_pair = ordered(far, [last], place.core, 1)
    return ordered(pair, [far_pair], place.chip, 1).reshape(value.shape[0], -1)


def dot_f32(left_side, right_side):
    return jnp.dot(left_side, right_side, preferred_element_type=jnp.float32)


def dot_first(left_side, right_side):
    return contract(left_side, right_side, 0, 0)


def dot_second(left_side, right_side):
    return contract(left_side, right_side, 1, 1)


def norm_forward(hidden, norm_gain, norm_shift):
    row_mean = jnp.mean(hidden, axis=-1, keepdims=True)
    centred = hidden - row_mean
    variance = jnp.mean(centred * centred, axis=-1, keepdims=True)
    inv_std = lax.rsqrt(variance + norm_eps)
    norm_hat = centred * inv_std
    return ((norm_hat * norm_gain + norm_shift).astype(jnp.bfloat16), norm_hat, inv_std)


def norm_backward(grad_out, norm_hat, inv_std, norm_gain):
    scaled = grad_out * norm_gain
    mean_one = jnp.mean(scaled, axis=-1, keepdims=True)
    mean_two = jnp.mean(scaled * norm_hat, axis=-1, keepdims=True)
    grad_input = inv_std * (scaled - mean_one - norm_hat * mean_two)
    return (grad_input, jnp.sum(grad_out * norm_hat, axis=0), jnp.sum(grad_out, axis=0))


def wide(value):
    return value.astype(jnp.float32)


def narrow(value):
    return value.astype(jnp.bfloat16)


def pick_block(value, index, count):
    size = value.shape[0] // count
    return lax.dynamic_slice_in_dim(value, index * size, size, 0)


def scatter_chip_first(left_side, right_side, place):
    features = left_side.shape[1] // place.chips

    def part(steps):
        start = ((place.chip + steps) % place.chips) * features
        columns = lax.dynamic_slice_in_dim(left_side, start, features, 1)
        return narrow(dot_first(columns, right_side))

    sent = [chip_shift(part(steps), steps) for steps in range(1, place.chips)]
    own = part(0)
    sent = yield sent
    total = wide(own)
    for piece in sent:
        total = total + wide(piece)
    total = narrow(total)
    across = yield cross_home(total)

    def rows(core):
        return narrow(wide(pick_block(total, core, 2)) + wide(pick_block(across, core, 2)))

    other = yield mate(rows(1 - place.core))
    return jnp.where(place.home, rows(place.core), other)


def scatter_tp_first(left_side, right_side, place):
    whole = narrow(dot_first(left_side, right_side))
    across = yield cross_home(whole)

    def part(steps):
        index = (place.chip + steps) % place.chips
        return wide(pick_block(whole, index, place.chips)) + wide(
            pick_block(across, index, place.chips)
        )

    sent = yield [
        chip_shift(narrow(part(steps)), steps, True) for steps in range(1, place.chips)
    ]

    def rows(core):
        total = pick_block(part(0), core, 2)
        for piece in sent:
            total = total + wide(pick_block(piece, core, 2))
        return narrow(total)

    other = yield mate(rows(1 - place.core))
    return jnp.where(place.home, rows(place.core), other)


def ctx_total(share, place):
    if lax.axis_size("ctx") != 4:
        return (yield lax.psum(share, "ctx"))
    outer = (place.ctx == 0) | (place.ctx == 3)
    kind = share.dtype
    add = lambda first, second: (wide(first) + wide(second)).astype(kind)
    came = yield lax.ppermute(share, "ctx", [(0, 1), (3, 2)])
    inner = add(share, came)
    came = yield lax.ppermute(inner, "ctx", [(1, 2), (2, 1)])
    total = add(inner, came)
    back = yield lax.ppermute(total, "ctx", [(1, 0), (2, 3)])
    return jnp.where(outer, back, total)


def scatter_total(steps, place):
    share = yield from steps
    return (yield from ctx_total(share, place))


def small_total(value, place):
    if place.chips != 2 or lax.axis_size("ctx") != 4:
        return (yield lax.psum(value, ("shard", "ctx", "tp")))
    came = yield mate(value)
    value = value + came
    came = yield chip_shift(value, 1)
    value = value + came
    came = yield other_tp(value)
    return (yield from ctx_total(value + came, place))


def core_sum(own_part, mate_part):
    return own_part + wide(mate(narrow(mate_part)))


def gelu_slope(pre_act, grad_act):
    pullback = jax.vjp(lambda values: jax.nn.gelu(values, approximate=True), pre_act)[1]
    return pullback(grad_act)[0]


def pair_major(value):
    lead = value.shape[1:-1]
    pairs = value.shape[-1] // PAIR
    value = value.reshape((3,) + lead + (pairs, PAIR))
    return jnp.moveaxis(value, 0, -2).reshape(lead + (3 * pairs * PAIR,))


def from_pair_major(value):
    lead = value.shape[:-1]
    pairs = value.shape[-1] // (3 * PAIR)
    value = jnp.moveaxis(value.reshape(lead + (pairs, 3, PAIR)), -2, 0)
    return value.reshape((3,) + lead + (pairs * PAIR,))


def per_device(
    tokens,
    cotangent,
    doc_lengths,
    norm_gains,
    norm_biases,
    qkv_weight,
    qv_bias,
    proj_weight,
    fc_weight,
    fc_bias,
    out_weight,
):
    place = Place()
    block_len, model_width = tokens.shape[1:]
    shard_rows = qkv_weight.shape[2]
    half_width = qkv_weight.shape[3]
    layer_count = qkv_weight.shape[0]
    reach = WINDOW // block_len
    key_len = (reach + 1) * block_len
    last = reach * block_len

    def my_seq(value):
        return lax.dynamic_index_in_dim(value, place.tp, 0, False)

    def both_seqs(own, other):
        return ordered(own, [other], place.tp)

    pieces = [
        (
            pair_major(qkv_weight[layer]),
            jnp.transpose(proj_weight[layer]),
            fc_weight[layer],
            jnp.transpose(out_weight[layer]),
        )
        for layer in range(layer_count)
    ]

    def attn_flows(layer):
        return (
            Flow(gather_core_first(pieces[layer][0], place)),
            Flow(gather_chip_first(pieces[layer][1], place)),
        )

    def mlp_flows(layer):
        return (
            Flow(gather_core_first(pieces[layer][2], place)),
            Flow(gather_chip_first(pieces[layer][3], place)),
        )

    own_tokens = my_seq(tokens)
    flow_qkv, flow_proj = attn_flows(0)
    step_value = own_tokens
    halo = []
    for _ in range(reach):
        step_value = onward(step_value)
        halo.insert(0, step_value)
    vectors = jnp.concatenate([norm_gains, norm_biases], axis=1)
    vectors = wide(gather_small(vectors.reshape(-1, vectors.shape[2]), place))
    vectors = vectors.reshape(layer_count, 6, model_width)
    biases = jnp.concatenate([qv_bias.reshape(layer_count, -1), fc_bias], axis=1)
    biases = wide(jnp.where(place.home, biases, other_tp(biases)))
    lengths = my_seq(doc_lengths)
    lengths = jnp.stack([lengths, mate(lengths)])
    pump((), flow_qkv)
    pump((), flow_proj)
    pieces = pump(pieces, flow_qkv, flow_proj)
    flow_fc, flow_out = mlp_flows(0)
    pump((), flow_fc)

    doc_ends = jnp.cumsum(lengths, axis=1)
    first_pos = place.ctx * block_len
    query_pos = first_pos + jnp.arange(block_len, dtype=jnp.int32)
    started = doc_ends[:, None, :] <= query_pos[None, :, None]
    doc_start = jnp.max(jnp.where(started, doc_ends[:, None, :], 0), axis=-1)
    low_pos = jnp.maximum(doc_start, query_pos[None, :] - (WINDOW - 1))
    low_pos = (low_pos - first_pos + last).astype(jnp.int32)

    hidden = wide(own_tokens)
    stash = []
    weights = []
    for layer in range(layer_count):
        gains, shifts = vectors[layer, :2], vectors[layer, 2:]
        bias_q, bias_v = biases[layer, :half_width], biases[layer, half_width : 2 * half_width]
        bias_qkv = pair_major(jnp.stack([bias_q, jnp.zeros_like(bias_q), bias_v])[:, None])
        bias_fc = biases[layer, 2 * half_width :]
        attn_in, hat_attn, inv_attn = norm_forward(hidden, gains[0], shifts[0])
        own_near = [attn_in]
        if layer == 0:
            for part in reversed(halo):
                own_near.insert(0, norm_forward(wide(part), gains[0], shifts[0])[0])
            own_near = jnp.concatenate(own_near)
            near = jnp.concatenate([own_near, mate(own_near)])
        else:
            step_value = attn_in
            mate_near = [mate(attn_in)]
            for _ in range(reach):
                step_value = onward(step_value)
                own_near.insert(0, step_value)
                mate_near.insert(0, mate(step_value))
            near = jnp.concatenate(own_near + mate_near)
        near = pump(near, flow_qkv, flow_proj)
        w_qkv, w_proj_t = flow_qkv.result, flow_proj.result
        packed = narrow(dot_f32(near, w_qkv) + bias_qkv).reshape(2, key_len, -1)
        packed = pump(packed, flow_fc, flow_out)
        packed = pump(packed, flow_out)
        mixed, log_total = attention_forward(packed, low_pos)
        if layer + 1 < layer_count:
            mixed, pieces = lax.optimization_barrier((mixed, pieces))
            flow_qkv, flow_proj = attn_flows(layer + 1)
        mate_part = dot_second(mixed[1], w_proj_t)
        own_part = dot_second(mixed[0], w_proj_t)
        middle = hidden + core_sum(own_part, mate_part) + shifts[1]
        mlp_own, hat_mlp, inv_mlp = norm_forward(middle, gains[1], shifts[2])
        if layer + 1 < layer_count:
            mlp_own = pump(mlp_own, flow_qkv)
        mlp_in = jnp.concatenate([mlp_own, mate(mlp_own)])
        mlp_in = pump(mlp_in, flow_fc)
        w_fc = flow_fc.result
        pre_act = dot_f32(mlp_in, w_fc) + bias_fc
        activated = narrow(jax.nn.gelu(pre_act, approximate=True))
        activated = pump(activated, flow_out)
        w_out_t = flow_out.result
        if layer + 1 < layer_count:
            activated = pump(activated, flow_qkv, flow_proj)
            activated, pieces = lax.optimization_barrier((activated, pieces))
            flow_fc, flow_out = mlp_flows(layer + 1)
        mate_part = dot_second(activated[block_len:], w_out_t)
        own_part = dot_second(activated[:block_len], w_out_t)
        hidden = middle + core_sum(own_part, mate_part) + shifts[3]
        if layer + 1 < layer_count:
            hidden = pump(hidden, flow_fc, flow_proj)
        weights.append((w_qkv, w_proj_t, w_fc, w_out_t))
        stash.append(
            (near, hat_attn, inv_attn, packed, mixed, log_total, hat_mlp, inv_mlp, mlp_in,
             pre_act, activated)
        )

    own_output = narrow(hidden)
    output = both_seqs(own_output, other_tp(own_output))

    grad_hidden = wide(my_seq(cotangent))
    old = {}
    for layer in reversed(range(layer_count)):
        near, hat_attn, inv_attn, packed, mixed, log_total = stash[layer][:6]
        hat_mlp, inv_mlp, mlp_in, pre_act, activated = stash[layer][6:]
        gains = vectors[layer, :2]
        w_qkv, w_proj_t, w_fc, w_out_t = weights[layer]
        final = layer == 0

        def reduced(steps):
            return Flow(scatter_total(steps, place) if final else steps)

        grad_out_bias = jnp.sum(grad_hidden, axis=0)
        grad_low = narrow(grad_hidden)
        grad_low = jnp.concatenate([grad_low, mate(grad_low)])
        flow_out = reduced(scatter_tp_first(grad_low, activated, place))
        grad_pre = narrow(gelu_slope(pre_act, dot_f32(grad_low, w_out_t)))
        grad_pre = pump(grad_pre, old.get("qkv"))
        grad_fc_bias = jnp.sum(wide(grad_pre), axis=0)
        mate_part = dot_second(grad_pre[block_len:], w_fc)
        own_part = dot_second(grad_pre[:block_len], w_fc)
        flow_fc = reduced(scatter_chip_first(mlp_in, grad_pre, place))
        grad_norm_in = core_sum(own_part, mate_part)
        if final:
            share = jnp.concatenate(drain(old["fc"], old["out"]), axis=1)
            old["mlp_ctx"] = Flow(ctx_total(share, place))
        grad_norm_in = pump(grad_norm_in, old.get("qkv"), old.get("small"))
        grad_from_mlp, grad_gain_mlp, grad_shift_mlp = norm_backward(
            grad_norm_in, hat_mlp, inv_mlp, gains[1]
        )
        grad_middle = grad_hidden + grad_from_mlp
        grad_proj_bias = jnp.sum(grad_middle, axis=0)
        grad_low = narrow(grad_middle)
        grad_low = jnp.concatenate([grad_low, mate(grad_low)])
        grad_low = pump(grad_low, old.get("qkv"), old.get("small"))
        if final:
            share = jnp.concatenate(drain(old["qkv"], old["proj"]), axis=1)
            old["attn_ctx"] = Flow(ctx_total(share, place))
        grad_mixed = narrow(dot_f32(grad_low, w_proj_t)).reshape(mixed.shape)
        flow_proj = reduced(
            scatter_tp_first(grad_low, mixed.reshape(2 * block_len, half_width), place)
        )
        grad_mixed = pump(grad_mixed, flow_out, old.get("small"))
        grad_packed = attention_backward(packed, mixed, grad_mixed, log_total, low_pos)
        grad_packed = pump(
            grad_packed, flow_out, flow_fc, flow_proj, old.get("mlp_ctx"), old.get("small")
        )
        grad_packed = pump(grad_packed, flow_out)
        mate_part = dot_second(grad_packed[1], w_qkv)
        own_part = dot_second(grad_packed[0], w_qkv)
        grad_near = core_sum(own_part, mate_part)
        far_total, grad_attn_in = grad_near[:last], grad_near[last:]
        carried = backward_step(narrow(far_total[:block_len]))
        rows = grad_packed.reshape(2 * key_len, -1)
        third = rows.shape[1] // 3
        if final:
            flows_qkv = [
                reduced(scatter_chip_first(near, rows[:, :third], place)),
                reduced(scatter_tp_first(near, rows[:, third : 2 * third], place)),
                reduced(scatter_chip_first(near, rows[:, 2 * third :], place)),
            ]
        else:
            flows_qkv = [reduced(scatter_chip_first(near, rows, place))]
        for step in range(1, reach + 1):
            if step == 1:
                carried = pump(
                    carried, flow_proj, flow_fc, old.get("attn_ctx"), old.get("small"),
                    *((flow_out,) if final else ()),
                )
            if step == 2:
                carried = pump(
                    carried, flow_fc, flow_proj, old.get("mlp_ctx"),
                    *(flows_qkv if final else ()),
                )
            arrived = wide(carried)
            if step < reach:
                section = far_total[step * block_len : (step + 1) * block_len]
                carried = backward_step(narrow(arrived + section))
            else:
                grad_attn_in = grad_attn_in + arrived
        grad_from_attn, grad_gain_attn, grad_shift_attn = norm_backward(
            grad_attn_in, hat_attn, inv_attn, gains[0]
        )
        grad_hidden = grad_middle + grad_from_attn
        grad_bias = jnp.sum(wide(rows), axis=0).reshape(-1, 3, PAIR)
        halves = jnp.concatenate(
            [grad_bias[:, 0].reshape(-1), grad_bias[:, 2].reshape(-1), grad_fc_bias]
        )
        empty = jnp.zeros_like(halves)
        small = jnp.concatenate(
            [
                grad_gain_attn, grad_gain_mlp,
                grad_shift_attn, grad_proj_bias, grad_shift_mlp, grad_out_bias,
                jnp.where(place.core == 0, halves, empty),
                jnp.where(place.core == 1, halves, empty),
            ]
        )
        flow_small = Flow(small_total(small, place))
        if not final:
            old = {
                "qkv": flows_qkv[0], "proj": flow_proj, "fc": flow_fc, "out": flow_out,
                "small": flow_small,
            }

    far_grad = wide(other_tp(narrow(grad_hidden)))
    token_grad = both_seqs(grad_hidden, far_grad)
    mlp_old, attn_old, small_old, out_new, fc_new, proj_new, small_new, *qkv_new = drain(
        old["mlp_ctx"], old["attn_ctx"], old["small"], flow_out, flow_fc, flow_proj, flow_small,
        *flows_qkv,
    )
    fc_width = fc_weight.shape[2]
    qkv_new = jnp.concatenate(qkv_new, axis=1)
    small = jnp.stack([small_new, small_old])
    split = 6 * model_width
    norms = small[:, :split].reshape(layer_count, 6, model_width)
    norms = lax.dynamic_slice_in_dim(norms, place.shard * shard_rows, shard_rows, 2)
    halves = small[:, split:].reshape(layer_count, 2, -1)
    halves = lax.dynamic_index_in_dim(halves, place.tp, 1, False)
    return (
        output,
        token_grad,
        norms[:, :2],
        norms[:, 2:],
        jnp.stack([from_pair_major(wide(v)) for v in (qkv_new, attn_old[:, : 3 * half_width])]),
        halves[:, : 2 * half_width].reshape(layer_count, 2, half_width),
        jnp.stack([jnp.transpose(wide(v)) for v in (proj_new, attn_old[:, 3 * half_width :])]),
        jnp.stack([wide(v) for v in (fc_new, mlp_old[:, :fc_width])]),
        halves[:, 2 * half_width :],
        jnp.stack([jnp.transpose(wide(v)) for v in (out_new, mlp_old[:, fc_width:])]),
    )


def solution(mesh):
    placed = (
        P("shard", "ctx", None),
        P("shard", "ctx", None),
        P("shard", None),
        P(None, None, "shard"),
        P(None, None, "shard"),
        P(None, None, "shard", "tp"),
        P(None, None, "tp"),
        P(None, "tp", "shard"),
        P(None, "shard", "tp"),
        P(None, "tp"),
        P(None, "tp", "shard"),
    )
    return jax.shard_map(
        per_device,
        mesh=mesh,
        in_specs=placed,
        out_specs=(
            P("shard", "ctx", None),
            P("shard", "ctx", None),
            P(None, None, "shard"),
            P(None, None, "shard"),
            P(None, None, "shard", "tp"),
            P(None, None, "tp"),
            P(None, "tp", "shard"),
            P(None, "shard", "tp"),
            P(None, "tp"),
            P(None, "tp", "shard"),
        ),
        check_vma=False,
    )
```

```python
import jax
import jax.numpy as jnp
from jax import lax
from jax.experimental import pallas as pl
from jax.experimental.pallas import tpu as pltpu
from jax.sharding import PartitionSpec as P

HD = 64
WINDOW = 1024
TILE = 256
masked_score = -1e30


def contract(left_side, right_side, left_dim, right_dim):
    return lax.dot_general(
        left_side, right_side, (((left_dim,), (right_dim,)), ((), ())),
        preferred_element_type=jnp.float32,
    )


def half_mask(shape, half):
    lane = lax.broadcasted_iota(jnp.int32, shape, 1)
    return (lane < HD) if half == 0 else (lane >= HD)


PAIR = 2 * HD


def forward_kernel(qkv_ref, low_ref, mixed_ref, total_ref):
    block_len = mixed_ref.shape[1]
    first = qkv_ref.shape[1] - block_len
    span = WINDOW + TILE
    eye = lax.broadcasted_iota(jnp.int32, (TILE, TILE), 0) == lax.broadcasted_iota(
        jnp.int32, (TILE, TILE), 1
    )
    for block in range(block_len // TILE):
        rows = pl.ds(block * TILE, TILE)
        window = pl.ds(block * TILE, span)
        queries = qkv_ref[0, pl.ds(first + block * TILE, TILE), :PAIR]
        queries = queries * jnp.asarray(HD ** (-0.5), jnp.bfloat16)
        keys = qkv_ref[0, window, PAIR : 2 * PAIR]
        values = qkv_ref[0, window, 2 * PAIR :]
        low_pos = low_ref[0, rows, :] - block * TILE
        key_pos = lax.broadcasted_iota(jnp.int32, (TILE, span), 1)
        query_pos = lax.broadcasted_iota(jnp.int32, (TILE, TILE), 0) + WINDOW
        allowed = key_pos >= low_pos
        causal = key_pos[:, WINDOW:] <= query_pos
        mixed = jnp.zeros((TILE, 2 * HD), jnp.float32)
        for half in range(2):
            scores = contract(
                jnp.where(half_mask(queries.shape, half), queries, 0), keys, 1, 1
            )
            early = jnp.where(allowed[:, :WINDOW], scores[:, :WINDOW], masked_score)
            late = jnp.where(allowed[:, WINDOW:] & causal, scores[:, WINDOW:], masked_score)
            top_score = jnp.maximum(
                jnp.max(early, axis=1, keepdims=True), jnp.max(late, axis=1, keepdims=True)
            )
            early = jnp.exp(early - top_score)
            late = jnp.exp(late - top_score)
            row_total = jnp.sum(early, axis=1, keepdims=True) + jnp.sum(
                late, axis=1, keepdims=True
            )
            part = contract(early.astype(jnp.bfloat16), values[:WINDOW], 1, 0) + contract(
                late.astype(jnp.bfloat16), values[WINDOW:], 1, 0
            )
            part = part * (1.0 / row_total)
            mixed = jnp.where(half_mask(mixed.shape, half), part, mixed)
            log_total = top_score + jnp.log(row_total)
            total_ref[0, 0, half : half + 1, rows] = jnp.sum(
                jnp.where(eye, log_total, 0.0), axis=0, keepdims=True
            )
        mixed_ref[0, rows, :] = mixed.astype(jnp.bfloat16)


def attention_forward(packed, low_pos):
    groups, key_len, width = packed.shape
    block_len = low_pos.shape[1]
    pairs = width // (3 * PAIR)
    pick = lambda seq, pair: (seq, 0, pair)
    return pl.pallas_call(
        forward_kernel,
        grid=(groups, pairs),
        in_specs=[
            pl.BlockSpec((1, key_len, 3 * PAIR), pick),
            pl.BlockSpec((1, block_len, 1), lambda seq, pair: (seq, 0, 0)),
        ],
        out_specs=[
            pl.BlockSpec((1, block_len, PAIR), pick),
            pl.BlockSpec((1, 1, 2, block_len), lambda seq, pair: (seq, pair, 0, 0)),
        ],
        out_shape=[
            jax.ShapeDtypeStruct((groups, block_len, pairs * PAIR), jnp.bfloat16),
            jax.ShapeDtypeStruct((groups, pairs, 2, block_len), jnp.float32),
        ],
        compiler_params=pltpu.CompilerParams(vmem_limit_bytes=40 << 20),
        cost_estimate=pl.CostEstimate(
            flops=16 * groups * pairs * block_len * (WINDOW + TILE) * HD,
            bytes_accessed=2 * groups * width * key_len,
            transcendentals=2 * groups * pairs * block_len * (WINDOW + TILE),
        ),
    )(packed, low_pos[:, :, None])


def backward_kernel(qkv_ref, mixed_ref, grad_ref, total_ref, low_ref, out_ref, gk_sum, gv_sum):
    block_len = mixed_ref.shape[1]
    first = qkv_ref.shape[1] - block_len
    span = WINDOW + TILE
    scale = HD ** (-0.5)
    gk_sum[...] = jnp.zeros_like(gk_sum)
    gv_sum[...] = jnp.zeros_like(gv_sum)
    eye = lax.broadcasted_iota(jnp.int32, (TILE, TILE), 0) == lax.broadcasted_iota(
        jnp.int32, (TILE, TILE), 1
    )
    for block in range(block_len // TILE):
        rows = pl.ds(block * TILE, TILE)
        window = pl.ds(block * TILE, span)
        queries = qkv_ref[0, pl.ds(first + block * TILE, TILE), :PAIR]
        queries = queries * jnp.asarray(scale, jnp.bfloat16)
        keys = qkv_ref[0, window, PAIR : 2 * PAIR]
        values = qkv_ref[0, window, 2 * PAIR :]
        grads = grad_ref[0, rows, :]
        product = grads.astype(jnp.float32) * mixed_ref[0, rows, :].astype(jnp.float32)
        low_pos = low_ref[0, :, rows] - block * TILE
        key_pos = lax.broadcasted_iota(jnp.int32, (span, TILE), 0)
        query_pos = lax.broadcasted_iota(jnp.int32, (TILE, TILE), 1) + WINDOW
        allowed = key_pos >= low_pos
        late_allowed = allowed[WINDOW:] & (key_pos[WINDOW:] <= query_pos)
        keys_t = jnp.transpose(keys)
        gq_parts = []
        for half in range(2):
            mask = half_mask(queries.shape, half)
            q_half = jnp.where(mask, queries, 0)
            g_half = jnp.where(mask, grads, 0)
            delta = jnp.sum(jnp.where(mask, product, 0.0), axis=1, keepdims=True)
            delta = jnp.sum(jnp.where(eye, delta, 0.0), axis=0, keepdims=True)
            log_total = total_ref[0, 0, half : half + 1, rows]
            scores = contract(keys, q_half, 1, 1)
            probs = jnp.concatenate(
                [
                    jnp.where(allowed[:WINDOW], jnp.exp(scores[:WINDOW] - log_total), 0.0),
                    jnp.where(late_allowed, jnp.exp(scores[WINDOW:] - log_total), 0.0),
                ]
            )
            grad_probs = contract(values, g_half, 1, 1)
            grad_scores = (probs * (grad_probs - delta)).astype(jnp.bfloat16)
            gv_sum[window, :] += contract(probs.astype(jnp.bfloat16), g_half, 1, 0)
            gk_sum[window, :] += contract(grad_scores, q_half, 1, 0)
            gq_parts.append(contract(keys_t[half * HD : (half + 1) * HD], grad_scores, 1, 0))
        gq = jnp.transpose(jnp.concatenate(gq_parts)) * scale
        out_ref[0, pl.ds(first + block * TILE, TILE), :PAIR] = gq.astype(jnp.bfloat16)
    out_ref[0, :first, :PAIR] = jnp.zeros((first, PAIR), jnp.bfloat16)
    out_ref[0, :, PAIR : 2 * PAIR] = gk_sum[...].astype(jnp.bfloat16)
    out_ref[0, :, 2 * PAIR :] = gv_sum[...].astype(jnp.bfloat16)


def attention_backward(packed, mixed, grads, log_total, low_pos):
    groups, key_len, width = packed.shape
    block_len = mixed.shape[1]
    pairs = width // (3 * PAIR)
    pick = lambda seq, pair: (seq, 0, pair)
    row_spec = pl.BlockSpec((1, block_len, PAIR), pick)
    packed_spec = pl.BlockSpec((1, key_len, 3 * PAIR), pick)
    return pl.pallas_call(
        backward_kernel,
        grid=(groups, pairs),
        in_specs=[
            packed_spec, row_spec, row_spec,
            pl.BlockSpec((1, 1, 2, block_len), lambda seq, pair: (seq, pair, 0, 0)),
            pl.BlockSpec((1, 1, block_len), lambda seq, pair: (seq, 0, 0)),
        ],
        out_specs=packed_spec,
        out_shape=jax.ShapeDtypeStruct(packed.shape, jnp.bfloat16),
        scratch_shapes=[
            pltpu.VMEM((key_len, PAIR), jnp.float32),
            pltpu.VMEM((key_len, PAIR), jnp.float32),
        ],
        compiler_params=pltpu.CompilerParams(vmem_limit_bytes=40 << 20),
        cost_estimate=pl.CostEstimate(
            flops=40 * groups * pairs * block_len * (WINDOW + TILE) * HD,
            bytes_accessed=4 * groups * width * key_len,
            transcendentals=2 * groups * pairs * block_len * (WINDOW + TILE),
        ),
    )(packed, mixed, grads, log_total, low_pos[:, None, :])


norm_eps = 1e-05


def mate(value):
    return lax.ppermute(value, "core", [(0, 1), (1, 0)])


def other_tp(value):
    return lax.ppermute(value, "tp", [(0, 1), (1, 0)])


def onward(value):
    count = lax.axis_size("ctx")
    return lax.ppermute(value, "ctx", [(i, i + 1) for i in range(count - 1)])


def backward_step(value):
    count = lax.axis_size("ctx")
    return lax.ppermute(value, "ctx", [(i + 1, i) for i in range(count - 1)])


class Place:
    def __init__(self):
        self.chips = lax.axis_size("x")
        self.core = lax.axis_index("core")
        self.shard = lax.axis_index("x") * 2 + self.core
        self.tp = lax.axis_index("tp")
        self.ctx = lax.axis_index("ctx")
        self.home = self.core == self.tp


def tie(*values):
    return lax.optimization_barrier(values)


def ordered(own, other, position, axis=0):
    return jnp.where(
        position == 0,
        jnp.stack([own, other], axis=axis),
        jnp.stack([other, own], axis=axis),
    )


class CoreSwap:
    def __init__(self, blocks, place):
        self.place = place
        self.kept = lax.dynamic_index_in_dim(blocks, place.core, 1, False)
        self.came = mate(lax.dynamic_index_in_dim(blocks, 1 - place.core, 1, False))

    def join(self):
        whole = ordered(self.kept, self.came, self.place.core, 1)
        return whole.reshape(-1, whole.shape[-1])


def gather_blocks(piece, place):
    whole = lax.all_gather(piece, ("x", "tp"), axis=0, tiled=False)
    return whole.reshape((place.chips, 2) + piece.shape)


def scatter_swap(grads, place):
    return CoreSwap(grads.reshape(place.chips, 2, -1, grads.shape[1]), place)


def scatter_sum(blocks):
    return lax.psum_scatter(blocks, ("x", "tp"), scatter_dimension=0, tiled=True)


def dot_f32(left_side, right_side):
    return jnp.dot(left_side, right_side, preferred_element_type=jnp.float32)


def dot_first(left_side, right_side):
    return contract(left_side, right_side, 0, 0)


def dot_second(left_side, right_side):
    return contract(left_side, right_side, 1, 1)


def gather_small(value, place):
    if place.chips != 2:
        return lax.all_gather(value, ("x", "core"), axis=1, tiled=True)
    near = mate(value)
    pair = ordered(value, near, place.core, 1).reshape(value.shape[0], -1)
    far = lax.ppermute(pair, "x", [(0, 1), (1, 0)])
    return ordered(pair, far, lax.axis_index("x"), 1).reshape(value.shape[0], -1)


def norm_forward(hidden, norm_gain, norm_shift):
    row_mean = jnp.mean(hidden, axis=-1, keepdims=True)
    centred = hidden - row_mean
    variance = jnp.mean(centred * centred, axis=-1, keepdims=True)
    inv_std = lax.rsqrt(variance + norm_eps)
    norm_hat = centred * inv_std
    return ((norm_hat * norm_gain + norm_shift).astype(jnp.bfloat16), norm_hat, inv_std)


def norm_backward(grad_out, norm_hat, inv_std, norm_gain):
    scaled = grad_out * norm_gain
    mean_one = jnp.mean(scaled, axis=-1, keepdims=True)
    mean_two = jnp.mean(scaled * norm_hat, axis=-1, keepdims=True)
    grad_input = inv_std * (scaled - mean_one - norm_hat * mean_two)
    return (grad_input, jnp.sum(grad_out * norm_hat, axis=0), jnp.sum(grad_out, axis=0))


def wide(value):
    return value.astype(jnp.float32)


def narrow(value):
    return value.astype(jnp.bfloat16)


def pick_block(value, index, count):
    size = value.shape[0] // count
    return lax.dynamic_slice_in_dim(value, index * size, size, 0)


def core_sum(own_part, mate_part):
    return own_part + wide(mate(narrow(mate_part)))


def gelu_slope(pre_act, grad_act):
    pullback = jax.vjp(lambda values: jax.nn.gelu(values, approximate=True), pre_act)[1]
    return pullback(grad_act)[0]


def pair_major(value):
    width = value.shape[-1]
    return jnp.concatenate(
        [value[kind, ..., at : at + PAIR] for at in range(0, width, PAIR) for kind in range(3)],
        axis=-1,
    )


def from_pair_major(value):
    width = value.shape[-1]
    return jnp.stack(
        [
            jnp.concatenate(
                [value[..., at : at + PAIR] for at in range(kind * PAIR, width, 3 * PAIR)], axis=-1
            )
            for kind in range(3)
        ]
    )


def per_device(
    tokens,
    cotangent,
    doc_lengths,
    norm_gains,
    norm_biases,
    qkv_weight,
    qv_bias,
    proj_weight,
    fc_weight,
    fc_bias,
    out_weight,
):
    place = Place()
    block_len, model_width = tokens.shape[1:]
    shard_rows = qkv_weight.shape[2]
    half_width = qkv_weight.shape[3]
    layer_count = qkv_weight.shape[0]
    reach = WINDOW // block_len
    key_len = (reach + 1) * block_len
    last = reach * block_len

    def my_seq(value):
        return lax.dynamic_index_in_dim(value, place.tp, 0, False)

    def both_seqs(own, other):
        return ordered(own, other, place.tp)

    def attn_piece(layer):
        return jnp.concatenate(
            [pair_major(qkv_weight[layer]), jnp.transpose(proj_weight[layer])], axis=1
        )

    own_tokens = my_seq(tokens)
    attn_blocks = gather_blocks(attn_piece(0), place)
    step_value = own_tokens
    halo = []
    for _ in range(reach):
        step_value = onward(step_value)
        halo.insert(0, step_value)
    vectors = jnp.concatenate([norm_gains, norm_biases], axis=1)
    vectors = gather_small(vectors.reshape(-1, vectors.shape[2]), place)
    vectors = wide(vectors).reshape(layer_count, 6, model_width)
    biases = jnp.concatenate([qv_bias.reshape(layer_count, -1), fc_bias], axis=1)
    biases = wide(jnp.where(place.home, biases, other_tp(biases)))
    lengths = my_seq(doc_lengths)
    lengths = jnp.stack([lengths, mate(lengths)])
    attn_blocks, later = tie(
        attn_blocks,
        (fc_weight[0], jnp.transpose(out_weight[0]), attn_piece(1),
         fc_weight[1], jnp.transpose(out_weight[1])),
    )
    fc_blocks = gather_blocks(later[0], place)
    out_blocks = gather_blocks(later[1], place)

    doc_ends = jnp.cumsum(lengths, axis=1)
    first_pos = place.ctx * block_len
    query_pos = first_pos + jnp.arange(block_len, dtype=jnp.int32)
    started = doc_ends[:, None, :] <= query_pos[None, :, None]
    doc_start = jnp.max(jnp.where(started, doc_ends[:, None, :], 0), axis=-1)
    low_pos = jnp.maximum(doc_start, query_pos[None, :] - (WINDOW - 1))
    low_pos = (low_pos - first_pos + last).astype(jnp.int32)

    hidden = wide(own_tokens)
    stash = []
    weights = []
    for layer in range(layer_count):
        gains, shifts = vectors[layer, :2], vectors[layer, 2:]
        bias_q, bias_v = biases[layer, :half_width], biases[layer, half_width : 2 * half_width]
        bias_qkv = pair_major(jnp.stack([bias_q, jnp.zeros_like(bias_q), bias_v])[:, None])
        bias_fc = biases[layer, 2 * half_width :]
        attn_in, hat_attn, inv_attn = norm_forward(hidden, gains[0], shifts[0])
        own_near = [attn_in]
        mate_near = [mate(attn_in)]
        step_value = attn_in
        for index in range(reach):
            if layer == 0:
                part = norm_forward(wide(halo[reach - 1 - index]), gains[0], shifts[0])[0]
            else:
                step_value = part = onward(step_value)
            own_near.insert(0, part)
            mate_near.insert(0, mate(part))
        near = jnp.concatenate(own_near + mate_near)
        attn_swap = CoreSwap(attn_blocks, place)
        w_attn = attn_swap.join()
        w_qkv, w_proj_t = w_attn[:, : 3 * half_width], w_attn[:, 3 * half_width :]
        packed = narrow(dot_f32(near, w_qkv) + bias_qkv).reshape(2, key_len, -1)
        mixed, log_total = attention_forward(packed, low_pos)
        mate_part = dot_second(mixed[1], w_proj_t)
        own_part = dot_second(mixed[0], w_proj_t)
        middle = hidden + core_sum(own_part, mate_part) + shifts[1]
        mlp_own, hat_mlp, inv_mlp = norm_forward(middle, gains[1], shifts[2])
        mlp_in = jnp.concatenate([mlp_own, mate(mlp_own)])
        mlp_in, fc_blocks = tie(mlp_in, fc_blocks)
        w_fc = CoreSwap(fc_blocks, place).join()
        if layer + 1 < layer_count:
            fc_blocks, piece = tie(fc_blocks, later[2])
            attn_blocks = gather_blocks(piece, place)
        pre_act = dot_f32(mlp_in, w_fc) + bias_fc
        activated = narrow(jax.nn.gelu(pre_act, approximate=True))
        activated, out_blocks = tie(activated, out_blocks)
        w_out_t = CoreSwap(out_blocks, place).join()
        if layer + 1 < layer_count:
            out_blocks, pieces = tie(out_blocks, later[3:])
            fc_blocks = gather_blocks(pieces[0], place)
            out_blocks = gather_blocks(pieces[1], place)
        mate_part = dot_second(activated[block_len:], w_out_t)
        own_part = dot_second(activated[:block_len], w_out_t)
        hidden = middle + core_sum(own_part, mate_part) + shifts[3]
        weights.append((w_qkv, w_proj_t, w_fc, w_out_t))
        stash.append(
            (near, hat_attn, inv_attn, packed, mixed, log_total, hat_mlp, inv_mlp, mlp_in,
             pre_act, activated)
        )

    own_output = narrow(hidden)
    output = both_seqs(own_output, other_tp(own_output))

    grad_hidden = wide(my_seq(cotangent))
    last_sum = None
    sums = {}
    waiting = []
    small_parts = [None] * layer_count

    def advance(value, name):
        nonlocal last_sum
        share = waiting.pop(0)
        assert share[0] == name
        value, share, last_sum = tie(value, share[1], last_sum)
        last_sum = lax.psum(share, "ctx")
        sums[name] = last_sum
        return value

    for layer in reversed(range(layer_count)):
        near, hat_attn, inv_attn, packed, mixed, log_total = stash[layer][:6]
        hat_mlp, inv_mlp, mlp_in, pre_act, activated = stash[layer][6:]
        gains = vectors[layer, :2]
        w_qkv, w_proj_t, w_fc, w_out_t = weights[layer]
        final = layer == 0
        grad_out_bias = jnp.sum(grad_hidden, axis=0)
        grad_low = narrow(grad_hidden)
        grad_low = jnp.concatenate([grad_low, mate(grad_low)])
        out_swap = scatter_swap(narrow(dot_first(grad_low, activated)), place)
        grad_pre = narrow(gelu_slope(pre_act, dot_f32(grad_low, w_out_t)))
        grad_pre, out_swap.came = tie(grad_pre, out_swap.came)
        waiting.append(("out%d" % layer, scatter_sum(out_swap.join())))
        grad_fc_bias = jnp.sum(wide(grad_pre), axis=0)
        mate_part = dot_second(grad_pre[block_len:], w_fc)
        own_part = dot_second(grad_pre[:block_len], w_fc)
        grad_norm_in = core_sum(own_part, mate_part)
        fc_swap = scatter_swap(narrow(dot_first(mlp_in, grad_pre)), place)
        if final:
            grad_norm_in = advance(grad_norm_in, "attn1")
        grad_from_mlp, grad_gain_mlp, grad_shift_mlp = norm_backward(
            grad_norm_in, hat_mlp, inv_mlp, gains[1]
        )
        grad_middle = grad_hidden + grad_from_mlp
        grad_proj_bias = jnp.sum(grad_middle, axis=0)
        grad_low = narrow(grad_middle)
        grad_low, fc_swap.came = tie(grad_low, fc_swap.came)
        waiting.append(("fc%d" % layer, scatter_sum(fc_swap.join())))
        grad_low = jnp.concatenate([grad_low, mate(grad_low)])
        grad_mixed = narrow(dot_f32(grad_low, w_proj_t)).reshape(mixed.shape)
        grad_proj = narrow(dot_first(grad_low, mixed.reshape(2 * block_len, half_width)))
        grad_packed = attention_backward(packed, mixed, grad_mixed, log_total, low_pos)
        grad_packed = advance(grad_packed, "out%d" % layer)
        mate_part = dot_second(grad_packed[1], w_qkv)
        own_part = dot_second(grad_packed[0], w_qkv)
        grad_near = core_sum(own_part, mate_part)
        far_total, grad_attn_in = grad_near[:last], grad_near[last:]
        carried = backward_step(narrow(far_total[:block_len]))
        rows = grad_packed.reshape(2 * key_len, -1)
        grad_attn = jnp.concatenate([narrow(dot_first(near, rows)), grad_proj], axis=1)
        attn_swap = scatter_swap(grad_attn, place)
        for step in range(1, reach + 1):
            if step == 1:
                carried, attn_swap.came = tie(carried, attn_swap.came)
                waiting.append(("attn%d" % layer, scatter_sum(attn_swap.join())))
            if step == 2:
                carried = advance(carried, "fc%d" % layer)
            arrived = wide(carried)
            if step < reach:
                section = far_total[step * block_len : (step + 1) * block_len]
                carried = backward_step(narrow(arrived + section))
            else:
                grad_attn_in = grad_attn_in + arrived
        grad_from_attn, grad_gain_attn, grad_shift_attn = norm_backward(
            grad_attn_in, hat_attn, inv_attn, gains[0]
        )
        grad_hidden = grad_middle + grad_from_attn
        grad_bias = jnp.sum(wide(rows), axis=0).reshape(-1, 3, PAIR)
        halves = jnp.concatenate(
            [grad_bias[:, 0].reshape(-1), grad_bias[:, 2].reshape(-1), grad_fc_bias]
        )
        empty = jnp.zeros_like(halves)
        small_parts[layer] = jnp.concatenate(
            [
                grad_gain_attn, grad_gain_mlp,
                grad_shift_attn, grad_proj_bias, grad_shift_mlp, grad_out_bias,
                jnp.where(place.core == 0, halves, empty),
                jnp.where(place.core == 1, halves, empty),
            ]
        )

    small = lax.psum(jnp.stack(small_parts), ("x", "core", "ctx", "tp"))
    far_grad = wide(other_tp(narrow(grad_hidden)))
    token_grad = both_seqs(grad_hidden, far_grad)
    advance((), "attn0")
    split = 6 * model_width
    norms = small[:, :split].reshape(layer_count, 6, model_width)
    norms = lax.dynamic_slice_in_dim(norms, place.shard * shard_rows, shard_rows, 2)
    halves = small[:, split:].reshape(layer_count, 2, -1)
    halves = lax.dynamic_index_in_dim(halves, place.tp, 1, False)
    packed_width = 3 * half_width
    attn = [sums["attn%d" % layer] for layer in range(layer_count)]
    return (
        output,
        token_grad,
        norms[:, :2],
        norms[:, 2:],
        jnp.stack([from_pair_major(wide(v[:, :packed_width])) for v in attn]),
        halves[:, : 2 * half_width].reshape(layer_count, 2, half_width),
        jnp.stack([jnp.transpose(wide(v[:, packed_width:])) for v in attn]),
        jnp.stack([wide(sums["fc%d" % layer]) for layer in range(layer_count)]),
        halves[:, 2 * half_width :],
        jnp.stack([jnp.transpose(wide(sums["out%d" % layer])) for layer in range(layer_count)]),
    )


def solution(mesh):
    devices = mesh.devices
    devices = devices.reshape((devices.shape[0] // 2, 2) + devices.shape[1:])
    mesh = jax.sharding.Mesh(devices, ("x", "core", "ctx", "tp"))
    placed = (
        P(("x", "core"), "ctx", None),
        P(("x", "core"), "ctx", None),
        P(("x", "core"), None),
        P(None, None, ("x", "core")),
        P(None, None, ("x", "core")),
        P(None, None, ("x", "core"), "tp"),
        P(None, None, "tp"),
        P(None, "tp", ("x", "core")),
        P(None, ("x", "core"), "tp"),
        P(None, "tp"),
        P(None, "tp", ("x", "core")),
    )
    return jax.shard_map(
        per_device,
        mesh=mesh,
        in_specs=placed,
        out_specs=(
            P(("x", "core"), "ctx", None),
            P(("x", "core"), "ctx", None),
            P(None, None, ("x", "core")),
            P(None, None, ("x", "core")),
            P(None, None, ("x", "core"), "tp"),
            P(None, None, "tp"),
            P(None, "tp", ("x", "core")),
            P(None, ("x", "core"), "tp"),
            P(None, "tp"),
            P(None, "tp", ("x", "core")),
        ),
        check_vma=False,
    )
```

```python
import jax
import jax.numpy as jnp
from jax import lax
from jax.experimental import pallas as pl
from jax.experimental.pallas import tpu as pltpu
from jax.sharding import PartitionSpec as P

HD = 64
WINDOW = 1024
TILE = 256
masked_score = -1e30


def contract(left_side, right_side, left_dim, right_dim):
    return lax.dot_general(
        left_side, right_side, (((left_dim,), (right_dim,)), ((), ())),
        preferred_element_type=jnp.float32,
    )


def half_mask(shape, half):
    lane = lax.broadcasted_iota(jnp.int32, shape, 1)
    return (lane < HD) if half == 0 else (lane >= HD)


PAIR = 2 * HD


def forward_kernel(qkv_ref, low_ref, mixed_ref, total_ref):
    block_len = mixed_ref.shape[1]
    first = qkv_ref.shape[1] - block_len
    span = WINDOW + TILE
    eye = lax.broadcasted_iota(jnp.int32, (TILE, TILE), 0) == lax.broadcasted_iota(
        jnp.int32, (TILE, TILE), 1
    )
    for block in range(block_len // TILE):
        rows = pl.ds(block * TILE, TILE)
        window = pl.ds(block * TILE, span)
        queries = qkv_ref[0, pl.ds(first + block * TILE, TILE), :PAIR]
        queries = queries * jnp.asarray(HD ** (-0.5), jnp.bfloat16)
        keys = qkv_ref[0, window, PAIR : 2 * PAIR]
        values = qkv_ref[0, window, 2 * PAIR :]
        low_pos = low_ref[0, rows, :] - block * TILE
        key_pos = lax.broadcasted_iota(jnp.int32, (TILE, span), 1)
        query_pos = lax.broadcasted_iota(jnp.int32, (TILE, TILE), 0) + WINDOW
        allowed = key_pos >= low_pos
        causal = key_pos[:, WINDOW:] <= query_pos
        mixed = jnp.zeros((TILE, 2 * HD), jnp.float32)
        for half in range(2):
            scores = contract(
                jnp.where(half_mask(queries.shape, half), queries, 0), keys, 1, 1
            )
            early = jnp.where(allowed[:, :WINDOW], scores[:, :WINDOW], masked_score)
            late = jnp.where(allowed[:, WINDOW:] & causal, scores[:, WINDOW:], masked_score)
            top_score = jnp.maximum(
                jnp.max(early, axis=1, keepdims=True), jnp.max(late, axis=1, keepdims=True)
            )
            early = jnp.exp(early - top_score)
            late = jnp.exp(late - top_score)
            row_total = jnp.sum(early, axis=1, keepdims=True) + jnp.sum(
                late, axis=1, keepdims=True
            )
            part = contract(early.astype(jnp.bfloat16), values[:WINDOW], 1, 0) + contract(
                late.astype(jnp.bfloat16), values[WINDOW:], 1, 0
            )
            part = part * (1.0 / row_total)
            mixed = jnp.where(half_mask(mixed.shape, half), part, mixed)
            log_total = top_score + jnp.log(row_total)
            total_ref[0, 0, half : half + 1, rows] = jnp.sum(
                jnp.where(eye, log_total, 0.0), axis=0, keepdims=True
            )
        mixed_ref[0, rows, :] = mixed.astype(jnp.bfloat16)


def attention_forward(packed, low_pos):
    groups, key_len, width = packed.shape
    block_len = low_pos.shape[1]
    pairs = width // (3 * PAIR)
    pick = lambda seq, pair: (seq, 0, pair)
    return pl.pallas_call(
        forward_kernel,
        grid=(groups, pairs),
        in_specs=[
            pl.BlockSpec((1, key_len, 3 * PAIR), pick),
            pl.BlockSpec((1, block_len, 1), lambda seq, pair: (seq, 0, 0)),
        ],
        out_specs=[
            pl.BlockSpec((1, block_len, PAIR), pick),
            pl.BlockSpec((1, 1, 2, block_len), lambda seq, pair: (seq, pair, 0, 0)),
        ],
        out_shape=[
            jax.ShapeDtypeStruct((groups, block_len, pairs * PAIR), jnp.bfloat16),
            jax.ShapeDtypeStruct((groups, pairs, 2, block_len), jnp.float32),
        ],
        compiler_params=pltpu.CompilerParams(vmem_limit_bytes=40 << 20),
        cost_estimate=pl.CostEstimate(
            flops=16 * groups * pairs * block_len * (WINDOW + TILE) * HD,
            bytes_accessed=2 * groups * width * key_len,
            transcendentals=2 * groups * pairs * block_len * (WINDOW + TILE),
        ),
    )(packed, low_pos[:, :, None])


def backward_kernel(qkv_ref, mixed_ref, grad_ref, total_ref, low_ref, out_ref, gk_sum, gv_sum):
    block_len = mixed_ref.shape[1]
    first = qkv_ref.shape[1] - block_len
    span = WINDOW + TILE
    scale = HD ** (-0.5)
    gk_sum[...] = jnp.zeros_like(gk_sum)
    gv_sum[...] = jnp.zeros_like(gv_sum)
    eye = lax.broadcasted_iota(jnp.int32, (TILE, TILE), 0) == lax.broadcasted_iota(
        jnp.int32, (TILE, TILE), 1
    )
    for block in range(block_len // TILE):
        rows = pl.ds(block * TILE, TILE)
        window = pl.ds(block * TILE, span)
        queries = qkv_ref[0, pl.ds(first + block * TILE, TILE), :PAIR]
        queries = queries * jnp.asarray(scale, jnp.bfloat16)
        keys = qkv_ref[0, window, PAIR : 2 * PAIR]
        values = qkv_ref[0, window, 2 * PAIR :]
        grads = grad_ref[0, rows, :]
        product = grads.astype(jnp.float32) * mixed_ref[0, rows, :].astype(jnp.float32)
        low_pos = low_ref[0, :, rows] - block * TILE
        key_pos = lax.broadcasted_iota(jnp.int32, (span, TILE), 0)
        query_pos = lax.broadcasted_iota(jnp.int32, (TILE, TILE), 1) + WINDOW
        allowed = key_pos >= low_pos
        late_allowed = allowed[WINDOW:] & (key_pos[WINDOW:] <= query_pos)
        keys_t = jnp.transpose(keys)
        gq_parts = []
        for half in range(2):
            mask = half_mask(queries.shape, half)
            q_half = jnp.where(mask, queries, 0)
            g_half = jnp.where(mask, grads, 0)
            delta = jnp.sum(jnp.where(mask, product, 0.0), axis=1, keepdims=True)
            delta = jnp.sum(jnp.where(eye, delta, 0.0), axis=0, keepdims=True)
            log_total = total_ref[0, 0, half : half + 1, rows]
            scores = contract(keys, q_half, 1, 1)
            probs = jnp.concatenate(
                [
                    jnp.where(allowed[:WINDOW], jnp.exp(scores[:WINDOW] - log_total), 0.0),
                    jnp.where(late_allowed, jnp.exp(scores[WINDOW:] - log_total), 0.0),
                ]
            )
            grad_probs = contract(values, g_half, 1, 1)
            grad_scores = (probs * (grad_probs - delta)).astype(jnp.bfloat16)
            gv_sum[window, :] += contract(probs.astype(jnp.bfloat16), g_half, 1, 0)
            gk_sum[window, :] += contract(grad_scores, q_half, 1, 0)
            gq_parts.append(contract(keys_t[half * HD : (half + 1) * HD], grad_scores, 1, 0))
        gq = jnp.transpose(jnp.concatenate(gq_parts)) * scale
        out_ref[0, pl.ds(first + block * TILE, TILE), :PAIR] = gq.astype(jnp.bfloat16)
    out_ref[0, :first, :PAIR] = jnp.zeros((first, PAIR), jnp.bfloat16)
    out_ref[0, :, PAIR : 2 * PAIR] = gk_sum[...].astype(jnp.bfloat16)
    out_ref[0, :, 2 * PAIR :] = gv_sum[...].astype(jnp.bfloat16)


def attention_backward(packed, mixed, grads, log_total, low_pos):
    groups, key_len, width = packed.shape
    block_len = mixed.shape[1]
    pairs = width // (3 * PAIR)
    pick = lambda seq, pair: (seq, 0, pair)
    row_spec = pl.BlockSpec((1, block_len, PAIR), pick)
    packed_spec = pl.BlockSpec((1, key_len, 3 * PAIR), pick)
    return pl.pallas_call(
        backward_kernel,
        grid=(groups, pairs),
        in_specs=[
            packed_spec, row_spec, row_spec,
            pl.BlockSpec((1, 1, 2, block_len), lambda seq, pair: (seq, pair, 0, 0)),
            pl.BlockSpec((1, 1, block_len), lambda seq, pair: (seq, 0, 0)),
        ],
        out_specs=packed_spec,
        out_shape=jax.ShapeDtypeStruct(packed.shape, jnp.bfloat16),
        scratch_shapes=[
            pltpu.VMEM((key_len, PAIR), jnp.float32),
            pltpu.VMEM((key_len, PAIR), jnp.float32),
        ],
        compiler_params=pltpu.CompilerParams(vmem_limit_bytes=40 << 20),
        cost_estimate=pl.CostEstimate(
            flops=40 * groups * pairs * block_len * (WINDOW + TILE) * HD,
            bytes_accessed=4 * groups * width * key_len,
            transcendentals=2 * groups * pairs * block_len * (WINDOW + TILE),
        ),
    )(packed, mixed, grads, log_total, low_pos[:, None, :])


norm_eps = 1e-05


def mate(value):
    return lax.ppermute(value, "core", [(0, 1), (1, 0)])


def other_tp(value):
    return lax.ppermute(value, "tp", [(0, 1), (1, 0)])


def onward(value):
    count = lax.axis_size("ctx")
    return lax.ppermute(value, "ctx", [(i, i + 1) for i in range(count - 1)])


def backward_step(value):
    count = lax.axis_size("ctx")
    return lax.ppermute(value, "ctx", [(i + 1, i) for i in range(count - 1)])


class Place:
    def __init__(self):
        self.chips = lax.axis_size("x")
        self.core = lax.axis_index("core")
        self.shard = lax.axis_index("x") * 2 + self.core
        self.tp = lax.axis_index("tp")
        self.ctx = lax.axis_index("ctx")
        self.home = self.core == self.tp


def tie(*values):
    return lax.optimization_barrier(values)


def ordered(own, other, position, axis=0):
    return jnp.where(
        position == 0,
        jnp.stack([own, other], axis=axis),
        jnp.stack([other, own], axis=axis),
    )


class CoreSwap:
    def __init__(self, blocks, place):
        self.place = place
        self.blocks = blocks
        self.came = mate(jnp.where(place.core == 0, blocks[:, 1], blocks[:, 0]))

    def join(self):
        whole = jnp.where(
            self.place.core == 0,
            jnp.stack([self.blocks[:, 0], self.came], axis=1),
            jnp.stack([self.came, self.blocks[:, 1]], axis=1),
        )
        return whole.reshape(-1, whole.shape[-1])


def gather_blocks(piece, place):
    whole = lax.all_gather(piece, ("x", "tp"), axis=0, tiled=False)
    return whole.reshape((place.chips, 2) + piece.shape)


def scatter_swap(grads, place):
    return CoreSwap(grads.reshape(place.chips, 2, -1, grads.shape[1]), place)


def scatter_sum(blocks):
    return lax.psum_scatter(blocks, ("x", "tp"), scatter_dimension=0, tiled=True)


def dot_f32(left_side, right_side):
    return jnp.dot(left_side, right_side, preferred_element_type=jnp.float32)


def dot_first(left_side, right_side):
    return contract(left_side, right_side, 0, 0)


def dot_second(left_side, right_side):
    return contract(left_side, right_side, 1, 1)


def gather_small(value, place):
    if place.chips != 2:
        return lax.all_gather(value, ("x", "core"), axis=1, tiled=True)
    near = mate(value)
    pair = ordered(value, near, place.core, 1).reshape(value.shape[0], -1)
    far = lax.ppermute(pair, "x", [(0, 1), (1, 0)])
    return ordered(pair, far, lax.axis_index("x"), 1).reshape(value.shape[0], -1)


def norm_forward(hidden, norm_gain, norm_shift):
    row_mean = jnp.mean(hidden, axis=-1, keepdims=True)
    centred = hidden - row_mean
    variance = jnp.mean(centred * centred, axis=-1, keepdims=True)
    inv_std = lax.rsqrt(variance + norm_eps)
    norm_hat = centred * inv_std
    return ((norm_hat * norm_gain + norm_shift).astype(jnp.bfloat16), norm_hat, inv_std)


def norm_backward(grad_out, norm_hat, inv_std, norm_gain):
    scaled = grad_out * norm_gain
    mean_one = jnp.mean(scaled, axis=-1, keepdims=True)
    mean_two = jnp.mean(scaled * norm_hat, axis=-1, keepdims=True)
    grad_input = inv_std * (scaled - mean_one - norm_hat * mean_two)
    return (grad_input, jnp.sum(grad_out * norm_hat, axis=0), jnp.sum(grad_out, axis=0))


def wide(value):
    return value.astype(jnp.float32)


def narrow(value):
    return value.astype(jnp.bfloat16)


def pick_block(value, index, count):
    size = value.shape[0] // count
    return lax.dynamic_slice_in_dim(value, index * size, size, 0)


def small_total(value, place):
    if place.chips != 2 or lax.axis_size("ctx") != 4:
        return lax.psum(value, ("x", "core", "ctx", "tp"))
    value = value + mate(value)
    value = value + other_tp(value)
    value = value + lax.ppermute(value, "x", [(0, 1), (1, 0)])
    value = value + lax.ppermute(value, "ctx", [(0, 1), (3, 2)])
    value = value + lax.ppermute(value, "ctx", [(1, 2), (2, 1)])
    outer = (place.ctx == 0) | (place.ctx == 3)
    return jnp.where(outer, lax.ppermute(value, "ctx", [(1, 0), (2, 3)]), value)


def core_sum(own_part, mate_part):
    return own_part + wide(mate(narrow(mate_part)))


def gelu_slope(pre_act, grad_act):
    pullback = jax.vjp(lambda values: jax.nn.gelu(values, approximate=True), pre_act)[1]
    return pullback(grad_act)[0]


def pair_major(value):
    width = value.shape[-1]
    return jnp.concatenate(
        [value[kind, :, at : at + PAIR] for at in range(0, width, PAIR) for kind in range(3)],
        axis=-1,
    )


def pack_kernel(qkv_ref, proj_ref, out_ref):
    step = pl.program_id(0)
    head_steps = pl.num_programs(0) // 4 * 3

    @pl.when(step < head_steps)
    def _():
        out_ref[...] = qkv_ref[0, 0]

    @pl.when(step >= head_steps)
    def _():
        out_ref[...] = jnp.transpose(proj_ref[0])


def attn_piece(layer, qkv_weight, proj_weight):
    rows, width = qkv_weight.shape[2:]
    head_steps = 3 * width // PAIR

    def qkv_place(step):
        step = jnp.minimum(step, head_steps - 1)
        return (layer, step % 3, 0, step // 3)

    return pl.pallas_call(
        pack_kernel,
        grid=(head_steps + width // PAIR,),
        in_specs=[
            pl.BlockSpec((1, 1, rows, PAIR), qkv_place),
            pl.BlockSpec(
                (1, PAIR, rows), lambda step: (layer, jnp.maximum(step - head_steps, 0), 0)
            ),
        ],
        out_specs=pl.BlockSpec((rows, PAIR), lambda step: (0, step)),
        out_shape=jax.ShapeDtypeStruct((rows, 4 * width), jnp.bfloat16),
    )(qkv_weight, proj_weight)


def unpack_kernel(first_ref, second_ref, out_ref):
    out_ref[0, 0] = first_ref[...].astype(jnp.float32)
    out_ref[1, 0] = second_ref[...].astype(jnp.float32)


def unpack_heads(first, second):
    rows, width = first.shape
    width = width // 4
    block = pl.BlockSpec((rows, PAIR), lambda step: (0, step))
    return pl.pallas_call(
        unpack_kernel,
        grid=(3 * width // PAIR,),
        in_specs=[block, block],
        out_specs=pl.BlockSpec((2, 1, rows, PAIR), lambda step: (0, step % 3, 0, step // 3)),
        out_shape=jax.ShapeDtypeStruct((2, 3, rows, width), jnp.float32),
    )(first, second)


def per_device(
    tokens,
    cotangent,
    doc_lengths,
    norm_gains,
    norm_biases,
    qkv_weight,
    qv_bias,
    proj_weight,
    fc_weight,
    fc_bias,
    out_weight,
):
    place = Place()
    block_len, model_width = tokens.shape[1:]
    shard_rows = qkv_weight.shape[2]
    half_width = qkv_weight.shape[3]
    layer_count = qkv_weight.shape[0]
    reach = WINDOW // block_len
    key_len = (reach + 1) * block_len
    last = reach * block_len

    def my_seq(value):
        return lax.dynamic_index_in_dim(value, place.tp, 0, False)

    def both_seqs(own, other):
        return ordered(own, other, place.tp)

    own_tokens = my_seq(tokens)
    attn_blocks = gather_blocks(attn_piece(0, qkv_weight, proj_weight), place)
    halo = [onward(own_tokens)]
    for _ in range(reach - 1):
        halo.insert(0, onward(halo[0]))
    vectors = jnp.concatenate([norm_gains, norm_biases], axis=1)
    vectors = gather_small(vectors.reshape(-1, vectors.shape[2]), place)
    vectors = wide(vectors).reshape(layer_count, 6, model_width)
    biases = jnp.concatenate([qv_bias.reshape(layer_count, -1), fc_bias], axis=1)
    biases = wide(jnp.where(place.home, biases, other_tp(biases)))
    lengths = my_seq(doc_lengths)
    lengths = jnp.stack([lengths, mate(lengths)])
    mlp_pieces = [
        jnp.concatenate([fc_weight[layer], jnp.transpose(out_weight[layer])], axis=1)
        for layer in range(layer_count)
    ]
    attn_later = attn_piece(1, qkv_weight, proj_weight)
    halo[-1], mlp_pieces, attn_later = tie(halo[-1], mlp_pieces, attn_later)
    mlp_blocks = gather_blocks(mlp_pieces[0], place)
    fc_width = fc_weight.shape[2]

    doc_ends = jnp.cumsum(lengths, axis=1)
    first_pos = place.ctx * block_len
    query_pos = first_pos + jnp.arange(block_len, dtype=jnp.int32)
    started = doc_ends[:, None, :] <= query_pos[None, :, None]
    doc_start = jnp.max(jnp.where(started, doc_ends[:, None, :], 0), axis=-1)
    low_pos = jnp.maximum(doc_start, query_pos[None, :] - (WINDOW - 1))
    low_pos = (low_pos - first_pos + last).astype(jnp.int32)

    hidden = wide(own_tokens)
    stash = []
    weights = []
    for layer in range(layer_count):
        gains, shifts = vectors[layer, :2], vectors[layer, 2:]
        bias_q, bias_v = biases[layer, :half_width], biases[layer, half_width : 2 * half_width]
        bias_qkv = pair_major(jnp.stack([bias_q, jnp.zeros_like(bias_q), bias_v])[:, None])
        bias_fc = biases[layer, 2 * half_width :]
        attn_in, hat_attn, inv_attn = norm_forward(hidden, gains[0], shifts[0])
        own_near = [attn_in]
        mate_near = [mate(attn_in)]
        step_value = attn_in
        for index in range(reach):
            if layer == 0:
                part = norm_forward(wide(halo[reach - 1 - index]), gains[0], shifts[0])[0]
            else:
                step_value = part = onward(step_value)
            own_near.insert(0, part)
            mate_near.insert(0, mate(part))
        near = jnp.concatenate(own_near + mate_near)
        attn_swap = CoreSwap(attn_blocks, place)
        w_attn = attn_swap.join()
        w_qkv, w_proj_t = w_attn[:, : 3 * half_width], w_attn[:, 3 * half_width :]
        packed = narrow(dot_f32(near, w_qkv) + bias_qkv).reshape(2, key_len, -1)
        mixed, log_total = attention_forward(packed, low_pos)
        if layer + 1 < layer_count:
            mixed, attn_later = tie(mixed, attn_later)
            attn_blocks = gather_blocks(attn_later, place)
        mate_part = dot_second(mixed[1], w_proj_t)
        own_part = dot_second(mixed[0], w_proj_t)
        middle = hidden + core_sum(own_part, mate_part) + shifts[1]
        mlp_own, hat_mlp, inv_mlp = norm_forward(middle, gains[1], shifts[2])
        mlp_in = jnp.concatenate([mlp_own, mate(mlp_own)])
        mlp_in, mlp_blocks = tie(mlp_in, mlp_blocks)
        w_fc = CoreSwap(mlp_blocks[..., :fc_width], place).join()
        out_swap = CoreSwap(mlp_blocks[..., fc_width:], place)
        if layer + 1 < layer_count:
            w_fc, piece = tie(w_fc, mlp_pieces[layer + 1])
            mlp_blocks = gather_blocks(piece, place)
        pre_act = dot_f32(mlp_in, w_fc) + bias_fc
        activated = narrow(jax.nn.gelu(pre_act, approximate=True))
        w_out_t = out_swap.join()
        mate_part = dot_second(activated[block_len:], w_out_t)
        own_part = dot_second(activated[:block_len], w_out_t)
        hidden = middle + core_sum(own_part, mate_part) + shifts[3]
        weights.append((w_qkv, w_proj_t, w_fc, w_out_t))
        stash.append(
            (near, hat_attn, inv_attn, packed, mixed, log_total, hat_mlp, inv_mlp, mlp_in,
             pre_act, activated)
        )

    own_output = narrow(hidden)
    output = both_seqs(own_output, other_tp(own_output))

    grad_hidden, _ = tie(wide(my_seq(cotangent)), own_output)
    last_sum = None
    sums = {}
    waiting, latest, first_sum = [], [], []
    small_parts = [None] * layer_count

    def advance(value, name):
        nonlocal last_sum
        share = waiting.pop(0)
        assert share[0] == name
        value, share, last_sum = tie(value, share[1], last_sum)
        if latest:
            sums[latest[0]] = last_sum
        else:
            first_sum.append(last_sum)
        latest[:] = [name]
        last_sum = lax.psum(share, "ctx")
        sums[name] = last_sum
        return value

    for layer in reversed(range(layer_count)):
        near, hat_attn, inv_attn, packed, mixed, log_total = stash[layer][:6]
        hat_mlp, inv_mlp, mlp_in, pre_act, activated = stash[layer][6:]
        gains = vectors[layer, :2]
        w_qkv, w_proj_t, w_fc, w_out_t = weights[layer]
        final = layer == 0
        grad_out_bias = jnp.sum(grad_hidden, axis=0)
        if not final:
            bias_parts = jnp.sum(grad_hidden.reshape(16, -1, model_width), axis=1)
            grad_hidden, bias_parts = tie(grad_hidden, bias_parts)
            bias_parts = lax.psum(bias_parts, ("x", "core", "ctx", "tp"))
            last_sum = bias_parts
        grad_low = narrow(grad_hidden)
        grad_low = jnp.concatenate([grad_low, mate(grad_low)])
        out_swap = scatter_swap(narrow(dot_first(grad_low, activated)), place)
        grad_pre = narrow(gelu_slope(pre_act, dot_f32(grad_low, w_out_t)))
        grad_pre, out_swap.came = tie(grad_pre, out_swap.came)
        waiting.append(("out%d" % layer, scatter_sum(out_swap.join())))
        grad_fc_bias = jnp.sum(wide(grad_pre), axis=0)
        mate_part = dot_second(grad_pre[block_len:], w_fc)
        own_part = dot_second(grad_pre[:block_len], w_fc)
        grad_norm_in = core_sum(own_part, mate_part)
        fc_swap = scatter_swap(narrow(dot_first(mlp_in, grad_pre)), place)
        if final:
            grad_norm_in = advance(grad_norm_in, "attn1")
        grad_from_mlp, grad_gain_mlp, grad_shift_mlp = norm_backward(
            grad_norm_in, hat_mlp, inv_mlp, gains[1]
        )
        grad_middle = grad_hidden + grad_from_mlp
        grad_proj_bias = jnp.sum(grad_middle, axis=0)
        grad_low = narrow(grad_middle)
        grad_low, fc_swap.came = tie(grad_low, fc_swap.came)
        waiting.append(("fc%d" % layer, scatter_sum(fc_swap.join())))
        grad_low = jnp.concatenate([grad_low, mate(grad_low)])
        grad_mixed = narrow(dot_f32(grad_low, w_proj_t)).reshape(mixed.shape)
        grad_proj = narrow(dot_first(grad_low, mixed.reshape(2 * block_len, half_width)))
        grad_packed = attention_backward(packed, mixed, grad_mixed, log_total, low_pos)
        grad_packed = advance(grad_packed, "out%d" % layer)
        mate_part = dot_second(grad_packed[1], w_qkv)
        own_part = dot_second(grad_packed[0], w_qkv)
        grad_near = core_sum(own_part, mate_part)
        far_total, grad_attn_in = grad_near[:last], grad_near[last:]
        carried = backward_step(narrow(far_total[:block_len]))
        rows = grad_packed.reshape(2 * key_len, -1)
        grad_attn = jnp.concatenate([narrow(dot_first(near, rows)), grad_proj], axis=1)
        attn_swap = scatter_swap(grad_attn, place)
        for step in range(1, reach + 1):
            if step == 1:
                carried, attn_swap.came = tie(carried, attn_swap.came)
                waiting.append(("attn%d" % layer, scatter_sum(attn_swap.join())))
            if step == 2:
                carried = advance(carried, "fc%d" % layer)
            arrived = wide(carried)
            if step < reach:
                section = far_total[step * block_len : (step + 1) * block_len]
                carried = backward_step(narrow(arrived + section))
            else:
                grad_attn_in = grad_attn_in + arrived
        grad_from_attn, grad_gain_attn, grad_shift_attn = norm_backward(
            grad_attn_in, hat_attn, inv_attn, gains[0]
        )
        grad_hidden = grad_middle + grad_from_attn
        grad_bias = jnp.sum(wide(rows), axis=0).reshape(-1, 3, PAIR)
        halves = jnp.concatenate(
            [grad_bias[:, 0].reshape(-1), grad_bias[:, 2].reshape(-1), grad_fc_bias]
        )
        empty = jnp.zeros_like(halves)
        small_parts[layer] = jnp.concatenate(
            [
                grad_gain_attn, grad_gain_mlp,
                grad_shift_attn, grad_proj_bias, grad_shift_mlp, grad_out_bias,
                jnp.where(place.core == 0, halves, empty),
                jnp.where(place.core == 1, halves, empty),
            ]
        )

    small = small_total(jnp.stack(small_parts), place)
    far_grad = wide(other_tp(narrow(grad_hidden)))
    token_grad = both_seqs(grad_hidden, far_grad)
    advance((), "attn0")
    split = 6 * model_width
    norms = small[:, :split].reshape(layer_count, 6, model_width)
    norms = norms.at[1, 5].set(jnp.sum(first_sum[0], axis=0))
    norms = lax.dynamic_slice_in_dim(norms, place.shard * shard_rows, shard_rows, 2)
    halves = small[:, split:].reshape(layer_count, 2, -1)
    halves = lax.dynamic_index_in_dim(halves, place.tp, 1, False)
    packed_width = 3 * half_width
    attn = [sums["attn%d" % layer] for layer in range(layer_count)]
    return (
        output,
        token_grad,
        norms[:, :2],
        norms[:, 2:],
        unpack_heads(*attn),
        halves[:, : 2 * half_width].reshape(layer_count, 2, half_width),
        jnp.stack([jnp.transpose(wide(v[:, packed_width:])) for v in attn]),
        jnp.stack([wide(sums["fc%d" % layer]) for layer in range(layer_count)]),
        halves[:, 2 * half_width :],
        jnp.stack([jnp.transpose(wide(sums["out%d" % layer])) for layer in range(layer_count)]),
    )


def solution(mesh):
    devices = mesh.devices
    devices = devices.reshape((devices.shape[0] // 2, 2) + devices.shape[1:])
    mesh = jax.sharding.Mesh(devices, ("x", "core", "ctx", "tp"))
    placed = (
        P(("x", "core"), "ctx", None),
        P(("x", "core"), "ctx", None),
        P(("x", "core"), None),
        P(None, None, ("x", "core")),
        P(None, None, ("x", "core")),
        P(None, None, ("x", "core"), "tp"),
        P(None, None, "tp"),
        P(None, "tp", ("x", "core")),
        P(None, ("x", "core"), "tp"),
        P(None, "tp"),
        P(None, "tp", ("x", "core")),
    )
    return jax.shard_map(
        per_device,
        mesh=mesh,
        in_specs=placed,
        out_specs=(
            P(("x", "core"), "ctx", None),
            P(("x", "core"), "ctx", None),
            P(None, None, ("x", "core")),
            P(None, None, ("x", "core")),
            P(None, None, ("x", "core"), "tp"),
            P(None, None, "tp"),
            P(None, "tp", ("x", "core")),
            P(None, ("x", "core"), "tp"),
            P(None, "tp"),
            P(None, "tp", ("x", "core")),
        ),
        check_vma=False,
    )
```

```python
import jax
import jax.numpy as jnp
from jax import lax
from jax.experimental import pallas as pl
from jax.experimental.pallas import tpu as pltpu
from jax.sharding import PartitionSpec as P

HD = 64
WINDOW = 1024
TILE = 256
masked_score = -1e30


def contract(left_side, right_side, left_dim, right_dim):
    return lax.dot_general(
        left_side, right_side, (((left_dim,), (right_dim,)), ((), ())),
        preferred_element_type=jnp.float32,
    )


def half_mask(shape, half):
    lane = lax.broadcasted_iota(jnp.int32, shape, 1)
    return (lane < HD) if half == 0 else (lane >= HD)


PAIR = 2 * HD


def forward_kernel(qkv_ref, low_ref, mixed_ref, total_ref):
    block_len = mixed_ref.shape[1]
    first = qkv_ref.shape[1] - block_len
    span = WINDOW + TILE
    eye = lax.broadcasted_iota(jnp.int32, (TILE, TILE), 0) == lax.broadcasted_iota(
        jnp.int32, (TILE, TILE), 1
    )
    for block in range(block_len // TILE):
        rows = pl.ds(block * TILE, TILE)
        window = pl.ds(block * TILE, span)
        queries = qkv_ref[0, pl.ds(first + block * TILE, TILE), :PAIR]
        queries = queries * jnp.asarray(HD ** (-0.5), jnp.bfloat16)
        keys = qkv_ref[0, window, PAIR : 2 * PAIR]
        values = qkv_ref[0, window, 2 * PAIR :]
        low_pos = low_ref[0, rows, :] - block * TILE
        key_pos = lax.broadcasted_iota(jnp.int32, (TILE, span), 1)
        query_pos = lax.broadcasted_iota(jnp.int32, (TILE, TILE), 0) + WINDOW
        allowed = key_pos >= low_pos
        causal = key_pos[:, WINDOW:] <= query_pos
        mixed = jnp.zeros((TILE, 2 * HD), jnp.float32)
        for half in range(2):
            scores = contract(
                jnp.where(half_mask(queries.shape, half), queries, 0), keys, 1, 1
            )
            early = jnp.where(allowed[:, :WINDOW], scores[:, :WINDOW], masked_score)
            late = jnp.where(allowed[:, WINDOW:] & causal, scores[:, WINDOW:], masked_score)
            top_score = jnp.maximum(
                jnp.max(early, axis=1, keepdims=True), jnp.max(late, axis=1, keepdims=True)
            )
            early = jnp.exp(early - top_score)
            late = jnp.exp(late - top_score)
            row_total = jnp.sum(early, axis=1, keepdims=True) + jnp.sum(
                late, axis=1, keepdims=True
            )
            part = contract(early.astype(jnp.bfloat16), values[:WINDOW], 1, 0) + contract(
                late.astype(jnp.bfloat16), values[WINDOW:], 1, 0
            )
            part = part * (1.0 / row_total)
            mixed = jnp.where(half_mask(mixed.shape, half), part, mixed)
            log_total = top_score + jnp.log(row_total)
            total_ref[0, 0, half : half + 1, rows] = jnp.sum(
                jnp.where(eye, log_total, 0.0), axis=0, keepdims=True
            )
        mixed_ref[0, rows, :] = mixed.astype(jnp.bfloat16)


def attention_forward(packed, low_pos):
    groups, key_len, width = packed.shape
    block_len = low_pos.shape[1]
    pairs = width // (3 * PAIR)
    pick = lambda seq, pair: (seq, 0, pair)
    return pl.pallas_call(
        forward_kernel,
        grid=(groups, pairs),
        in_specs=[
            pl.BlockSpec((1, key_len, 3 * PAIR), pick),
            pl.BlockSpec((1, block_len, 1), lambda seq, pair: (seq, 0, 0)),
        ],
        out_specs=[
            pl.BlockSpec((1, block_len, PAIR), pick),
            pl.BlockSpec((1, 1, 2, block_len), lambda seq, pair: (seq, pair, 0, 0)),
        ],
        out_shape=[
            jax.ShapeDtypeStruct((groups, block_len, pairs * PAIR), jnp.bfloat16),
            jax.ShapeDtypeStruct((groups, pairs, 2, block_len), jnp.float32),
        ],
        compiler_params=pltpu.CompilerParams(vmem_limit_bytes=40 << 20),
        cost_estimate=pl.CostEstimate(
            flops=16 * groups * pairs * block_len * (WINDOW + TILE) * HD,
            bytes_accessed=2 * groups * width * key_len,
            transcendentals=2 * groups * pairs * block_len * (WINDOW + TILE),
        ),
    )(packed, low_pos[:, :, None])


def backward_kernel(qkv_ref, mixed_ref, grad_ref, total_ref, low_ref, out_ref, gk_sum, gv_sum):
    block_len = mixed_ref.shape[1]
    first = qkv_ref.shape[1] - block_len
    span = WINDOW + TILE
    scale = HD ** (-0.5)
    gk_sum[...] = jnp.zeros_like(gk_sum)
    gv_sum[...] = jnp.zeros_like(gv_sum)
    eye = lax.broadcasted_iota(jnp.int32, (TILE, TILE), 0) == lax.broadcasted_iota(
        jnp.int32, (TILE, TILE), 1
    )
    for block in range(block_len // TILE):
        rows = pl.ds(block * TILE, TILE)
        window = pl.ds(block * TILE, span)
        queries = qkv_ref[0, pl.ds(first + block * TILE, TILE), :PAIR]
        queries = queries * jnp.asarray(scale, jnp.bfloat16)
        keys = qkv_ref[0, window, PAIR : 2 * PAIR]
        values = qkv_ref[0, window, 2 * PAIR :]
        grads = grad_ref[0, rows, :]
        product = grads.astype(jnp.float32) * mixed_ref[0, rows, :].astype(jnp.float32)
        low_pos = low_ref[0, :, rows] - block * TILE
        key_pos = lax.broadcasted_iota(jnp.int32, (span, TILE), 0)
        query_pos = lax.broadcasted_iota(jnp.int32, (TILE, TILE), 1) + WINDOW
        allowed = key_pos >= low_pos
        late_allowed = allowed[WINDOW:] & (key_pos[WINDOW:] <= query_pos)
        keys_t = jnp.transpose(keys)
        gq_parts = []
        for half in range(2):
            mask = half_mask(queries.shape, half)
            q_half = jnp.where(mask, queries, 0)
            g_half = jnp.where(mask, grads, 0)
            delta = jnp.sum(jnp.where(mask, product, 0.0), axis=1, keepdims=True)
            delta = jnp.sum(jnp.where(eye, delta, 0.0), axis=0, keepdims=True)
            log_total = total_ref[0, 0, half : half + 1, rows]
            scores = contract(keys, q_half, 1, 1)
            probs = jnp.concatenate(
                [
                    jnp.where(allowed[:WINDOW], jnp.exp(scores[:WINDOW] - log_total), 0.0),
                    jnp.where(late_allowed, jnp.exp(scores[WINDOW:] - log_total), 0.0),
                ]
            )
            grad_probs = contract(values, g_half, 1, 1)
            grad_scores = (probs * (grad_probs - delta)).astype(jnp.bfloat16)
            gv_sum[window, :] += contract(probs.astype(jnp.bfloat16), g_half, 1, 0)
            gk_sum[window, :] += contract(grad_scores, q_half, 1, 0)
            gq_parts.append(contract(keys_t[half * HD : (half + 1) * HD], grad_scores, 1, 0))
        gq = jnp.transpose(jnp.concatenate(gq_parts)) * scale
        out_ref[0, pl.ds(first + block * TILE, TILE), :PAIR] = gq.astype(jnp.bfloat16)
    out_ref[0, :first, :PAIR] = jnp.zeros((first, PAIR), jnp.bfloat16)
    out_ref[0, :, PAIR : 2 * PAIR] = gk_sum[...].astype(jnp.bfloat16)
    out_ref[0, :, 2 * PAIR :] = gv_sum[...].astype(jnp.bfloat16)


def attention_backward(packed, mixed, grads, log_total, low_pos):
    groups, key_len, width = packed.shape
    block_len = mixed.shape[1]
    pairs = width // (3 * PAIR)
    pick = lambda seq, pair: (seq, 0, pair)
    row_spec = pl.BlockSpec((1, block_len, PAIR), pick)
    packed_spec = pl.BlockSpec((1, key_len, 3 * PAIR), pick)
    return pl.pallas_call(
        backward_kernel,
        grid=(groups, pairs),
        in_specs=[
            packed_spec, row_spec, row_spec,
            pl.BlockSpec((1, 1, 2, block_len), lambda seq, pair: (seq, pair, 0, 0)),
            pl.BlockSpec((1, 1, block_len), lambda seq, pair: (seq, 0, 0)),
        ],
        out_specs=packed_spec,
        out_shape=jax.ShapeDtypeStruct(packed.shape, jnp.bfloat16),
        scratch_shapes=[
            pltpu.VMEM((key_len, PAIR), jnp.float32),
            pltpu.VMEM((key_len, PAIR), jnp.float32),
        ],
        compiler_params=pltpu.CompilerParams(vmem_limit_bytes=40 << 20),
        cost_estimate=pl.CostEstimate(
            flops=40 * groups * pairs * block_len * (WINDOW + TILE) * HD,
            bytes_accessed=4 * groups * width * key_len,
            transcendentals=2 * groups * pairs * block_len * (WINDOW + TILE),
        ),
    )(packed, mixed, grads, log_total, low_pos[:, None, :])


norm_eps = 1e-05


def mate(value):
    return lax.ppermute(value, "core", [(0, 1), (1, 0)])


def other_tp(value):
    return lax.ppermute(value, "tp", [(0, 1), (1, 0)])


def onward(value):
    count = lax.axis_size("ctx")
    return lax.ppermute(value, "ctx", [(i, i + 1) for i in range(count - 1)])


def backward_step(value):
    count = lax.axis_size("ctx")
    return lax.ppermute(value, "ctx", [(i + 1, i) for i in range(count - 1)])


class Place:
    def __init__(self):
        self.chips = lax.axis_size("x")
        self.core = lax.axis_index("core")
        self.shard = lax.axis_index("x") * 2 + self.core
        self.tp = lax.axis_index("tp")
        self.ctx = lax.axis_index("ctx")
        self.home = self.core == self.tp


def tie(*values):
    return lax.optimization_barrier(values)


def ordered(own, other, position, axis=0):
    return jnp.where(
        position == 0,
        jnp.stack([own, other], axis=axis),
        jnp.stack([other, own], axis=axis),
    )


def join_kernel(core_ref, *refs):
    out_ref = refs[-1]
    own = pl.program_id(1) == core_ref[0]
    at = 0
    for blocks_ref, came_ref in zip(refs[0:-1:2], refs[1:-1:2]):
        width = came_ref.shape[2]

        @pl.when(own)
        def _(at=at, width=width, blocks_ref=blocks_ref):
            out_ref[:, at : at + width] = blocks_ref[0, 0]

        @pl.when(jnp.logical_not(own))
        def _(at=at, width=width, came_ref=came_ref):
            out_ref[:, at : at + width] = came_ref[0]

        at += width


class CoreSwap:
    def __init__(self, blocks, place, column=0, width=None):
        self.place, self.blocks, self.column = place, blocks, column
        width = blocks.shape[3] if width is None else width
        other = lax.dynamic_index_in_dim(blocks, 1 - place.core, 1, False)
        self.came = mate(other[..., column * width : (column + 1) * width])


def join(*swaps):
    chips, rows = swaps[0].came.shape[:2]
    in_specs, operands, total = [], [], 0
    for swap in swaps:
        width = swap.came.shape[2]
        in_specs += [
            pl.BlockSpec(
                (1, 1, rows, width),
                lambda chip, part, core, column=swap.column: (chip, core[0], 0, column),
            ),
            pl.BlockSpec((1, rows, width), lambda chip, part, core: (chip, 0, 0)),
        ]
        operands += [swap.blocks, swap.came]
        total += width
    return pl.pallas_call(
        join_kernel,
        grid_spec=pltpu.PrefetchScalarGridSpec(
            num_scalar_prefetch=1,
            grid=(chips, 2),
            in_specs=in_specs,
            out_specs=pl.BlockSpec((rows, total), lambda chip, part, core: (chip * 2 + part, 0)),
        ),
        out_shape=jax.ShapeDtypeStruct((chips * 2 * rows, total), jnp.bfloat16),
        compiler_params=pltpu.CompilerParams(vmem_limit_bytes=24 << 20),
        cost_estimate=pl.CostEstimate(
            flops=0, bytes_accessed=8 * chips * rows * total, transcendentals=0
        ),
    )(swaps[0].place.core.reshape(1).astype(jnp.int32), *operands)


def gather_blocks(piece, place):
    whole = lax.all_gather(piece, ("x", "tp"), axis=0, tiled=False)
    return whole.reshape((place.chips, 2) + piece.shape)


def scatter_swap(grads, place):
    return CoreSwap(grads.reshape(place.chips, 2, -1, grads.shape[1]), place)


def scatter_sum(blocks):
    return lax.psum_scatter(blocks, ("x", "tp"), scatter_dimension=0, tiled=True)


def dot_f32(left_side, right_side):
    return jnp.dot(left_side, right_side, preferred_element_type=jnp.float32)


def dot_first(left_side, right_side):
    return contract(left_side, right_side, 0, 0)


def dot_second(left_side, right_side):
    return contract(left_side, right_side, 1, 1)


def gather_small(value, place):
    if place.chips != 2:
        return lax.all_gather(value, ("x", "core"), axis=1, tiled=True)
    near = mate(value)
    pair = ordered(value, near, place.core, 1).reshape(value.shape[0], -1)
    far = lax.ppermute(pair, "x", [(0, 1), (1, 0)])
    return ordered(pair, far, lax.axis_index("x"), 1).reshape(value.shape[0], -1)


def norm_forward(hidden, norm_gain, norm_shift):
    row_mean = jnp.mean(hidden, axis=-1, keepdims=True)
    centred = hidden - row_mean
    variance = jnp.mean(centred * centred, axis=-1, keepdims=True)
    inv_std = lax.rsqrt(variance + norm_eps)
    norm_hat = centred * inv_std
    return ((norm_hat * norm_gain + norm_shift).astype(jnp.bfloat16), norm_hat, inv_std)


def norm_backward(grad_out, norm_hat, inv_std, norm_gain):
    scaled = grad_out * norm_gain
    mean_one = jnp.mean(scaled, axis=-1, keepdims=True)
    mean_two = jnp.mean(scaled * norm_hat, axis=-1, keepdims=True)
    grad_input = inv_std * (scaled - mean_one - norm_hat * mean_two)
    return (grad_input, jnp.sum(grad_out * norm_hat, axis=0), jnp.sum(grad_out, axis=0))


def wide(value):
    return value.astype(jnp.float32)


def narrow(value):
    return value.astype(jnp.bfloat16)


def pick_block(value, index, count):
    size = value.shape[0] // count
    return lax.dynamic_slice_in_dim(value, index * size, size, 0)


def small_total(value, place):
    if place.chips != 2 or lax.axis_size("ctx") != 4:
        return lax.psum(value, ("x", "core", "ctx", "tp"))
    value = value + mate(value)
    value = value + other_tp(value)
    value = value + lax.ppermute(value, "x", [(0, 1), (1, 0)])
    value = value + lax.ppermute(value, "ctx", [(0, 1), (3, 2)])
    value = value + lax.ppermute(value, "ctx", [(1, 2), (2, 1)])
    outer = (place.ctx == 0) | (place.ctx == 3)
    return jnp.where(outer, lax.ppermute(value, "ctx", [(1, 0), (2, 3)]), value)


def core_sum(own_part, mate_part):
    return own_part + wide(mate(narrow(mate_part)))


def gelu_slope(pre_act, grad_act):
    pullback = jax.vjp(lambda values: jax.nn.gelu(values, approximate=True), pre_act)[1]
    return pullback(grad_act)[0]


def pair_major(value):
    width = value.shape[-1]
    return jnp.concatenate(
        [value[kind, :, at : at + PAIR] for at in range(0, width, PAIR) for kind in range(3)],
        axis=-1,
    )


def pack_kernel(qkv_ref, proj_ref, out_ref):
    width = qkv_ref.shape[3]
    for pair in range(width // PAIR):
        for kind in range(3):
            at = (3 * pair + kind) * PAIR
            out_ref[:, at : at + PAIR] = qkv_ref[0, kind, :, pair * PAIR : (pair + 1) * PAIR]
    out_ref[:, 3 * width :] = jnp.transpose(proj_ref[0])


def attn_piece(layer, qkv_weight, proj_weight):
    rows, width = qkv_weight.shape[2:]
    return pl.pallas_call(
        pack_kernel,
        grid=(1,),
        in_specs=[
            pl.BlockSpec((1, 3, rows, width), lambda step: (layer, 0, 0, 0)),
            pl.BlockSpec((1, width, rows), lambda step: (layer, 0, 0)),
        ],
        out_specs=pl.BlockSpec((rows, 4 * width), lambda step: (0, 0)),
        out_shape=jax.ShapeDtypeStruct((rows, 4 * width), jnp.bfloat16),
        compiler_params=pltpu.CompilerParams(vmem_limit_bytes=24 << 20),
    )(qkv_weight, proj_weight)


def unpack_kernel(first_ref, second_ref, out_ref):
    kind = pl.program_id(0)
    width = out_ref.shape[3]
    for pair in range(width // PAIR):
        at = pl.multiple_of((3 * pair + kind) * PAIR, PAIR)
        for layer, ref in enumerate((first_ref, second_ref)):
            out_ref[layer, 0, :, pair * PAIR : (pair + 1) * PAIR] = ref[
                :, pl.ds(at, PAIR)
            ].astype(jnp.float32)


def unpack_heads(first, second):
    rows, width = first.shape
    width = width // 4
    block = pl.BlockSpec((rows, 4 * width), lambda kind: (0, 0))
    return pl.pallas_call(
        unpack_kernel,
        grid=(3,),
        in_specs=[block, block],
        out_specs=pl.BlockSpec((2, 1, rows, width), lambda kind: (0, kind, 0, 0)),
        out_shape=jax.ShapeDtypeStruct((2, 3, rows, width), jnp.float32),
        compiler_params=pltpu.CompilerParams(vmem_limit_bytes=24 << 20),
    )(first, second)


def per_device(
    tokens,
    cotangent,
    doc_lengths,
    norm_gains,
    norm_biases,
    qkv_weight,
    qv_bias,
    proj_weight,
    fc_weight,
    fc_bias,
    out_weight,
):
    place = Place()
    block_len, model_width = tokens.shape[1:]
    shard_rows = qkv_weight.shape[2]
    half_width = qkv_weight.shape[3]
    layer_count = qkv_weight.shape[0]
    reach = WINDOW // block_len
    key_len = (reach + 1) * block_len
    last = reach * block_len

    def my_seq(value):
        return lax.dynamic_index_in_dim(value, place.tp, 0, False)

    def both_seqs(own, other):
        return ordered(own, other, place.tp)

    own_tokens = my_seq(tokens)
    grad_hidden = wide(my_seq(cotangent))
    bias_parts = jnp.sum(grad_hidden.reshape(16, -1, model_width), axis=1)
    bias_parts = lax.psum(bias_parts, ("x", "core", "ctx", "tp"))
    attn_blocks = gather_blocks(attn_piece(0, qkv_weight, proj_weight), place)
    halo = [onward(own_tokens)]
    for _ in range(reach - 1):
        halo.insert(0, onward(halo[0]))
    vectors = jnp.concatenate([norm_gains, norm_biases], axis=1)
    vectors = gather_small(vectors.reshape(-1, vectors.shape[2]), place)
    vectors = wide(vectors).reshape(layer_count, 6, model_width)
    biases = jnp.concatenate([qv_bias.reshape(layer_count, -1), fc_bias], axis=1)
    biases = wide(jnp.where(place.home, biases, other_tp(biases)))
    lengths = my_seq(doc_lengths)
    lengths = jnp.stack([lengths, mate(lengths)])
    mlp_pieces = [
        jnp.concatenate([fc_weight[layer], jnp.transpose(out_weight[layer])], axis=1)
        for layer in range(layer_count)
    ]
    attn_later = attn_piece(1, qkv_weight, proj_weight)
    halo[-1], mlp_pieces, attn_later = tie(halo[-1], mlp_pieces, attn_later)
    mlp_blocks = gather_blocks(mlp_pieces[0], place)
    fc_width = fc_weight.shape[2]

    doc_ends = jnp.cumsum(lengths, axis=1)
    first_pos = place.ctx * block_len
    query_pos = first_pos + jnp.arange(block_len, dtype=jnp.int32)
    started = doc_ends[:, None, :] <= query_pos[None, :, None]
    doc_start = jnp.max(jnp.where(started, doc_ends[:, None, :], 0), axis=-1)
    low_pos = jnp.maximum(doc_start, query_pos[None, :] - (WINDOW - 1))
    low_pos = (low_pos - first_pos + last).astype(jnp.int32)

    hidden = wide(own_tokens)
    stash = []
    weights = []
    for layer in range(layer_count):
        gains, shifts = vectors[layer, :2], vectors[layer, 2:]
        bias_q, bias_v = biases[layer, :half_width], biases[layer, half_width : 2 * half_width]
        bias_qkv = pair_major(jnp.stack([bias_q, jnp.zeros_like(bias_q), bias_v])[:, None])
        bias_fc = biases[layer, 2 * half_width :]
        attn_in, hat_attn, inv_attn = norm_forward(hidden, gains[0], shifts[0])
        own_near = [attn_in]
        mate_near = [mate(attn_in)]
        step_value = attn_in
        for index in range(reach):
            if layer == 0:
                part = norm_forward(wide(halo[reach - 1 - index]), gains[0], shifts[0])[0]
            else:
                step_value = part = onward(step_value)
                if index == 0:
                    step_value, piece = tie(step_value, mlp_pieces[layer])
                    mlp_blocks = gather_blocks(piece, place)
                    part = step_value
            own_near.insert(0, part)
            mate_near.insert(0, mate(part))
        near = jnp.concatenate(own_near + mate_near)
        if layer == 0:
            near, bias_parts = tie(near, bias_parts)
        attn_swap = CoreSwap(attn_blocks, place)
        w_attn = join(attn_swap)
        w_qkv, w_proj_t = w_attn[:, : 3 * half_width], w_attn[:, 3 * half_width :]
        packed = narrow(dot_f32(near, w_qkv) + bias_qkv).reshape(2, key_len, -1)
        mixed, log_total = attention_forward(packed, low_pos)
        if layer + 1 < layer_count:
            mixed, attn_later = tie(mixed, attn_later)
            attn_blocks = gather_blocks(attn_later, place)
        mate_part = dot_second(mixed[1], w_proj_t)
        own_part = dot_second(mixed[0], w_proj_t)
        middle = hidden + core_sum(own_part, mate_part) + shifts[1]
        mlp_own, hat_mlp, inv_mlp = norm_forward(middle, gains[1], shifts[2])
        mlp_in = jnp.concatenate([mlp_own, mate(mlp_own)])
        mlp_in, mlp_blocks = tie(mlp_in, mlp_blocks)
        w_fc = join(CoreSwap(mlp_blocks, place, 0, fc_width))
        out_swap = CoreSwap(mlp_blocks, place, 1, fc_width)
        pre_act = dot_f32(mlp_in, w_fc) + bias_fc
        activated = narrow(jax.nn.gelu(pre_act, approximate=True))
        w_out_t = join(out_swap)
        mate_part = dot_second(activated[block_len:], w_out_t)
        own_part = dot_second(activated[:block_len], w_out_t)
        hidden = middle + core_sum(own_part, mate_part) + shifts[3]
        weights.append((w_qkv, w_proj_t, w_fc, w_out_t))
        stash.append(
            (near, hat_attn, inv_attn, packed, mixed, log_total, hat_mlp, inv_mlp, mlp_in,
             pre_act, activated)
        )

    own_output = narrow(hidden)
    output = both_seqs(own_output, other_tp(own_output))

    last_sum = None
    sums = {}
    waiting, latest, first_sum = [], [], []
    small_parts = [None] * layer_count

    def advance(value, name):
        nonlocal last_sum
        share = waiting.pop(0)
        assert share[0] == name
        value, share, last_sum = tie(value, share[1], last_sum)
        if latest:
            sums[latest[0]] = last_sum
        else:
            first_sum.append(last_sum)
        latest[:] = [name]
        last_sum = lax.psum(share, "ctx")
        sums[name] = last_sum
        return value

    for layer in reversed(range(layer_count)):
        near, hat_attn, inv_attn, packed, mixed, log_total = stash[layer][:6]
        hat_mlp, inv_mlp, mlp_in, pre_act, activated = stash[layer][6:]
        gains = vectors[layer, :2]
        w_qkv, w_proj_t, w_fc, w_out_t = weights[layer]
        final = layer == 0
        grad_out_bias = jnp.sum(grad_hidden, axis=0)
        if not final:
            last_sum = bias_parts
        grad_low = narrow(grad_hidden)
        grad_low = jnp.concatenate([grad_low, mate(grad_low)])
        out_swap = scatter_swap(narrow(dot_first(grad_low, activated)), place)
        grad_pre = narrow(gelu_slope(pre_act, dot_f32(grad_low, w_out_t)))
        grad_pre, out_swap.came = tie(grad_pre, out_swap.came)
        if final:
            grad_pre = advance(grad_pre, "attn1")
        waiting.append(("out%d" % layer, scatter_sum(join(out_swap))))
        grad_fc_bias = jnp.sum(wide(grad_pre), axis=0)
        mate_part = dot_second(grad_pre[block_len:], w_fc)
        own_part = dot_second(grad_pre[:block_len], w_fc)
        grad_norm_in = core_sum(own_part, mate_part)
        fc_swap = scatter_swap(narrow(dot_first(mlp_in, grad_pre)), place)
        grad_from_mlp, grad_gain_mlp, grad_shift_mlp = norm_backward(
            grad_norm_in, hat_mlp, inv_mlp, gains[1]
        )
        grad_middle = grad_hidden + grad_from_mlp
        grad_proj_bias = jnp.sum(grad_middle, axis=0)
        grad_low = narrow(grad_middle)
        grad_low, fc_swap.came = tie(grad_low, fc_swap.came)
        waiting.append(("fc%d" % layer, scatter_sum(join(fc_swap))))
        grad_low = jnp.concatenate([grad_low, mate(grad_low)])
        grad_mixed = narrow(dot_f32(grad_low, w_proj_t)).reshape(mixed.shape)
        proj_swap = scatter_swap(
            narrow(dot_first(grad_low, mixed.reshape(2 * block_len, half_width))), place
        )
        grad_packed = attention_backward(packed, mixed, grad_mixed, log_total, low_pos)
        grad_packed = advance(grad_packed, "out%d" % layer)
        mate_part = dot_second(grad_packed[1], w_qkv)
        own_part = dot_second(grad_packed[0], w_qkv)
        grad_near = core_sum(own_part, mate_part)
        far_total, grad_attn_in = grad_near[:last], grad_near[last:]
        rows = grad_packed.reshape(2 * key_len, -1)
        grad_near, rows = tie(grad_near, rows)
        far_total, grad_attn_in = grad_near[:last], grad_near[last:]
        carried = backward_step(narrow(far_total[:block_len]))
        attn_swap = scatter_swap(narrow(dot_first(near, rows)), place)
        for step in range(1, reach + 1):
            if step == 1:
                carried, attn_swap.came = tie(carried, attn_swap.came)
                carried = advance(carried, "fc%d" % layer)
                waiting.append(("attn%d" % layer, scatter_sum(join(attn_swap, proj_swap))))
            arrived = wide(carried)
            if step < reach:
                section = far_total[step * block_len : (step + 1) * block_len]
                carried = backward_step(narrow(arrived + section))
            else:
                grad_attn_in = grad_attn_in + arrived
        grad_from_attn, grad_gain_attn, grad_shift_attn = norm_backward(
            grad_attn_in, hat_attn, inv_attn, gains[0]
        )
        grad_hidden = grad_middle + grad_from_attn
        grad_bias = jnp.sum(wide(rows), axis=0).reshape(-1, 3, PAIR)
        halves = jnp.concatenate(
            [grad_bias[:, 0].reshape(-1), grad_bias[:, 2].reshape(-1), grad_fc_bias]
        )
        empty = jnp.zeros_like(halves)
        small_parts[layer] = jnp.concatenate(
            [
                grad_gain_attn, grad_gain_mlp,
                grad_shift_attn, grad_proj_bias, grad_shift_mlp, grad_out_bias,
                jnp.where(place.core == 0, halves, empty),
                jnp.where(place.core == 1, halves, empty),
            ]
        )

    small = small_total(jnp.stack(small_parts), place)
    far_grad = wide(other_tp(narrow(grad_hidden)))
    token_grad = both_seqs(grad_hidden, far_grad)
    advance((), "attn0")
    split = 6 * model_width
    norms = small[:, :split].reshape(layer_count, 6, model_width)
    norms = norms.at[1, 5].set(jnp.sum(first_sum[0], axis=0))
    norms = lax.dynamic_slice_in_dim(norms, place.shard * shard_rows, shard_rows, 2)
    halves = small[:, split:].reshape(layer_count, 2, -1)
    halves = lax.dynamic_index_in_dim(halves, place.tp, 1, False)
    packed_width = 3 * half_width
    attn = [sums["attn%d" % layer] for layer in range(layer_count)]
    return (
        output,
        token_grad,
        norms[:, :2],
        norms[:, 2:],
        unpack_heads(*attn),
        halves[:, : 2 * half_width].reshape(layer_count, 2, half_width),
        jnp.stack([jnp.transpose(wide(v[:, packed_width:])) for v in attn]),
        jnp.stack([wide(sums["fc%d" % layer]) for layer in range(layer_count)]),
        halves[:, 2 * half_width :],
        jnp.stack([jnp.transpose(wide(sums["out%d" % layer])) for layer in range(layer_count)]),
    )


def solution(mesh):
    devices = mesh.devices
    devices = devices.reshape((devices.shape[0] // 2, 2) + devices.shape[1:])
    mesh = jax.sharding.Mesh(devices, ("x", "core", "ctx", "tp"))
    placed = (
        P(("x", "core"), "ctx", None),
        P(("x", "core"), "ctx", None),
        P(("x", "core"), None),
        P(None, None, ("x", "core")),
        P(None, None, ("x", "core")),
        P(None, None, ("x", "core"), "tp"),
        P(None, None, "tp"),
        P(None, "tp", ("x", "core")),
        P(None, ("x", "core"), "tp"),
        P(None, "tp"),
        P(None, "tp", ("x", "core")),
    )
    return jax.shard_map(
        per_device,
        mesh=mesh,
        in_specs=placed,
        out_specs=(
            P(("x", "core"), "ctx", None),
            P(("x", "core"), "ctx", None),
            P(None, None, ("x", "core")),
            P(None, None, ("x", "core")),
            P(None, None, ("x", "core"), "tp"),
            P(None, None, "tp"),
            P(None, "tp", ("x", "core")),
            P(None, ("x", "core"), "tp"),
            P(None, "tp"),
            P(None, "tp", ("x", "core")),
        ),
        check_vma=False,
    )
```

```python
import jax
import jax.numpy as jnp
from jax import lax
from jax.experimental import pallas as pl
from jax.experimental.pallas import tpu as pltpu
from jax.sharding import PartitionSpec as P

HD = 64
WINDOW = 1024
TILE = 256
masked_score = -1e30


def contract(left_side, right_side, left_dim, right_dim):
    return lax.dot_general(
        left_side, right_side, (((left_dim,), (right_dim,)), ((), ())),
        preferred_element_type=jnp.float32,
    )


def half_mask(shape, half):
    lane = lax.broadcasted_iota(jnp.int32, shape, 1)
    return (lane < HD) if half == 0 else (lane >= HD)


PAIR = 2 * HD


def forward_kernel(qkv_ref, low_ref, mixed_ref, total_ref):
    block_len = mixed_ref.shape[1]
    first = qkv_ref.shape[1] - block_len
    span = WINDOW + TILE
    eye = lax.broadcasted_iota(jnp.int32, (TILE, TILE), 0) == lax.broadcasted_iota(
        jnp.int32, (TILE, TILE), 1
    )
    for block in range(block_len // TILE):
        rows = pl.ds(block * TILE, TILE)
        window = pl.ds(block * TILE, span)
        queries = qkv_ref[0, pl.ds(first + block * TILE, TILE), :PAIR]
        queries = queries * jnp.asarray(HD ** (-0.5), jnp.bfloat16)
        keys = qkv_ref[0, window, PAIR : 2 * PAIR]
        values = qkv_ref[0, window, 2 * PAIR :]
        low_pos = low_ref[0, rows, :] - block * TILE
        key_pos = lax.broadcasted_iota(jnp.int32, (TILE, span), 1)
        query_pos = lax.broadcasted_iota(jnp.int32, (TILE, TILE), 0) + WINDOW
        allowed = key_pos >= low_pos
        causal = key_pos[:, WINDOW:] <= query_pos
        mixed = jnp.zeros((TILE, 2 * HD), jnp.float32)
        for half in range(2):
            scores = contract(
                jnp.where(half_mask(queries.shape, half), queries, 0), keys, 1, 1
            )
            early = jnp.where(allowed[:, :WINDOW], scores[:, :WINDOW], masked_score)
            late = jnp.where(allowed[:, WINDOW:] & causal, scores[:, WINDOW:], masked_score)
            top_score = jnp.maximum(
                jnp.max(early, axis=1, keepdims=True), jnp.max(late, axis=1, keepdims=True)
            )
            early = jnp.exp(early - top_score)
            late = jnp.exp(late - top_score)
            row_total = jnp.sum(early, axis=1, keepdims=True) + jnp.sum(
                late, axis=1, keepdims=True
            )
            part = contract(early.astype(jnp.bfloat16), values[:WINDOW], 1, 0) + contract(
                late.astype(jnp.bfloat16), values[WINDOW:], 1, 0
            )
            part = part * (1.0 / row_total)
            mixed = jnp.where(half_mask(mixed.shape, half), part, mixed)
            log_total = top_score + jnp.log(row_total)
            total_ref[0, 0, half : half + 1, rows] = jnp.sum(
                jnp.where(eye, log_total, 0.0), axis=0, keepdims=True
            )
        mixed_ref[0, rows, :] = mixed.astype(jnp.bfloat16)


def attention_forward(packed, low_pos):
    groups, key_len, width = packed.shape
    block_len = low_pos.shape[1]
    pairs = width // (3 * PAIR)
    pick = lambda seq, pair: (seq, 0, pair)
    return pl.pallas_call(
        forward_kernel,
        grid=(groups, pairs),
        in_specs=[
            pl.BlockSpec((1, key_len, 3 * PAIR), pick),
            pl.BlockSpec((1, block_len, 1), lambda seq, pair: (seq, 0, 0)),
        ],
        out_specs=[
            pl.BlockSpec((1, block_len, PAIR), pick),
            pl.BlockSpec((1, 1, 2, block_len), lambda seq, pair: (seq, pair, 0, 0)),
        ],
        out_shape=[
            jax.ShapeDtypeStruct((groups, block_len, pairs * PAIR), jnp.bfloat16),
            jax.ShapeDtypeStruct((groups, pairs, 2, block_len), jnp.float32),
        ],
        compiler_params=pltpu.CompilerParams(vmem_limit_bytes=56 << 20),
        cost_estimate=pl.CostEstimate(
            flops=16 * groups * pairs * block_len * (WINDOW + TILE) * HD,
            bytes_accessed=2 * groups * width * key_len,
            transcendentals=2 * groups * pairs * block_len * (WINDOW + TILE),
        ),
    )(packed, low_pos[:, :, None])


def backward_kernel(qkv_ref, mixed_ref, grad_ref, total_ref, low_ref, out_ref, gk_sum, gv_sum):
    block_len = mixed_ref.shape[1]
    first = qkv_ref.shape[1] - block_len
    span = WINDOW + TILE
    scale = HD ** (-0.5)
    gk_sum[...] = jnp.zeros_like(gk_sum)
    gv_sum[...] = jnp.zeros_like(gv_sum)
    eye = lax.broadcasted_iota(jnp.int32, (TILE, TILE), 0) == lax.broadcasted_iota(
        jnp.int32, (TILE, TILE), 1
    )
    for block in range(block_len // TILE):
        rows = pl.ds(block * TILE, TILE)
        window = pl.ds(block * TILE, span)
        queries = qkv_ref[0, pl.ds(first + block * TILE, TILE), :PAIR]
        queries = queries * jnp.asarray(scale, jnp.bfloat16)
        keys = qkv_ref[0, window, PAIR : 2 * PAIR]
        values = qkv_ref[0, window, 2 * PAIR :]
        grads = grad_ref[0, rows, :]
        product = grads.astype(jnp.float32) * mixed_ref[0, rows, :].astype(jnp.float32)
        low_pos = low_ref[0, :, rows] - block * TILE
        key_pos = lax.broadcasted_iota(jnp.int32, (span, TILE), 0)
        query_pos = lax.broadcasted_iota(jnp.int32, (TILE, TILE), 1) + WINDOW
        allowed = key_pos >= low_pos
        late_allowed = allowed[WINDOW:] & (key_pos[WINDOW:] <= query_pos)
        keys_t = jnp.transpose(keys)
        gq_parts = []
        for half in range(2):
            mask = half_mask(queries.shape, half)
            q_half = jnp.where(mask, queries, 0)
            g_half = jnp.where(mask, grads, 0)
            delta = jnp.sum(jnp.where(mask, product, 0.0), axis=1, keepdims=True)
            delta = jnp.sum(jnp.where(eye, delta, 0.0), axis=0, keepdims=True)
            log_total = total_ref[0, 0, half : half + 1, rows]
            scores = contract(keys, q_half, 1, 1)
            probs = jnp.concatenate(
                [
                    jnp.where(allowed[:WINDOW], jnp.exp(scores[:WINDOW] - log_total), 0.0),
                    jnp.where(late_allowed, jnp.exp(scores[WINDOW:] - log_total), 0.0),
                ]
            )
            grad_probs = contract(values, g_half, 1, 1)
            grad_scores = (probs * (grad_probs - delta)).astype(jnp.bfloat16)
            gv_sum[window, :] += contract(probs.astype(jnp.bfloat16), g_half, 1, 0)
            gk_sum[window, :] += contract(grad_scores, q_half, 1, 0)
            gq_parts.append(contract(keys_t[half * HD : (half + 1) * HD], grad_scores, 1, 0))
        gq = jnp.transpose(jnp.concatenate(gq_parts)) * scale
        out_ref[0, pl.ds(first + block * TILE, TILE), :PAIR] = gq.astype(jnp.bfloat16)
    out_ref[0, :first, :PAIR] = jnp.zeros((first, PAIR), jnp.bfloat16)
    out_ref[0, :, PAIR : 2 * PAIR] = gk_sum[...].astype(jnp.bfloat16)
    out_ref[0, :, 2 * PAIR :] = gv_sum[...].astype(jnp.bfloat16)


def attention_backward(packed, mixed, grads, log_total, low_pos):
    groups, key_len, width = packed.shape
    block_len = mixed.shape[1]
    pairs = width // (3 * PAIR)
    pick = lambda seq, pair: (seq, 0, pair)
    row_spec = pl.BlockSpec((1, block_len, PAIR), pick)
    packed_spec = pl.BlockSpec((1, key_len, 3 * PAIR), pick)
    return pl.pallas_call(
        backward_kernel,
        grid=(groups, pairs),
        in_specs=[
            packed_spec, row_spec, row_spec,
            pl.BlockSpec((1, 1, 2, block_len), lambda seq, pair: (seq, pair, 0, 0)),
            pl.BlockSpec((1, 1, block_len), lambda seq, pair: (seq, 0, 0)),
        ],
        out_specs=packed_spec,
        out_shape=jax.ShapeDtypeStruct(packed.shape, jnp.bfloat16),
        scratch_shapes=[
            pltpu.VMEM((key_len, PAIR), jnp.float32),
            pltpu.VMEM((key_len, PAIR), jnp.float32),
        ],
        compiler_params=pltpu.CompilerParams(vmem_limit_bytes=56 << 20),
        cost_estimate=pl.CostEstimate(
            flops=40 * groups * pairs * block_len * (WINDOW + TILE) * HD,
            bytes_accessed=4 * groups * width * key_len,
            transcendentals=2 * groups * pairs * block_len * (WINDOW + TILE),
        ),
    )(packed, mixed, grads, log_total, low_pos[:, None, :])


norm_eps = 1e-05


def mate(value):
    return lax.ppermute(value, "core", [(0, 1), (1, 0)])


def other_tp(value):
    return lax.ppermute(value, "tp", [(0, 1), (1, 0)])


def onward(value):
    count = lax.axis_size("ctx")
    return lax.ppermute(value, "ctx", [(i, i + 1) for i in range(count - 1)])


def backward_step(value):
    count = lax.axis_size("ctx")
    return lax.ppermute(value, "ctx", [(i + 1, i) for i in range(count - 1)])


class Place:
    def __init__(self):
        self.chips = lax.axis_size("x")
        self.core = lax.axis_index("core")
        self.shard = lax.axis_index("x") * 2 + self.core
        self.tp = lax.axis_index("tp")
        self.ctx = lax.axis_index("ctx")
        self.home = self.core == self.tp


def tie(*values):
    return lax.optimization_barrier(values)


def ordered(own, other, position, axis=0):
    return jnp.where(
        position == 0,
        jnp.stack([own, other], axis=axis),
        jnp.stack([other, own], axis=axis),
    )


def join_kernel(core_ref, *refs):
    out_ref = refs[-1]
    own = pl.program_id(1) == core_ref[0]
    at = 0
    for blocks_ref, came_ref in zip(refs[0:-1:2], refs[1:-1:2]):
        width = came_ref.shape[2]

        @pl.when(own)
        def _(at=at, width=width, blocks_ref=blocks_ref):
            out_ref[:, at : at + width] = blocks_ref[0, 0]

        @pl.when(jnp.logical_not(own))
        def _(at=at, width=width, came_ref=came_ref):
            out_ref[:, at : at + width] = came_ref[0]

        at += width


class CoreSwap:
    def __init__(self, blocks, place, column=0, width=None):
        self.place, self.blocks, self.column = place, blocks, column
        width = blocks.shape[3] if width is None else width
        other = lax.dynamic_index_in_dim(blocks, 1 - place.core, 1, False)
        self.came = mate(other[..., column * width : (column + 1) * width])


def join(*swaps):
    chips, rows = swaps[0].came.shape[:2]
    in_specs, operands, total = [], [], 0
    for swap in swaps:
        width = swap.came.shape[2]
        in_specs += [
            pl.BlockSpec(
                (1, 1, rows, width),
                lambda chip, part, core, column=swap.column: (chip, core[0], 0, column),
            ),
            pl.BlockSpec((1, rows, width), lambda chip, part, core: (chip, 0, 0)),
        ]
        operands += [swap.blocks, swap.came]
        total += width
    return pl.pallas_call(
        join_kernel,
        grid_spec=pltpu.PrefetchScalarGridSpec(
            num_scalar_prefetch=1,
            grid=(chips, 2),
            in_specs=in_specs,
            out_specs=pl.BlockSpec((rows, total), lambda chip, part, core: (chip * 2 + part, 0)),
        ),
        out_shape=jax.ShapeDtypeStruct((chips * 2 * rows, total), jnp.bfloat16),
        compiler_params=pltpu.CompilerParams(vmem_limit_bytes=56 << 20),
        cost_estimate=pl.CostEstimate(
            flops=0, bytes_accessed=8 * chips * rows * total, transcendentals=0
        ),
    )(swaps[0].place.core.reshape(1).astype(jnp.int32), *operands)


def gather_blocks(piece, place):
    whole = lax.all_gather(piece, ("x", "tp"), axis=0, tiled=False)
    return whole.reshape((place.chips, 2) + piece.shape)


def scatter_swap(grads, place):
    return CoreSwap(grads.reshape(place.chips, 2, -1, grads.shape[1]), place)


def scatter_sum(blocks):
    return lax.psum_scatter(blocks, ("x", "tp"), scatter_dimension=0, tiled=True)


def dot_f32(left_side, right_side):
    return jnp.dot(left_side, right_side, preferred_element_type=jnp.float32)


def dot_first(left_side, right_side):
    return contract(left_side, right_side, 0, 0)


def dot_second(left_side, right_side):
    return contract(left_side, right_side, 1, 1)


def gather_small(value, place):
    if place.chips != 2:
        return lax.all_gather(value, ("x", "core"), axis=1, tiled=True)
    near = mate(value)
    pair = ordered(value, near, place.core, 1).reshape(value.shape[0], -1)
    far = lax.ppermute(pair, "x", [(0, 1), (1, 0)])
    return ordered(pair, far, lax.axis_index("x"), 1).reshape(value.shape[0], -1)


def norm_forward(hidden, norm_gain, norm_shift):
    row_mean = jnp.mean(hidden, axis=-1, keepdims=True)
    centred = hidden - row_mean
    variance = jnp.mean(centred * centred, axis=-1, keepdims=True)
    inv_std = lax.rsqrt(variance + norm_eps)
    norm_hat = centred * inv_std
    return ((norm_hat * norm_gain + norm_shift).astype(jnp.bfloat16), norm_hat, inv_std)


def norm_backward(grad_out, norm_hat, inv_std, norm_gain):
    scaled = grad_out * norm_gain
    mean_one = jnp.mean(scaled, axis=-1, keepdims=True)
    mean_two = jnp.mean(scaled * norm_hat, axis=-1, keepdims=True)
    grad_input = inv_std * (scaled - mean_one - norm_hat * mean_two)
    return (grad_input, jnp.sum(grad_out * norm_hat, axis=0), jnp.sum(grad_out, axis=0))


def wide(value):
    return value.astype(jnp.float32)


def narrow(value):
    return value.astype(jnp.bfloat16)


def pick_block(value, index, count):
    size = value.shape[0] // count
    return lax.dynamic_slice_in_dim(value, index * size, size, 0)


def small_total(value, place):
    if place.chips != 2 or lax.axis_size("ctx") != 4:
        return lax.psum(value, ("x", "core", "ctx", "tp"))
    value = value + mate(value)
    value = value + other_tp(value)
    value = value + lax.ppermute(value, "x", [(0, 1), (1, 0)])
    value = value + lax.ppermute(value, "ctx", [(0, 1), (3, 2)])
    value = value + lax.ppermute(value, "ctx", [(1, 2), (2, 1)])
    outer = (place.ctx == 0) | (place.ctx == 3)
    return jnp.where(outer, lax.ppermute(value, "ctx", [(1, 0), (2, 3)]), value)


def core_sum(own_part, mate_part):
    return own_part + wide(mate(narrow(mate_part)))


def gelu_slope(pre_act, grad_act):
    pullback = jax.vjp(lambda values: jax.nn.gelu(values, approximate=True), pre_act)[1]
    return pullback(grad_act)[0]


def pair_major(value):
    width = value.shape[-1]
    return jnp.concatenate(
        [value[kind, :, at : at + PAIR] for at in range(0, width, PAIR) for kind in range(3)],
        axis=-1,
    )


def pack_kernel(qkv_ref, proj_ref, out_ref):
    width = qkv_ref.shape[3]
    for pair in range(width // PAIR):
        for kind in range(3):
            at = (3 * pair + kind) * PAIR
            out_ref[:, at : at + PAIR] = qkv_ref[0, kind, :, pair * PAIR : (pair + 1) * PAIR]
    out_ref[:, 3 * width :] = jnp.transpose(proj_ref[0])


def attn_piece(layer, qkv_weight, proj_weight):
    rows, width = qkv_weight.shape[2:]
    return pl.pallas_call(
        pack_kernel,
        grid=(1,),
        in_specs=[
            pl.BlockSpec((1, 3, rows, width), lambda step: (layer, 0, 0, 0)),
            pl.BlockSpec((1, width, rows), lambda step: (layer, 0, 0)),
        ],
        out_specs=pl.BlockSpec((rows, 4 * width), lambda step: (0, 0)),
        out_shape=jax.ShapeDtypeStruct((rows, 4 * width), jnp.bfloat16),
        compiler_params=pltpu.CompilerParams(vmem_limit_bytes=56 << 20),
    )(qkv_weight, proj_weight)


def unpack_kernel(first_ref, second_ref, out_ref):
    kind = pl.program_id(0)
    width = out_ref.shape[3]
    for pair in range(width // PAIR):
        at = pl.multiple_of((3 * pair + kind) * PAIR, PAIR)
        for layer, ref in enumerate((first_ref, second_ref)):
            out_ref[layer, 0, :, pair * PAIR : (pair + 1) * PAIR] = ref[
                :, pl.ds(at, PAIR)
            ].astype(jnp.float32)


def unpack_heads(first, second):
    rows, width = first.shape
    width = width // 3
    block = pl.BlockSpec((rows, 3 * width), lambda kind: (0, 0))
    return pl.pallas_call(
        unpack_kernel,
        grid=(3,),
        in_specs=[block, block],
        out_specs=pl.BlockSpec((2, 1, rows, width), lambda kind: (0, kind, 0, 0)),
        out_shape=jax.ShapeDtypeStruct((2, 3, rows, width), jnp.float32),
        compiler_params=pltpu.CompilerParams(vmem_limit_bytes=56 << 20),
    )(first, second)


def per_device(
    tokens,
    cotangent,
    doc_lengths,
    norm_gains,
    norm_biases,
    qkv_weight,
    qv_bias,
    proj_weight,
    fc_weight,
    fc_bias,
    out_weight,
):
    place = Place()
    block_len, model_width = tokens.shape[1:]
    shard_rows = qkv_weight.shape[2]
    half_width = qkv_weight.shape[3]
    layer_count = qkv_weight.shape[0]
    reach = WINDOW // block_len
    key_len = (reach + 1) * block_len
    last = reach * block_len

    def my_seq(value):
        return lax.dynamic_index_in_dim(value, place.tp, 0, False)

    def both_seqs(own, other):
        return ordered(own, other, place.tp)

    own_tokens = my_seq(tokens)
    grad_hidden = wide(my_seq(cotangent))
    bias_parts = jnp.sum(grad_hidden.reshape(16, -1, model_width), axis=1)
    bias_parts = lax.psum(bias_parts, "ctx")
    attn_blocks = gather_blocks(attn_piece(0, qkv_weight, proj_weight), place)
    halo = [onward(own_tokens)]
    for _ in range(reach - 1):
        halo.insert(0, onward(halo[0]))
    vectors = jnp.concatenate([norm_gains, norm_biases], axis=1)
    vectors = gather_small(vectors.reshape(-1, vectors.shape[2]), place)
    vectors = wide(vectors).reshape(layer_count, 6, model_width)
    biases = jnp.concatenate([qv_bias.reshape(layer_count, -1), fc_bias], axis=1)
    biases = wide(jnp.where(place.home, biases, other_tp(biases)))
    lengths = my_seq(doc_lengths)
    lengths = jnp.stack([lengths, mate(lengths)])
    mlp_pieces = [
        jnp.concatenate([fc_weight[layer], jnp.transpose(out_weight[layer])], axis=1)
        for layer in range(layer_count)
    ]
    attn_later = attn_piece(1, qkv_weight, proj_weight)
    halo[-1], mlp_pieces, attn_later = tie(halo[-1], mlp_pieces, attn_later)
    mlp_blocks = gather_blocks(mlp_pieces[0], place)
    fc_width = fc_weight.shape[2]

    doc_ends = jnp.cumsum(lengths, axis=1)
    first_pos = place.ctx * block_len
    query_pos = first_pos + jnp.arange(block_len, dtype=jnp.int32)
    started = doc_ends[:, None, :] <= query_pos[None, :, None]
    doc_start = jnp.max(jnp.where(started, doc_ends[:, None, :], 0), axis=-1)
    low_pos = jnp.maximum(doc_start, query_pos[None, :] - (WINDOW - 1))
    low_pos = (low_pos - first_pos + last).astype(jnp.int32)

    hidden = wide(own_tokens)
    stash = []
    weights = []
    for layer in range(layer_count):
        gains, shifts = vectors[layer, :2], vectors[layer, 2:]
        bias_q, bias_v = biases[layer, :half_width], biases[layer, half_width : 2 * half_width]
        bias_qkv = pair_major(jnp.stack([bias_q, jnp.zeros_like(bias_q), bias_v])[:, None])
        bias_fc = biases[layer, 2 * half_width :]
        attn_in, hat_attn, inv_attn = norm_forward(hidden, gains[0], shifts[0])
        own_near = [attn_in]
        mate_near = [mate(attn_in)]
        step_value = attn_in
        for index in range(reach):
            if layer == 0:
                part = norm_forward(wide(halo[reach - 1 - index]), gains[0], shifts[0])[0]
            else:
                step_value = part = onward(step_value)
                if index == 0:
                    step_value, piece = tie(step_value, mlp_pieces[layer])
                    mlp_blocks = gather_blocks(piece, place)
                    part = step_value
            own_near.insert(0, part)
            mate_near.insert(0, mate(part))
        near = jnp.concatenate(own_near + mate_near)
        if layer == 0:
            near, bias_parts = tie(near, bias_parts)
        attn_swap = CoreSwap(attn_blocks, place)
        w_attn = join(attn_swap)
        w_qkv, w_proj_t = w_attn[:, : 3 * half_width], w_attn[:, 3 * half_width :]
        packed = narrow(dot_f32(near, w_qkv) + bias_qkv).reshape(2, key_len, -1)
        mixed, log_total = attention_forward(packed, low_pos)
        if layer + 1 < layer_count:
            mixed, attn_later = tie(mixed, attn_later)
            attn_blocks = gather_blocks(attn_later, place)
        mate_part = dot_second(mixed[1], w_proj_t)
        own_part = dot_second(mixed[0], w_proj_t)
        middle = hidden + core_sum(own_part, mate_part) + shifts[1]
        mlp_own, hat_mlp, inv_mlp = norm_forward(middle, gains[1], shifts[2])
        mlp_in = jnp.concatenate([mlp_own, mate(mlp_own)])
        mlp_in, mlp_blocks = tie(mlp_in, mlp_blocks)
        w_fc = join(CoreSwap(mlp_blocks, place, 0, fc_width))
        out_swap = CoreSwap(mlp_blocks, place, 1, fc_width)
        pre_act = dot_f32(mlp_in, w_fc) + bias_fc
        activated = narrow(jax.nn.gelu(pre_act, approximate=True))
        w_out_t = join(out_swap)
        mate_part = dot_second(activated[block_len:], w_out_t)
        own_part = dot_second(activated[:block_len], w_out_t)
        hidden = middle + core_sum(own_part, mate_part) + shifts[3]
        weights.append((w_qkv, w_proj_t, w_fc, w_out_t))
        stash.append(
            (near, hat_attn, inv_attn, packed, mixed, log_total, hat_mlp, inv_mlp, mlp_in,
             pre_act, activated)
        )

    own_output = narrow(hidden)
    output = both_seqs(own_output, other_tp(own_output))

    last_sum = None
    sums = {}
    waiting, latest, first_sum = [], [], []
    small_parts = [None] * layer_count

    def advance(value, name):
        nonlocal last_sum
        share = waiting.pop(0)
        assert share[0] == name
        value, share, last_sum = tie(value, share[1], last_sum)
        if latest:
            sums[latest[0]] = last_sum
        else:
            first_sum.append(last_sum)
        latest[:] = [name]
        last_sum = lax.psum(share, "ctx")
        sums[name] = last_sum
        return value

    for layer in reversed(range(layer_count)):
        near, hat_attn, inv_attn, packed, mixed, log_total = stash[layer][:6]
        hat_mlp, inv_mlp, mlp_in, pre_act, activated = stash[layer][6:]
        gains = vectors[layer, :2]
        w_qkv, w_proj_t, w_fc, w_out_t = weights[layer]
        final = layer == 0
        grad_out_bias = jnp.sum(grad_hidden, axis=0)
        if not final:
            last_sum = bias_parts
        grad_low = narrow(grad_hidden)
        grad_low = jnp.concatenate([grad_low, mate(grad_low)])
        out_swap = scatter_swap(narrow(dot_first(grad_low, activated)), place)
        grad_pre = narrow(gelu_slope(pre_act, dot_f32(grad_low, w_out_t)))
        grad_pre, out_swap.came = tie(grad_pre, out_swap.came)
        if final:
            grad_pre = advance(grad_pre, "attn1")
        waiting.append(("out%d" % layer, scatter_sum(join(out_swap))))
        grad_fc_bias = jnp.sum(wide(grad_pre), axis=0)
        mate_part = dot_second(grad_pre[block_len:], w_fc)
        own_part = dot_second(grad_pre[:block_len], w_fc)
        grad_norm_in = core_sum(own_part, mate_part)
        fc_swap = scatter_swap(narrow(dot_first(mlp_in, grad_pre)), place)
        grad_from_mlp, grad_gain_mlp, grad_shift_mlp = norm_backward(
            grad_norm_in, hat_mlp, inv_mlp, gains[1]
        )
        grad_middle = grad_hidden + grad_from_mlp
        grad_proj_bias = jnp.sum(grad_middle, axis=0)
        grad_low = narrow(grad_middle)
        grad_low = jnp.concatenate([grad_low, mate(grad_low)])
        grad_mixed = narrow(dot_f32(grad_low, w_proj_t)).reshape(mixed.shape)
        proj_swap = scatter_swap(
            narrow(dot_first(grad_low, mixed.reshape(2 * block_len, half_width))), place
        )
        grad_mixed, fc_swap.came, proj_swap.came = tie(grad_mixed, fc_swap.came, proj_swap.came)
        grad_fc = join(fc_swap, proj_swap)
        grad_packed = attention_backward(packed, mixed, grad_mixed, log_total, low_pos)
        grad_packed = advance(grad_packed, "out%d" % layer)
        grad_packed, grad_fc = tie(grad_packed, grad_fc)
        waiting.append(("fc%d" % layer, scatter_sum(grad_fc)))
        mate_part = dot_second(grad_packed[1], w_qkv)
        own_part = dot_second(grad_packed[0], w_qkv)
        grad_near = core_sum(own_part, mate_part)
        far_total, grad_attn_in = grad_near[:last], grad_near[last:]
        rows = grad_packed.reshape(2 * key_len, -1)
        grad_near, rows = tie(grad_near, rows)
        far_total, grad_attn_in = grad_near[:last], grad_near[last:]
        carried = backward_step(narrow(far_total[:block_len]))
        attn_swap = scatter_swap(narrow(dot_first(near, rows)), place)
        for step in range(1, reach + 1):
            if step == 1:
                carried, grad_attn = tie(carried, join(attn_swap))
                if final:
                    carried = advance(carried, "fc%d" % layer)
                else:
                    carried, grad_attn, waiting[0] = tie(carried, grad_attn, waiting[0][1])
                    waiting[0] = ("fc%d" % layer, waiting[0])
                waiting.append(("attn%d" % layer, scatter_sum(grad_attn)))
            if step == 2 and not final:
                carried = advance(carried, "fc%d" % layer)
            arrived = wide(carried)
            if step < reach:
                section = far_total[step * block_len : (step + 1) * block_len]
                carried = backward_step(narrow(arrived + section))
            else:
                grad_attn_in = grad_attn_in + arrived
        grad_from_attn, grad_gain_attn, grad_shift_attn = norm_backward(
            grad_attn_in, hat_attn, inv_attn, gains[0]
        )
        grad_hidden = grad_middle + grad_from_attn
        grad_bias = jnp.sum(wide(rows), axis=0).reshape(-1, 3, PAIR)
        halves = jnp.concatenate(
            [grad_bias[:, 0].reshape(-1), grad_bias[:, 2].reshape(-1), grad_fc_bias]
        )
        empty = jnp.zeros_like(halves)
        if not final:
            grad_out_bias = jnp.where(place.ctx == 0, jnp.sum(first_sum[0], axis=0), 0.0)
        small_parts[layer] = jnp.concatenate(
            [
                grad_gain_attn, grad_gain_mlp,
                grad_shift_attn, grad_proj_bias, grad_shift_mlp, grad_out_bias,
                jnp.where(place.core == 0, halves, empty),
                jnp.where(place.core == 1, halves, empty),
            ]
        )

    small = small_total(jnp.stack(small_parts), place)
    far_grad = wide(other_tp(narrow(grad_hidden)))
    token_grad = both_seqs(grad_hidden, far_grad)
    advance((), "attn0")
    split = 6 * model_width
    norms = small[:, :split].reshape(layer_count, 6, model_width)
    norms = lax.dynamic_slice_in_dim(norms, place.shard * shard_rows, shard_rows, 2)
    halves = small[:, split:].reshape(layer_count, 2, -1)
    halves = lax.dynamic_index_in_dim(halves, place.tp, 1, False)
    attn = [sums["attn%d" % layer] for layer in range(layer_count)]
    fc_proj = [sums["fc%d" % layer] for layer in range(layer_count)]
    return (
        output,
        token_grad,
        norms[:, :2],
        norms[:, 2:],
        unpack_heads(*attn),
        halves[:, : 2 * half_width].reshape(layer_count, 2, half_width),
        jnp.stack([jnp.transpose(wide(v[:, fc_width:])) for v in fc_proj]),
        jnp.stack([wide(v[:, :fc_width]) for v in fc_proj]),
        halves[:, 2 * half_width :],
        jnp.stack([jnp.transpose(wide(sums["out%d" % layer])) for layer in range(layer_count)]),
    )


def solution(mesh):
    devices = mesh.devices
    devices = devices.reshape((devices.shape[0] // 2, 2) + devices.shape[1:])
    mesh = jax.sharding.Mesh(devices, ("x", "core", "ctx", "tp"))
    placed = (
        P(("x", "core"), "ctx", None),
        P(("x", "core"), "ctx", None),
        P(("x", "core"), None),
        P(None, None, ("x", "core")),
        P(None, None, ("x", "core")),
        P(None, None, ("x", "core"), "tp"),
        P(None, None, "tp"),
        P(None, "tp", ("x", "core")),
        P(None, ("x", "core"), "tp"),
        P(None, "tp"),
        P(None, "tp", ("x", "core")),
    )
    return jax.shard_map(
        per_device,
        mesh=mesh,
        in_specs=placed,
        out_specs=(
            P(("x", "core"), "ctx", None),
            P(("x", "core"), "ctx", None),
            P(None, None, ("x", "core")),
            P(None, None, ("x", "core")),
            P(None, None, ("x", "core"), "tp"),
            P(None, None, "tp"),
            P(None, "tp", ("x", "core")),
            P(None, ("x", "core"), "tp"),
            P(None, "tp"),
            P(None, "tp", ("x", "core")),
        ),
        check_vma=False,
    )
```

```python
import jax
import jax.numpy as jnp
from jax import lax
from jax.experimental import pallas as pl
from jax.experimental.pallas import tpu as pltpu
from jax.sharding import PartitionSpec as P

HD = 64
WINDOW = 1024
TILE = 256
masked_score = -1e30


def contract(left_side, right_side, left_dim, right_dim):
    return lax.dot_general(
        left_side, right_side, (((left_dim,), (right_dim,)), ((), ())),
        preferred_element_type=jnp.float32,
    )


def half_mask(shape, half):
    lane = lax.broadcasted_iota(jnp.int32, shape, 1)
    return (lane < HD) if half == 0 else (lane >= HD)


PAIR = 2 * HD


def forward_kernel(qkv_ref, low_ref, mixed_ref, total_ref):
    block_len = mixed_ref.shape[1]
    first = qkv_ref.shape[1] - block_len
    span = WINDOW + TILE
    eye = lax.broadcasted_iota(jnp.int32, (TILE, TILE), 0) == lax.broadcasted_iota(
        jnp.int32, (TILE, TILE), 1
    )
    for block in range(block_len // TILE):
        rows = pl.ds(block * TILE, TILE)
        window = pl.ds(block * TILE, span)
        queries = qkv_ref[0, pl.ds(first + block * TILE, TILE), :PAIR]
        queries = queries * jnp.asarray(HD ** (-0.5), jnp.bfloat16)
        keys = qkv_ref[0, window, PAIR : 2 * PAIR]
        values = qkv_ref[0, window, 2 * PAIR :]
        low_pos = low_ref[0, rows, :] - block * TILE
        key_pos = lax.broadcasted_iota(jnp.int32, (TILE, span), 1)
        query_pos = lax.broadcasted_iota(jnp.int32, (TILE, TILE), 0) + WINDOW
        allowed = key_pos >= low_pos
        causal = key_pos[:, WINDOW:] <= query_pos
        mixed = jnp.zeros((TILE, 2 * HD), jnp.float32)
        for half in range(2):
            scores = contract(
                jnp.where(half_mask(queries.shape, half), queries, 0), keys, 1, 1
            )
            early = jnp.where(allowed[:, :WINDOW], scores[:, :WINDOW], masked_score)
            late = jnp.where(allowed[:, WINDOW:] & causal, scores[:, WINDOW:], masked_score)
            top_score = jnp.maximum(
                jnp.max(early, axis=1, keepdims=True), jnp.max(late, axis=1, keepdims=True)
            )
            early = jnp.exp(early - top_score)
            late = jnp.exp(late - top_score)
            row_total = jnp.sum(early, axis=1, keepdims=True) + jnp.sum(
                late, axis=1, keepdims=True
            )
            part = contract(early.astype(jnp.bfloat16), values[:WINDOW], 1, 0) + contract(
                late.astype(jnp.bfloat16), values[WINDOW:], 1, 0
            )
            part = part * (1.0 / row_total)
            mixed = jnp.where(half_mask(mixed.shape, half), part, mixed)
            log_total = top_score + jnp.log(row_total)
            total_ref[0, 0, half : half + 1, rows] = jnp.sum(
                jnp.where(eye, log_total, 0.0), axis=0, keepdims=True
            )
        mixed_ref[0, rows, :] = mixed.astype(jnp.bfloat16)


def attention_forward(packed, low_pos):
    groups, key_len, width = packed.shape
    block_len = low_pos.shape[1]
    pairs = width // (3 * PAIR)
    pick = lambda seq, pair: (seq, 0, pair)
    return pl.pallas_call(
        forward_kernel,
        grid=(groups, pairs),
        in_specs=[
            pl.BlockSpec((1, key_len, 3 * PAIR), pick),
            pl.BlockSpec((1, block_len, 1), lambda seq, pair: (seq, 0, 0)),
        ],
        out_specs=[
            pl.BlockSpec((1, block_len, PAIR), pick),
            pl.BlockSpec((1, 1, 2, block_len), lambda seq, pair: (seq, pair, 0, 0)),
        ],
        out_shape=[
            jax.ShapeDtypeStruct((groups, block_len, pairs * PAIR), jnp.bfloat16),
            jax.ShapeDtypeStruct((groups, pairs, 2, block_len), jnp.float32),
        ],
        compiler_params=pltpu.CompilerParams(vmem_limit_bytes=56 << 20),
        cost_estimate=pl.CostEstimate(
            flops=16 * groups * pairs * block_len * (WINDOW + TILE) * HD,
            bytes_accessed=2 * groups * width * key_len,
            transcendentals=2 * groups * pairs * block_len * (WINDOW + TILE),
        ),
    )(packed, low_pos[:, :, None])


def backward_kernel(qkv_ref, mixed_ref, grad_ref, total_ref, low_ref, out_ref, gk_sum, gv_sum):
    block_len = mixed_ref.shape[1]
    first = qkv_ref.shape[1] - block_len
    span = WINDOW + TILE
    scale = HD ** (-0.5)
    gk_sum[...] = jnp.zeros_like(gk_sum)
    gv_sum[...] = jnp.zeros_like(gv_sum)
    eye = lax.broadcasted_iota(jnp.int32, (TILE, TILE), 0) == lax.broadcasted_iota(
        jnp.int32, (TILE, TILE), 1
    )
    for block in range(block_len // TILE):
        rows = pl.ds(block * TILE, TILE)
        window = pl.ds(block * TILE, span)
        queries = qkv_ref[0, pl.ds(first + block * TILE, TILE), :PAIR]
        queries = queries * jnp.asarray(scale, jnp.bfloat16)
        keys = qkv_ref[0, window, PAIR : 2 * PAIR]
        values = qkv_ref[0, window, 2 * PAIR :]
        grads = grad_ref[0, rows, :]
        product = grads.astype(jnp.float32) * mixed_ref[0, rows, :].astype(jnp.float32)
        low_pos = low_ref[0, :, rows] - block * TILE
        key_pos = lax.broadcasted_iota(jnp.int32, (span, TILE), 0)
        query_pos = lax.broadcasted_iota(jnp.int32, (TILE, TILE), 1) + WINDOW
        allowed = key_pos >= low_pos
        late_allowed = allowed[WINDOW:] & (key_pos[WINDOW:] <= query_pos)
        keys_t = jnp.transpose(keys)
        gq_parts = []
        for half in range(2):
            mask = half_mask(queries.shape, half)
            q_half = jnp.where(mask, queries, 0)
            g_half = jnp.where(mask, grads, 0)
            delta = jnp.sum(jnp.where(mask, product, 0.0), axis=1, keepdims=True)
            delta = jnp.sum(jnp.where(eye, delta, 0.0), axis=0, keepdims=True)
            log_total = total_ref[0, 0, half : half + 1, rows]
            scores = contract(keys, q_half, 1, 1)
            probs = jnp.concatenate(
                [
                    jnp.where(allowed[:WINDOW], jnp.exp(scores[:WINDOW] - log_total), 0.0),
                    jnp.where(late_allowed, jnp.exp(scores[WINDOW:] - log_total), 0.0),
                ]
            )
            grad_probs = contract(values, g_half, 1, 1)
            grad_scores = (probs * (grad_probs - delta)).astype(jnp.bfloat16)
            gv_sum[window, :] += contract(probs.astype(jnp.bfloat16), g_half, 1, 0)
            gk_sum[window, :] += contract(grad_scores, q_half, 1, 0)
            gq_parts.append(contract(keys_t[half * HD : (half + 1) * HD], grad_scores, 1, 0))
        gq = jnp.transpose(jnp.concatenate(gq_parts)) * scale
        out_ref[0, pl.ds(first + block * TILE, TILE), :PAIR] = gq.astype(jnp.bfloat16)
    out_ref[0, :first, :PAIR] = jnp.zeros((first, PAIR), jnp.bfloat16)
    out_ref[0, :, PAIR : 2 * PAIR] = gk_sum[...].astype(jnp.bfloat16)
    out_ref[0, :, 2 * PAIR :] = gv_sum[...].astype(jnp.bfloat16)


def attention_backward(packed, mixed, grads, log_total, low_pos):
    groups, key_len, width = packed.shape
    block_len = mixed.shape[1]
    pairs = width // (3 * PAIR)
    pick = lambda seq, pair: (seq, 0, pair)
    row_spec = pl.BlockSpec((1, block_len, PAIR), pick)
    packed_spec = pl.BlockSpec((1, key_len, 3 * PAIR), pick)
    return pl.pallas_call(
        backward_kernel,
        grid=(groups, pairs),
        in_specs=[
            packed_spec, row_spec, row_spec,
            pl.BlockSpec((1, 1, 2, block_len), lambda seq, pair: (seq, pair, 0, 0)),
            pl.BlockSpec((1, 1, block_len), lambda seq, pair: (seq, 0, 0)),
        ],
        out_specs=packed_spec,
        out_shape=jax.ShapeDtypeStruct(packed.shape, jnp.bfloat16),
        scratch_shapes=[
            pltpu.VMEM((key_len, PAIR), jnp.float32),
            pltpu.VMEM((key_len, PAIR), jnp.float32),
        ],
        compiler_params=pltpu.CompilerParams(vmem_limit_bytes=56 << 20),
        cost_estimate=pl.CostEstimate(
            flops=40 * groups * pairs * block_len * (WINDOW + TILE) * HD,
            bytes_accessed=4 * groups * width * key_len,
            transcendentals=2 * groups * pairs * block_len * (WINDOW + TILE),
        ),
    )(packed, mixed, grads, log_total, low_pos[:, None, :])


norm_eps = 1e-05


def mate(value):
    return lax.ppermute(value, "core", [(0, 1), (1, 0)])


def other_tp(value):
    return lax.ppermute(value, "tp", [(0, 1), (1, 0)])


def onward(value):
    count = lax.axis_size("ctx")
    return lax.ppermute(value, "ctx", [(i, i + 1) for i in range(count - 1)])


def backward_step(value):
    count = lax.axis_size("ctx")
    return lax.ppermute(value, "ctx", [(i + 1, i) for i in range(count - 1)])


class Place:
    def __init__(self):
        self.chips = lax.axis_size("x")
        self.core = lax.axis_index("core")
        self.shard = lax.axis_index("x") * 2 + self.core
        self.tp = lax.axis_index("tp")
        self.ctx = lax.axis_index("ctx")
        self.home = self.core == self.tp


def tie(*values):
    return lax.optimization_barrier(values)


def ordered(own, other, position, axis=0):
    return jnp.where(
        position == 0,
        jnp.stack([own, other], axis=axis),
        jnp.stack([other, own], axis=axis),
    )


def join_kernel(core_ref, *refs):
    out_ref = refs[-1]
    own = pl.program_id(1) == core_ref[0]
    at = 0
    for blocks_ref, came_ref in zip(refs[0:-1:2], refs[1:-1:2]):
        width = came_ref.shape[2]

        @pl.when(own)
        def _(at=at, width=width, blocks_ref=blocks_ref):
            out_ref[:, at : at + width] = blocks_ref[0, 0]

        @pl.when(jnp.logical_not(own))
        def _(at=at, width=width, came_ref=came_ref):
            out_ref[:, at : at + width] = came_ref[0]

        at += width


class CoreSwap:
    def __init__(self, blocks, place, column=0, width=None):
        self.place, self.blocks, self.column = place, blocks, column
        width = blocks.shape[3] if width is None else width
        other = lax.dynamic_index_in_dim(blocks, 1 - place.core, 1, False)
        self.came = mate(other[..., column * width : (column + 1) * width])


def join(*swaps):
    chips, rows = swaps[0].came.shape[:2]
    in_specs, operands, total = [], [], 0
    for swap in swaps:
        width = swap.came.shape[2]
        in_specs += [
            pl.BlockSpec(
                (1, 1, rows, width),
                lambda chip, part, core, column=swap.column: (chip, core[0], 0, column),
            ),
            pl.BlockSpec((1, rows, width), lambda chip, part, core: (chip, 0, 0)),
        ]
        operands += [swap.blocks, swap.came]
        total += width
    return pl.pallas_call(
        join_kernel,
        grid_spec=pltpu.PrefetchScalarGridSpec(
            num_scalar_prefetch=1,
            grid=(chips, 2),
            in_specs=in_specs,
            out_specs=pl.BlockSpec((rows, total), lambda chip, part, core: (chip * 2 + part, 0)),
        ),
        out_shape=jax.ShapeDtypeStruct((chips * 2 * rows, total), jnp.bfloat16),
        compiler_params=pltpu.CompilerParams(vmem_limit_bytes=24 << 20),
        cost_estimate=pl.CostEstimate(
            flops=0, bytes_accessed=8 * chips * rows * total, transcendentals=0
        ),
    )(swaps[0].place.core.reshape(1).astype(jnp.int32), *operands)


def gather_blocks(piece, place):
    whole = lax.all_gather(piece, ("x", "tp"), axis=0, tiled=False)
    return whole.reshape((place.chips, 2) + piece.shape)


def scatter_swap(grads, place):
    return CoreSwap(grads.reshape(place.chips, 2, -1, grads.shape[1]), place)


def scatter_sum(blocks):
    return lax.psum_scatter(blocks, ("x", "tp"), scatter_dimension=0, tiled=True)


def dot_f32(left_side, right_side):
    return jnp.dot(left_side, right_side, preferred_element_type=jnp.float32)


def dot_first(left_side, right_side):
    return contract(left_side, right_side, 0, 0)


def dot_second(left_side, right_side):
    return contract(left_side, right_side, 1, 1)


def gather_small(value, place):
    if place.chips != 2:
        return lax.all_gather(value, ("x", "core"), axis=1, tiled=True)
    near = mate(value)
    pair = ordered(value, near, place.core, 1).reshape(value.shape[0], -1)
    far = lax.ppermute(pair, "x", [(0, 1), (1, 0)])
    return ordered(pair, far, lax.axis_index("x"), 1).reshape(value.shape[0], -1)


def norm_forward(hidden, norm_gain, norm_shift):
    row_mean = jnp.mean(hidden, axis=-1, keepdims=True)
    centred = hidden - row_mean
    variance = jnp.mean(centred * centred, axis=-1, keepdims=True)
    inv_std = lax.rsqrt(variance + norm_eps)
    norm_hat = centred * inv_std
    return ((norm_hat * norm_gain + norm_shift).astype(jnp.bfloat16), norm_hat, inv_std)


def norm_backward(grad_out, norm_hat, inv_std, norm_gain):
    scaled = grad_out * norm_gain
    mean_one = jnp.mean(scaled, axis=-1, keepdims=True)
    mean_two = jnp.mean(scaled * norm_hat, axis=-1, keepdims=True)
    grad_input = inv_std * (scaled - mean_one - norm_hat * mean_two)
    return (grad_input, jnp.sum(grad_out * norm_hat, axis=0), jnp.sum(grad_out, axis=0))


def wide(value):
    return value.astype(jnp.float32)


def narrow(value):
    return value.astype(jnp.bfloat16)


def pick_block(value, index, count):
    size = value.shape[0] // count
    return lax.dynamic_slice_in_dim(value, index * size, size, 0)


def small_total(value, place):
    if place.chips != 2 or lax.axis_size("ctx") != 4:
        return lax.psum(value, ("x", "core", "ctx", "tp"))
    value = value + mate(value)
    value = value + other_tp(value)
    value = value + lax.ppermute(value, "x", [(0, 1), (1, 0)])
    value = value + lax.ppermute(value, "ctx", [(0, 1), (3, 2)])
    value = value + lax.ppermute(value, "ctx", [(1, 2), (2, 1)])
    outer = (place.ctx == 0) | (place.ctx == 3)
    return jnp.where(outer, lax.ppermute(value, "ctx", [(1, 0), (2, 3)]), value)


def core_sum(own_part, mate_part):
    return own_part + wide(mate(narrow(mate_part)))


def gelu_slope(pre_act, grad_act):
    pullback = jax.vjp(lambda values: jax.nn.gelu(values, approximate=True), pre_act)[1]
    return pullback(grad_act)[0]


def pair_major(value):
    width = value.shape[-1]
    return jnp.concatenate(
        [value[kind, :, at : at + PAIR] for at in range(0, width, PAIR) for kind in range(3)],
        axis=-1,
    )


def pack_kernel(qkv_ref, proj_ref, out_ref):
    width = qkv_ref.shape[3]
    for pair in range(width // PAIR):
        for kind in range(3):
            at = (3 * pair + kind) * PAIR
            out_ref[:, at : at + PAIR] = qkv_ref[0, kind, :, pair * PAIR : (pair + 1) * PAIR]
    out_ref[:, 3 * width :] = jnp.transpose(proj_ref[0])


def attn_piece(layer, qkv_weight, proj_weight):
    rows, width = qkv_weight.shape[2:]
    return pl.pallas_call(
        pack_kernel,
        grid=(1,),
        in_specs=[
            pl.BlockSpec((1, 3, rows, width), lambda step: (layer, 0, 0, 0)),
            pl.BlockSpec((1, width, rows), lambda step: (layer, 0, 0)),
        ],
        out_specs=pl.BlockSpec((rows, 4 * width), lambda step: (0, 0)),
        out_shape=jax.ShapeDtypeStruct((rows, 4 * width), jnp.bfloat16),
        compiler_params=pltpu.CompilerParams(vmem_limit_bytes=24 << 20),
    )(qkv_weight, proj_weight)


def unpack_kernel(first_ref, second_ref, out_ref):
    kind = pl.program_id(0)
    width = out_ref.shape[3]
    for pair in range(width // PAIR):
        at = pl.multiple_of((3 * pair + kind) * PAIR, PAIR)
        for layer, ref in enumerate((first_ref, second_ref)):
            out_ref[layer, 0, :, pair * PAIR : (pair + 1) * PAIR] = ref[
                :, pl.ds(at, PAIR)
            ].astype(jnp.float32)


def unpack_heads(first, second):
    rows, width = first.shape
    width = width // 3
    block = pl.BlockSpec((rows, 3 * width), lambda kind: (0, 0))
    return pl.pallas_call(
        unpack_kernel,
        grid=(3,),
        in_specs=[block, block],
        out_specs=pl.BlockSpec((2, 1, rows, width), lambda kind: (0, kind, 0, 0)),
        out_shape=jax.ShapeDtypeStruct((2, 3, rows, width), jnp.float32),
        compiler_params=pltpu.CompilerParams(vmem_limit_bytes=24 << 20),
    )(first, second)


def per_device(
    tokens,
    cotangent,
    doc_lengths,
    norm_gains,
    norm_biases,
    qkv_weight,
    qv_bias,
    proj_weight,
    fc_weight,
    fc_bias,
    out_weight,
):
    place = Place()
    block_len, model_width = tokens.shape[1:]
    shard_rows = qkv_weight.shape[2]
    half_width = qkv_weight.shape[3]
    layer_count = qkv_weight.shape[0]
    reach = WINDOW // block_len
    key_len = (reach + 1) * block_len
    last = reach * block_len

    def my_seq(value):
        return lax.dynamic_index_in_dim(value, place.tp, 0, False)

    def both_seqs(own, other):
        return ordered(own, other, place.tp)

    own_tokens = my_seq(tokens)
    grad_hidden = wide(my_seq(cotangent))
    bias_parts = jnp.sum(grad_hidden.reshape(16, -1, model_width), axis=1)
    bias_parts = lax.psum(bias_parts, "ctx")
    attn_blocks = gather_blocks(attn_piece(0, qkv_weight, proj_weight), place)
    halo = [onward(own_tokens)]
    for _ in range(reach - 1):
        halo.insert(0, onward(halo[0]))
    vectors = jnp.concatenate([norm_gains, norm_biases], axis=1)
    vectors = gather_small(vectors.reshape(-1, vectors.shape[2]), place)
    vectors = wide(vectors).reshape(layer_count, 6, model_width)
    biases = jnp.concatenate([qv_bias.reshape(layer_count, -1), fc_bias], axis=1)
    biases = wide(jnp.where(place.home, biases, other_tp(biases)))
    lengths = my_seq(doc_lengths)
    lengths = jnp.stack([lengths, mate(lengths)])
    mlp_pieces = [
        jnp.concatenate([fc_weight[layer], jnp.transpose(out_weight[layer])], axis=1)
        for layer in range(layer_count)
    ]
    attn_later = attn_piece(1, qkv_weight, proj_weight)
    halo[-1], mlp_pieces, attn_later = tie(halo[-1], mlp_pieces, attn_later)
    mlp_blocks = gather_blocks(mlp_pieces[0], place)
    fc_width = fc_weight.shape[2]

    doc_ends = jnp.cumsum(lengths, axis=1)
    first_pos = place.ctx * block_len
    query_pos = first_pos + jnp.arange(block_len, dtype=jnp.int32)
    started = doc_ends[:, None, :] <= query_pos[None, :, None]
    doc_start = jnp.max(jnp.where(started, doc_ends[:, None, :], 0), axis=-1)
    low_pos = jnp.maximum(doc_start, query_pos[None, :] - (WINDOW - 1))
    low_pos = (low_pos - first_pos + last).astype(jnp.int32)

    hidden = wide(own_tokens)
    stash = []
    weights = []
    for layer in range(layer_count):
        gains, shifts = vectors[layer, :2], vectors[layer, 2:]
        bias_q, bias_v = biases[layer, :half_width], biases[layer, half_width : 2 * half_width]
        bias_qkv = pair_major(jnp.stack([bias_q, jnp.zeros_like(bias_q), bias_v])[:, None])
        bias_fc = biases[layer, 2 * half_width :]
        attn_in, hat_attn, inv_attn = norm_forward(hidden, gains[0], shifts[0])
        own_near = [attn_in]
        mate_near = [mate(attn_in)]
        attn_swap = CoreSwap(attn_blocks, place)
        if layer == 0:
            w_attn = join(attn_swap)
        step_value = attn_in
        for index in range(reach):
            if layer == 0:
                part = norm_forward(wide(halo[reach - 1 - index]), gains[0], shifts[0])[0]
            else:
                step_value = part = onward(step_value)
                if index == 0:
                    step_value, piece = tie(step_value, mlp_pieces[layer])
                    mlp_blocks = gather_blocks(piece, place)
                    part = step_value
                if index == 1:
                    step_value, w_attn = tie(step_value, join(attn_swap))
                    part = step_value
            own_near.insert(0, part)
            mate_near.insert(0, mate(part))
        near = jnp.concatenate(own_near + mate_near)
        if layer == 0:
            near, bias_parts = tie(near, bias_parts)
        w_qkv, w_proj_t = w_attn[:, : 3 * half_width], w_attn[:, 3 * half_width :]
        packed = narrow(dot_f32(near, w_qkv) + bias_qkv).reshape(2, key_len, -1)
        mixed, log_total = attention_forward(packed, low_pos)
        if layer + 1 < layer_count:
            mixed, attn_later = tie(mixed, attn_later)
            attn_blocks = gather_blocks(attn_later, place)
        mate_part = dot_second(mixed[1], w_proj_t)
        own_part = dot_second(mixed[0], w_proj_t)
        middle = hidden + core_sum(own_part, mate_part) + shifts[1]
        mlp_own, hat_mlp, inv_mlp = norm_forward(middle, gains[1], shifts[2])
        mlp_in = jnp.concatenate([mlp_own, mate(mlp_own)])
        mlp_in, mlp_blocks = tie(mlp_in, mlp_blocks)
        w_fc = join(CoreSwap(mlp_blocks, place, 0, fc_width))
        out_swap = CoreSwap(mlp_blocks, place, 1, fc_width)
        pre_act = dot_f32(mlp_in, w_fc) + bias_fc
        activated = narrow(jax.nn.gelu(pre_act, approximate=True))
        w_out_t = join(out_swap)
        mate_part = dot_second(activated[block_len:], w_out_t)
        own_part = dot_second(activated[:block_len], w_out_t)
        hidden = middle + core_sum(own_part, mate_part) + shifts[3]
        weights.append((w_qkv, w_proj_t, w_fc, w_out_t))
        stash.append(
            (near, hat_attn, inv_attn, packed, mixed, log_total, hat_mlp, inv_mlp, mlp_in,
             pre_act, activated)
        )

    own_output = narrow(hidden)
    far_output = other_tp(own_output)

    last_sum = None
    sums = {}
    waiting, latest, first_sum = [], [], []
    small_parts = [None] * layer_count

    def advance(value, name):
        nonlocal last_sum
        share = waiting.pop(0)
        assert share[0] == name
        value, share, last_sum = tie(value, share[1], last_sum)
        if latest:
            sums[latest[0]] = last_sum
        else:
            first_sum.append(last_sum)
        latest[:] = [name]
        last_sum = lax.psum(share, "ctx")
        sums[name] = last_sum
        return value

    for layer in reversed(range(layer_count)):
        near, hat_attn, inv_attn, packed, mixed, log_total = stash[layer][:6]
        hat_mlp, inv_mlp, mlp_in, pre_act, activated = stash[layer][6:]
        gains = vectors[layer, :2]
        w_qkv, w_proj_t, w_fc, w_out_t = weights[layer]
        final = layer == 0
        grad_out_bias = jnp.sum(grad_hidden, axis=0)
        if not final:
            last_sum = bias_parts
        grad_low = narrow(grad_hidden)
        grad_low = jnp.concatenate([grad_low, mate(grad_low)])
        out_swap = scatter_swap(narrow(dot_first(grad_low, activated)), place)
        grad_pre = narrow(gelu_slope(pre_act, dot_f32(grad_low, w_out_t)))
        grad_pre, out_swap.came = tie(grad_pre, out_swap.came)
        if final:
            grad_pre = advance(grad_pre, "attn1")
        waiting.append(("out%d" % layer, scatter_sum(join(out_swap))))
        grad_fc_bias = jnp.sum(wide(grad_pre), axis=0)
        mate_part = dot_second(grad_pre[block_len:], w_fc)
        own_part = dot_second(grad_pre[:block_len], w_fc)
        grad_norm_in = core_sum(own_part, mate_part)
        fc_swap = scatter_swap(narrow(dot_first(mlp_in, grad_pre)), place)
        grad_from_mlp, grad_gain_mlp, grad_shift_mlp = norm_backward(
            grad_norm_in, hat_mlp, inv_mlp, gains[1]
        )
        grad_middle = grad_hidden + grad_from_mlp
        grad_proj_bias = jnp.sum(grad_middle, axis=0)
        grad_low = narrow(grad_middle)
        grad_low = jnp.concatenate([grad_low, mate(grad_low)])
        grad_mixed = narrow(dot_f32(grad_low, w_proj_t)).reshape(mixed.shape)
        proj_swap = scatter_swap(
            narrow(dot_first(grad_low, mixed.reshape(2 * block_len, half_width))), place
        )
        grad_mixed, fc_swap.came, proj_swap.came = tie(grad_mixed, fc_swap.came, proj_swap.came)
        grad_mixed, grad_fc = tie(grad_mixed, join(fc_swap, proj_swap))
        if not final:
            grad_mixed = advance(grad_mixed, "out%d" % layer)
        grad_packed = attention_backward(packed, mixed, grad_mixed, log_total, low_pos)
        if final:
            grad_packed = advance(grad_packed, "out%d" % layer)
        else:
            grad_packed, far_output = tie(grad_packed, far_output)
        waiting.append(("fc%d" % layer, scatter_sum(grad_fc)))
        mate_part = dot_second(grad_packed[1], w_qkv)
        own_part = dot_second(grad_packed[0], w_qkv)
        grad_near = core_sum(own_part, mate_part)
        far_total, grad_attn_in = grad_near[:last], grad_near[last:]
        rows = grad_packed.reshape(2 * key_len, -1)
        grad_near, rows = tie(grad_near, rows)
        far_total, grad_attn_in = grad_near[:last], grad_near[last:]
        carried = backward_step(narrow(far_total[:block_len]))
        grad_qkv = narrow(dot_first(near, rows))
        grad_bias = jnp.sum(wide(rows), axis=0)
        if final:
            grad_qkv = advance(grad_qkv, "fc%d" % layer)
            attn_swap = scatter_swap(grad_qkv, place)
        for step in range(1, reach + 1):
            if step == 1 and not final:
                carried, grad_qkv, last_sum = tie(carried, grad_qkv, last_sum)
                attn_swap = scatter_swap(grad_qkv, place)
            if step == 1 and final:
                carried, grad_attn = tie(carried, join(attn_swap))
                waiting.append(("attn%d" % layer, scatter_sum(grad_attn)))
            if step == 2 and not final:
                carried, grad_bias, grad_attn = tie(carried, grad_bias, join(attn_swap))
                carried = advance(carried, "fc%d" % layer)
                waiting.append(("attn%d" % layer, scatter_sum(grad_attn)))
            if step == 2 and final:
                carried, grad_bias = tie(carried, grad_bias)
                carried = advance(carried, "attn%d" % layer)
            arrived = wide(carried)
            if step < reach:
                section = far_total[step * block_len : (step + 1) * block_len]
                carried = backward_step(narrow(arrived + section))
            else:
                grad_attn_in = grad_attn_in + arrived
        grad_from_attn, grad_gain_attn, grad_shift_attn = norm_backward(
            grad_attn_in, hat_attn, inv_attn, gains[0]
        )
        grad_hidden = grad_middle + grad_from_attn
        grad_bias = grad_bias.reshape(-1, 3, PAIR)
        halves = jnp.concatenate(
            [grad_bias[:, 0].reshape(-1), grad_bias[:, 2].reshape(-1), grad_fc_bias]
        )
        empty = jnp.zeros_like(halves)
        if not final:
            grad_out_bias = jnp.where(place.ctx == 0, jnp.sum(first_sum[0], axis=0), 0.0)
        small_parts[layer] = jnp.concatenate(
            [
                grad_gain_attn, grad_gain_mlp,
                grad_shift_attn, grad_proj_bias, grad_shift_mlp, grad_out_bias,
                jnp.where(place.core == 0, halves, empty),
                jnp.where(place.core == 1, halves, empty),
            ]
        )

    small = small_total(jnp.stack(small_parts), place)
    far_grad = wide(other_tp(narrow(grad_hidden)))
    token_grad = both_seqs(grad_hidden, far_grad)
    split = 6 * model_width
    norms = small[:, :split].reshape(layer_count, 6, model_width)
    norms = lax.dynamic_slice_in_dim(norms, place.shard * shard_rows, shard_rows, 2)
    halves = small[:, split:].reshape(layer_count, 2, -1)
    halves = lax.dynamic_index_in_dim(halves, place.tp, 1, False)
    attn = [sums["attn%d" % layer] for layer in range(layer_count)]
    fc_proj = [sums["fc%d" % layer] for layer in range(layer_count)]
    return (
        both_seqs(own_output, far_output),
        token_grad,
        norms[:, :2],
        norms[:, 2:],
        unpack_heads(*attn),
        halves[:, : 2 * half_width].reshape(layer_count, 2, half_width),
        jnp.stack([jnp.transpose(wide(v[:, fc_width:])) for v in fc_proj]),
        jnp.stack([wide(v[:, :fc_width]) for v in fc_proj]),
        halves[:, 2 * half_width :],
        jnp.stack([jnp.transpose(wide(sums["out%d" % layer])) for layer in range(layer_count)]),
    )


def solution(mesh):
    devices = mesh.devices
    devices = devices.reshape((devices.shape[0] // 2, 2) + devices.shape[1:])
    mesh = jax.sharding.Mesh(devices, ("x", "core", "ctx", "tp"))
    placed = (
        P(("x", "core"), "ctx", None),
        P(("x", "core"), "ctx", None),
        P(("x", "core"), None),
        P(None, None, ("x", "core")),
        P(None, None, ("x", "core")),
        P(None, None, ("x", "core"), "tp"),
        P(None, None, "tp"),
        P(None, "tp", ("x", "core")),
        P(None, ("x", "core"), "tp"),
        P(None, "tp"),
        P(None, "tp", ("x", "core")),
    )
    return jax.shard_map(
        per_device,
        mesh=mesh,
        in_specs=placed,
        out_specs=(
            P(("x", "core"), "ctx", None),
            P(("x", "core"), "ctx", None),
            P(None, None, ("x", "core")),
            P(None, None, ("x", "core")),
            P(None, None, ("x", "core"), "tp"),
            P(None, None, "tp"),
            P(None, "tp", ("x", "core")),
            P(None, ("x", "core"), "tp"),
            P(None, "tp"),
            P(None, "tp", ("x", "core")),
        ),
        check_vma=False,
    )
```

```python
import jax
import jax.numpy as jnp
from jax import lax
from jax.experimental import pallas as pl
from jax.experimental.pallas import tpu as pltpu
from jax.sharding import PartitionSpec as P

HD = 64
WINDOW = 1024
TILE = 256
masked_score = -1e30


def contract(left_side, right_side, left_dim, right_dim):
    return lax.dot_general(
        left_side, right_side, (((left_dim,), (right_dim,)), ((), ())),
        preferred_element_type=jnp.float32,
    )


def half_mask(shape, half):
    lane = lax.broadcasted_iota(jnp.int32, shape, 1)
    return (lane < HD) if half == 0 else (lane >= HD)


PAIR = 2 * HD


def forward_kernel(qkv_ref, low_ref, mixed_ref, total_ref):
    block_len = mixed_ref.shape[1]
    first = qkv_ref.shape[1] - block_len
    span = WINDOW + TILE
    eye = lax.broadcasted_iota(jnp.int32, (TILE, TILE), 0) == lax.broadcasted_iota(
        jnp.int32, (TILE, TILE), 1
    )
    for block in range(block_len // TILE):
        rows = pl.ds(block * TILE, TILE)
        window = pl.ds(block * TILE, span)
        queries = qkv_ref[0, pl.ds(first + block * TILE, TILE), :PAIR]
        queries = queries * jnp.asarray(HD ** (-0.5), jnp.bfloat16)
        keys = qkv_ref[0, window, PAIR : 2 * PAIR]
        values = qkv_ref[0, window, 2 * PAIR :]
        low_pos = low_ref[0, rows, :] - block * TILE
        key_pos = lax.broadcasted_iota(jnp.int32, (TILE, span), 1)
        query_pos = lax.broadcasted_iota(jnp.int32, (TILE, TILE), 0) + WINDOW
        allowed = key_pos >= low_pos
        causal = key_pos[:, WINDOW:] <= query_pos
        mixed = jnp.zeros((TILE, 2 * HD), jnp.float32)
        for half in range(2):
            scores = contract(
                jnp.where(half_mask(queries.shape, half), queries, 0), keys, 1, 1
            )
            early = jnp.where(allowed[:, :WINDOW], scores[:, :WINDOW], masked_score)
            late = jnp.where(allowed[:, WINDOW:] & causal, scores[:, WINDOW:], masked_score)
            top_score = jnp.maximum(
                jnp.max(early, axis=1, keepdims=True), jnp.max(late, axis=1, keepdims=True)
            )
            early = jnp.exp(early - top_score)
            late = jnp.exp(late - top_score)
            row_total = jnp.sum(early, axis=1, keepdims=True) + jnp.sum(
                late, axis=1, keepdims=True
            )
            part = contract(early.astype(jnp.bfloat16), values[:WINDOW], 1, 0) + contract(
                late.astype(jnp.bfloat16), values[WINDOW:], 1, 0
            )
            part = part * (1.0 / row_total)
            mixed = jnp.where(half_mask(mixed.shape, half), part, mixed)
            log_total = top_score + jnp.log(row_total)
            total_ref[0, 0, half : half + 1, rows] = jnp.sum(
                jnp.where(eye, log_total, 0.0), axis=0, keepdims=True
            )
        mixed_ref[0, rows, :] = mixed.astype(jnp.bfloat16)


def attention_forward(packed, low_pos):
    groups, key_len, width = packed.shape
    block_len = low_pos.shape[1]
    pairs = width // (3 * PAIR)
    pick = lambda seq, pair: (seq, 0, pair)
    return pl.pallas_call(
        forward_kernel,
        grid=(groups, pairs),
        in_specs=[
            pl.BlockSpec((1, key_len, 3 * PAIR), pick),
            pl.BlockSpec((1, block_len, 1), lambda seq, pair: (seq, 0, 0)),
        ],
        out_specs=[
            pl.BlockSpec((1, block_len, PAIR), pick),
            pl.BlockSpec((1, 1, 2, block_len), lambda seq, pair: (seq, pair, 0, 0)),
        ],
        out_shape=[
            jax.ShapeDtypeStruct((groups, block_len, pairs * PAIR), jnp.bfloat16),
            jax.ShapeDtypeStruct((groups, pairs, 2, block_len), jnp.float32),
        ],
        compiler_params=pltpu.CompilerParams(vmem_limit_bytes=56 << 20),
        cost_estimate=pl.CostEstimate(
            flops=block_len,
            bytes_accessed=block_len,
            transcendentals=0,
        ),
    )(packed, low_pos[:, :, None])


def backward_kernel(qkv_ref, mixed_ref, grad_ref, total_ref, low_ref, out_ref, gk_sum, gv_sum):
    block_len = mixed_ref.shape[1]
    first = qkv_ref.shape[1] - block_len
    span = WINDOW + TILE
    scale = HD ** (-0.5)
    gk_sum[...] = jnp.zeros_like(gk_sum)
    gv_sum[...] = jnp.zeros_like(gv_sum)
    eye = lax.broadcasted_iota(jnp.int32, (TILE, TILE), 0) == lax.broadcasted_iota(
        jnp.int32, (TILE, TILE), 1
    )
    for block in range(block_len // TILE):
        rows = pl.ds(block * TILE, TILE)
        window = pl.ds(block * TILE, span)
        queries = qkv_ref[0, pl.ds(first + block * TILE, TILE), :PAIR]
        queries = queries * jnp.asarray(scale, jnp.bfloat16)
        keys = qkv_ref[0, window, PAIR : 2 * PAIR]
        values = qkv_ref[0, window, 2 * PAIR :]
        grads = grad_ref[0, rows, :]
        product = grads.astype(jnp.float32) * mixed_ref[0, rows, :].astype(jnp.float32)
        low_pos = low_ref[0, :, rows] - block * TILE
        key_pos = lax.broadcasted_iota(jnp.int32, (span, TILE), 0)
        query_pos = lax.broadcasted_iota(jnp.int32, (TILE, TILE), 1) + WINDOW
        allowed = key_pos >= low_pos
        late_allowed = allowed[WINDOW:] & (key_pos[WINDOW:] <= query_pos)
        keys_t = jnp.transpose(keys)
        gq_parts = []
        for half in range(2):
            mask = half_mask(queries.shape, half)
            q_half = jnp.where(mask, queries, 0)
            g_half = jnp.where(mask, grads, 0)
            delta = jnp.sum(jnp.where(mask, product, 0.0), axis=1, keepdims=True)
            delta = jnp.sum(jnp.where(eye, delta, 0.0), axis=0, keepdims=True)
            log_total = total_ref[0, 0, half : half + 1, rows]
            scores = contract(keys, q_half, 1, 1)
            probs = jnp.concatenate(
                [
                    jnp.where(allowed[:WINDOW], jnp.exp(scores[:WINDOW] - log_total), 0.0),
                    jnp.where(late_allowed, jnp.exp(scores[WINDOW:] - log_total), 0.0),
                ]
            )
            grad_probs = contract(values, g_half, 1, 1)
            grad_scores = (probs * (grad_probs - delta)).astype(jnp.bfloat16)
            gv_sum[window, :] += contract(probs.astype(jnp.bfloat16), g_half, 1, 0)
            gk_sum[window, :] += contract(grad_scores, q_half, 1, 0)
            gq_parts.append(contract(keys_t[half * HD : (half + 1) * HD], grad_scores, 1, 0))
        gq = jnp.transpose(jnp.concatenate(gq_parts)) * scale
        out_ref[0, pl.ds(first + block * TILE, TILE), :PAIR] = gq.astype(jnp.bfloat16)
    out_ref[0, :first, :PAIR] = jnp.zeros((first, PAIR), jnp.bfloat16)
    out_ref[0, :, PAIR : 2 * PAIR] = gk_sum[...].astype(jnp.bfloat16)
    out_ref[0, :, 2 * PAIR :] = gv_sum[...].astype(jnp.bfloat16)


def attention_backward(packed, mixed, grads, log_total, low_pos):
    groups, key_len, width = packed.shape
    block_len = mixed.shape[1]
    pairs = width // (3 * PAIR)
    pick = lambda seq, pair: (seq, 0, pair)
    row_spec = pl.BlockSpec((1, block_len, PAIR), pick)
    packed_spec = pl.BlockSpec((1, key_len, 3 * PAIR), pick)
    return pl.pallas_call(
        backward_kernel,
        grid=(groups, pairs),
        in_specs=[
            packed_spec, row_spec, row_spec,
            pl.BlockSpec((1, 1, 2, block_len), lambda seq, pair: (seq, pair, 0, 0)),
            pl.BlockSpec((1, 1, block_len), lambda seq, pair: (seq, 0, 0)),
        ],
        out_specs=packed_spec,
        out_shape=jax.ShapeDtypeStruct(packed.shape, jnp.bfloat16),
        scratch_shapes=[
            pltpu.VMEM((key_len, PAIR), jnp.float32),
            pltpu.VMEM((key_len, PAIR), jnp.float32),
        ],
        compiler_params=pltpu.CompilerParams(vmem_limit_bytes=56 << 20),
        cost_estimate=pl.CostEstimate(
            flops=block_len,
            bytes_accessed=block_len,
            transcendentals=0,
        ),
    )(packed, mixed, grads, log_total, low_pos[:, None, :])


norm_eps = 1e-05


def mate(value):
    return lax.ppermute(value, "core", [(0, 1), (1, 0)])


def other_tp(value):
    return lax.ppermute(value, "tp", [(0, 1), (1, 0)])


def onward(value):
    count = lax.axis_size("ctx")
    return lax.ppermute(value, "ctx", [(i, i + 1) for i in range(count - 1)])


def backward_step(value):
    count = lax.axis_size("ctx")
    return lax.ppermute(value, "ctx", [(i + 1, i) for i in range(count - 1)])


class Place:
    def __init__(self):
        self.chips = lax.axis_size("x")
        self.core = lax.axis_index("core")
        self.shard = lax.axis_index("x") * 2 + self.core
        self.tp = lax.axis_index("tp")
        self.ctx = lax.axis_index("ctx")
        self.home = self.core == self.tp


def tie(*values):
    return lax.optimization_barrier(values)


def ordered(own, other, position, axis=0):
    return jnp.where(
        position == 0,
        jnp.stack([own, other], axis=axis),
        jnp.stack([other, own], axis=axis),
    )


def join_kernel(core_ref, *refs):
    out_ref = refs[-1]
    own = pl.program_id(1) == core_ref[0]
    at = 0
    for blocks_ref, came_ref in zip(refs[0:-1:2], refs[1:-1:2]):
        width = came_ref.shape[2]

        @pl.when(own)
        def _(at=at, width=width, blocks_ref=blocks_ref):
            out_ref[:, at : at + width] = blocks_ref[0, 0]

        @pl.when(jnp.logical_not(own))
        def _(at=at, width=width, came_ref=came_ref):
            out_ref[:, at : at + width] = came_ref[0]

        at += width


class CoreSwap:
    def __init__(self, blocks, place, column=0, width=None):
        self.place, self.blocks, self.column = place, blocks, column
        width = blocks.shape[3] if width is None else width
        other = lax.dynamic_index_in_dim(blocks, 1 - place.core, 1, False)
        self.came = mate(other[..., column * width : (column + 1) * width])


def join(*swaps):
    chips, rows = swaps[0].came.shape[:2]
    in_specs, operands, total = [], [], 0
    for swap in swaps:
        width = swap.came.shape[2]
        in_specs += [
            pl.BlockSpec(
                (1, 1, rows, width),
                lambda chip, part, core, column=swap.column: (chip, core[0], 0, column),
            ),
            pl.BlockSpec((1, rows, width), lambda chip, part, core: (chip, 0, 0)),
        ]
        operands += [swap.blocks, swap.came]
        total += width
    return pl.pallas_call(
        join_kernel,
        grid_spec=pltpu.PrefetchScalarGridSpec(
            num_scalar_prefetch=1,
            grid=(chips, 2),
            in_specs=in_specs,
            out_specs=pl.BlockSpec((rows, total), lambda chip, part, core: (chip * 2 + part, 0)),
        ),
        out_shape=jax.ShapeDtypeStruct((chips * 2 * rows, total), jnp.bfloat16),
        compiler_params=pltpu.CompilerParams(vmem_limit_bytes=24 << 20),
        cost_estimate=pl.CostEstimate(
            flops=rows, bytes_accessed=rows, transcendentals=0
        ),
    )(swaps[0].place.core.reshape(1).astype(jnp.int32), *operands)


def gather_blocks(piece, place):
    whole = lax.all_gather(piece, ("x", "tp"), axis=0, tiled=False)
    return whole.reshape((place.chips, 2) + piece.shape)


def scatter_swap(grads, place):
    return CoreSwap(grads.reshape(place.chips, 2, -1, grads.shape[1]), place)


def scatter_sum(blocks):
    return lax.psum_scatter(blocks, ("x", "tp"), scatter_dimension=0, tiled=True)


def dot_f32(left_side, right_side):
    return jnp.dot(left_side, right_side, preferred_element_type=jnp.float32)


def dot_first(left_side, right_side):
    return contract(left_side, right_side, 0, 0)


def dot_second(left_side, right_side):
    return contract(left_side, right_side, 1, 1)


def gather_small(value, place):
    if place.chips != 2:
        return lax.all_gather(value, ("x", "core"), axis=1, tiled=True)
    near = mate(value)
    pair = ordered(value, near, place.core, 1).reshape(value.shape[0], -1)
    far = lax.ppermute(pair, "x", [(0, 1), (1, 0)])
    return ordered(pair, far, lax.axis_index("x"), 1).reshape(value.shape[0], -1)


def norm_forward(hidden, norm_gain, norm_shift):
    row_mean = jnp.mean(hidden, axis=-1, keepdims=True)
    centred = hidden - row_mean
    variance = jnp.mean(centred * centred, axis=-1, keepdims=True)
    inv_std = lax.rsqrt(variance + norm_eps)
    norm_hat = centred * inv_std
    return ((norm_hat * norm_gain + norm_shift).astype(jnp.bfloat16), norm_hat, inv_std)


def norm_backward(grad_out, norm_hat, inv_std, norm_gain):
    scaled = grad_out * norm_gain
    mean_one = jnp.mean(scaled, axis=-1, keepdims=True)
    mean_two = jnp.mean(scaled * norm_hat, axis=-1, keepdims=True)
    grad_input = inv_std * (scaled - mean_one - norm_hat * mean_two)
    return (grad_input, jnp.sum(grad_out * norm_hat, axis=0), jnp.sum(grad_out, axis=0))


def wide(value):
    return value.astype(jnp.float32)


def narrow(value):
    return value.astype(jnp.bfloat16)


def pick_block(value, index, count):
    size = value.shape[0] // count
    return lax.dynamic_slice_in_dim(value, index * size, size, 0)


def small_total(value, place):
    if place.chips != 2 or lax.axis_size("ctx") != 4:
        return lax.psum(value, ("x", "core", "ctx", "tp"))
    value = value + mate(value)
    value = value + other_tp(value)
    value = value + lax.ppermute(value, "x", [(0, 1), (1, 0)])
    value = value + lax.ppermute(value, "ctx", [(0, 1), (3, 2)])
    value = value + lax.ppermute(value, "ctx", [(1, 2), (2, 1)])
    outer = (place.ctx == 0) | (place.ctx == 3)
    return jnp.where(outer, lax.ppermute(value, "ctx", [(1, 0), (2, 3)]), value)


def core_sum(own_part, mate_part):
    return own_part + wide(mate(narrow(mate_part)))


def gelu_slope(pre_act, grad_act):
    pullback = jax.vjp(lambda values: jax.nn.gelu(values, approximate=True), pre_act)[1]
    return pullback(grad_act)[0]


def pair_major(value):
    width = value.shape[-1]
    return jnp.concatenate(
        [value[kind, :, at : at + PAIR] for at in range(0, width, PAIR) for kind in range(3)],
        axis=-1,
    )


def pack_kernel(qkv_ref, proj_ref, out_ref):
    width = qkv_ref.shape[3]
    for pair in range(width // PAIR):
        for kind in range(3):
            at = (3 * pair + kind) * PAIR
            out_ref[:, at : at + PAIR] = qkv_ref[0, kind, :, pair * PAIR : (pair + 1) * PAIR]
    out_ref[:, 3 * width :] = jnp.transpose(proj_ref[0])


def attn_piece(layer, qkv_weight, proj_weight):
    rows, width = qkv_weight.shape[2:]
    return pl.pallas_call(
        pack_kernel,
        grid=(1,),
        in_specs=[
            pl.BlockSpec((1, 3, rows, width), lambda step: (layer, 0, 0, 0)),
            pl.BlockSpec((1, width, rows), lambda step: (layer, 0, 0)),
        ],
        out_specs=pl.BlockSpec((rows, 4 * width), lambda step: (0, 0)),
        out_shape=jax.ShapeDtypeStruct((rows, 4 * width), jnp.bfloat16),
        compiler_params=pltpu.CompilerParams(vmem_limit_bytes=24 << 20),
    )(qkv_weight, proj_weight)


def unpack_kernel(first_ref, second_ref, out_ref):
    kind = pl.program_id(0)
    width = out_ref.shape[3]
    for pair in range(width // PAIR):
        at = pl.multiple_of((3 * pair + kind) * PAIR, PAIR)
        for layer, ref in enumerate((first_ref, second_ref)):
            out_ref[layer, 0, :, pair * PAIR : (pair + 1) * PAIR] = ref[
                :, pl.ds(at, PAIR)
            ].astype(jnp.float32)


def unpack_heads(first, second):
    rows, width = first.shape
    width = width // 3
    block = pl.BlockSpec((rows, 3 * width), lambda kind: (0, 0))
    return pl.pallas_call(
        unpack_kernel,
        grid=(3,),
        in_specs=[block, block],
        out_specs=pl.BlockSpec((2, 1, rows, width), lambda kind: (0, kind, 0, 0)),
        out_shape=jax.ShapeDtypeStruct((2, 3, rows, width), jnp.float32),
        compiler_params=pltpu.CompilerParams(vmem_limit_bytes=24 << 20),
    )(first, second)


def per_device(
    tokens,
    cotangent,
    doc_lengths,
    norm_gains,
    norm_biases,
    qkv_weight,
    qv_bias,
    proj_weight,
    fc_weight,
    fc_bias,
    out_weight,
):
    place = Place()
    block_len, model_width = tokens.shape[1:]
    shard_rows = qkv_weight.shape[2]
    half_width = qkv_weight.shape[3]
    layer_count = qkv_weight.shape[0]
    reach = WINDOW // block_len
    key_len = (reach + 1) * block_len
    last = reach * block_len

    def my_seq(value):
        return lax.dynamic_index_in_dim(value, place.tp, 0, False)

    def both_seqs(own, other):
        return ordered(own, other, place.tp)

    own_tokens = my_seq(tokens)
    grad_hidden = wide(my_seq(cotangent))
    bias_parts = jnp.sum(grad_hidden.reshape(16, -1, model_width), axis=1)
    bias_parts = lax.psum(bias_parts, "ctx")
    attn_blocks = gather_blocks(attn_piece(0, qkv_weight, proj_weight), place)
    halo = [onward(own_tokens)]
    for _ in range(reach - 1):
        halo.insert(0, onward(halo[0]))
    vectors = jnp.concatenate([norm_gains, norm_biases], axis=1)
    vectors = gather_small(vectors.reshape(-1, vectors.shape[2]), place)
    vectors = wide(vectors).reshape(layer_count, 6, model_width)
    biases = jnp.concatenate([qv_bias.reshape(layer_count, -1), fc_bias], axis=1)
    biases = wide(jnp.where(place.home, biases, other_tp(biases)))
    lengths = my_seq(doc_lengths)
    lengths = jnp.stack([lengths, mate(lengths)])
    mlp_piece, mlp_later = [
        jnp.concatenate([fc_weight[layer], jnp.transpose(out_weight[layer])], axis=1)
        for layer in range(layer_count)
    ]
    attn_later = attn_piece(1, qkv_weight, proj_weight)
    halo[-1], mlp_piece, mlp_later, attn_later = tie(
        halo[-1], mlp_piece, mlp_later, attn_later
    )
    mlp_blocks = gather_blocks(mlp_piece, place)
    fc_width = fc_weight.shape[2]

    doc_ends = jnp.cumsum(lengths, axis=1)
    first_pos = place.ctx * block_len
    query_pos = first_pos + jnp.arange(block_len, dtype=jnp.int32)
    started = doc_ends[:, None, :] <= query_pos[None, :, None]
    doc_start = jnp.max(jnp.where(started, doc_ends[:, None, :], 0), axis=-1)
    low_pos = jnp.maximum(doc_start, query_pos[None, :] - (WINDOW - 1))
    low_pos = (low_pos - first_pos + last).astype(jnp.int32)

    hidden = wide(own_tokens)
    stash = []
    weights = []
    for layer in range(layer_count):
        gains, shifts = vectors[layer, :2], vectors[layer, 2:]
        bias_q, bias_v = biases[layer, :half_width], biases[layer, half_width : 2 * half_width]
        bias_qkv = pair_major(jnp.stack([bias_q, jnp.zeros_like(bias_q), bias_v])[:, None])
        bias_fc = biases[layer, 2 * half_width :]
        attn_in, hat_attn, inv_attn = norm_forward(hidden, gains[0], shifts[0])
        own_near = [attn_in]
        mate_near = [mate(attn_in)]
        attn_swap = CoreSwap(attn_blocks, place)
        if layer == 0:
            w_attn = join(attn_swap)
        step_value = attn_in
        for index in range(reach):
            if layer == 0:
                part = norm_forward(wide(halo[reach - 1 - index]), gains[0], shifts[0])[0]
            else:
                step_value = part = onward(step_value)
                if index == 0:
                    step_value, mlp_later = tie(step_value, mlp_later)
                    mlp_blocks = gather_blocks(mlp_later, place)
                    part = step_value
                if index == 1:
                    step_value, w_attn = tie(step_value, join(attn_swap))
                    part = step_value
            own_near.insert(0, part)
            mate_near.insert(0, mate(part))
        near = jnp.concatenate(own_near + mate_near)
        if layer == 0:
            near, bias_parts = tie(near, bias_parts)
        w_qkv, w_proj_t = w_attn[:, : 3 * half_width], w_attn[:, 3 * half_width :]
        packed = narrow(dot_f32(near, w_qkv) + bias_qkv).reshape(2, key_len, -1)
        mixed, log_total = attention_forward(packed, low_pos)
        if layer + 1 < layer_count:
            mixed, attn_later = tie(mixed, attn_later)
            attn_blocks = gather_blocks(attn_later, place)
        mate_part = dot_second(mixed[1], w_proj_t)
        own_part = dot_second(mixed[0], w_proj_t)
        middle = hidden + core_sum(own_part, mate_part) + shifts[1]
        mlp_own, hat_mlp, inv_mlp = norm_forward(middle, gains[1], shifts[2])
        mlp_in = jnp.concatenate([mlp_own, mate(mlp_own)])
        mlp_in, mlp_blocks = tie(mlp_in, mlp_blocks)
        w_fc = join(CoreSwap(mlp_blocks, place, 0, fc_width))
        out_swap = CoreSwap(mlp_blocks, place, 1, fc_width)
        pre_act = dot_f32(mlp_in, w_fc) + bias_fc
        activated = narrow(jax.nn.gelu(pre_act, approximate=True))
        w_out_t = join(out_swap)
        mate_part = dot_second(activated[block_len:], w_out_t)
        own_part = dot_second(activated[:block_len], w_out_t)
        hidden = middle + core_sum(own_part, mate_part) + shifts[3]
        weights.append((w_qkv, w_proj_t, w_fc, w_out_t))
        stash.append(
            (near, hat_attn, inv_attn, packed, mixed, log_total, hat_mlp, inv_mlp, mlp_in,
             pre_act, activated)
        )

    own_output = narrow(hidden)
    last_sum = None
    sums = {}
    waiting, latest, first_sum = [], [], []
    small_parts = [None] * layer_count

    def advance(value, name):
        nonlocal last_sum
        share = waiting.pop(0)
        assert share[0] == name
        value, share, last_sum = tie(value, share[1], last_sum)
        if latest:
            sums[latest[0]] = last_sum
        else:
            first_sum.append(last_sum)
        latest[:] = [name]
        last_sum = lax.psum(share, "ctx")
        sums[name] = last_sum
        return value

    def settle(value, name):
        assert waiting[0][0] == name
        value, share = tie(value, waiting[0][1])
        waiting[0] = (name, share)
        return value

    for layer in reversed(range(layer_count)):
        near, hat_attn, inv_attn, packed, mixed, log_total = stash[layer][:6]
        hat_mlp, inv_mlp, mlp_in, pre_act, activated = stash[layer][6:]
        gains = vectors[layer, :2]
        w_qkv, w_proj_t, w_fc, w_out_t = weights[layer]
        final = layer == 0
        grad_out_bias = jnp.sum(grad_hidden, axis=0)
        if not final:
            last_sum = bias_parts
        grad_low = narrow(grad_hidden)
        grad_low = jnp.concatenate([grad_low, mate(grad_low)])
        out_swap = scatter_swap(narrow(dot_first(grad_low, activated)), place)
        grad_pre = narrow(gelu_slope(pre_act, dot_f32(grad_low, w_out_t)))
        if not final:
            grad_pre, out_swap.came = tie(grad_pre, out_swap.came)
            waiting.append(("out%d" % layer, scatter_sum(join(out_swap))))
        grad_fc_bias = jnp.sum(wide(grad_pre), axis=0)
        mate_part = dot_second(grad_pre[block_len:], w_fc)
        own_part = dot_second(grad_pre[:block_len], w_fc)
        grad_norm_in = core_sum(own_part, mate_part)
        if final:
            grad_norm_in, grad_out = tie(grad_norm_in, join(out_swap))
            (grad_norm_in, grad_out) = settle((grad_norm_in, grad_out), "attn1")
            attn_share = waiting.pop(0)[1]
            waiting.append(("out%d" % layer, scatter_sum(grad_out)))
        fc_swap = scatter_swap(narrow(dot_first(mlp_in, grad_pre)), place)
        grad_from_mlp, grad_gain_mlp, grad_shift_mlp = norm_backward(
            grad_norm_in, hat_mlp, inv_mlp, gains[1]
        )
        grad_middle = grad_hidden + grad_from_mlp
        grad_proj_bias = jnp.sum(grad_middle, axis=0)
        grad_low = narrow(grad_middle)
        grad_low = jnp.concatenate([grad_low, mate(grad_low)])
        grad_mixed = narrow(dot_f32(grad_low, w_proj_t)).reshape(mixed.shape)
        proj_swap = scatter_swap(
            narrow(dot_first(grad_low, mixed.reshape(2 * block_len, half_width))), place
        )
        grad_mixed, fc_swap.came, proj_swap.came = tie(grad_mixed, fc_swap.came, proj_swap.came)
        grad_mixed, grad_fc = tie(grad_mixed, join(fc_swap, proj_swap))
        if final:
            share = jnp.concatenate([early_share, attn_share], axis=1)
            waiting.insert(0, ("first", share))
            grad_mixed = advance(grad_mixed, "first")
        grad_packed = attention_backward(packed, mixed, grad_mixed, log_total, low_pos)
        if final:
            grad_packed, far_output, grad_fc = tie(grad_packed, far_output, grad_fc)
            grad_packed, grad_fc = settle((grad_packed, grad_fc), "out%d" % layer)
        else:
            grad_packed, grad_fc = tie(grad_packed, grad_fc)
            grad_packed = advance(grad_packed, "out%d" % layer)
        waiting.append(("fc%d" % layer, scatter_sum(grad_fc)))
        mate_part = dot_second(grad_packed[1], w_qkv)
        own_part = dot_second(grad_packed[0], w_qkv)
        grad_near = core_sum(own_part, mate_part)
        far_total, grad_attn_in = grad_near[:last], grad_near[last:]
        rows = grad_packed.reshape(2 * key_len, -1)
        grad_near, rows = tie(grad_near, rows)
        far_total, grad_attn_in = grad_near[:last], grad_near[last:]
        carried = backward_step(narrow(far_total[:block_len]))
        grad_qkv = narrow(dot_first(near, rows))
        grad_bias = jnp.sum(wide(rows), axis=0)
        if final:
            attn_swap = scatter_swap(grad_qkv, place)
        for step in range(1, reach + 1):
            if step == 1 and not final:
                carried, grad_qkv, last_sum = tie(carried, grad_qkv, last_sum)
                attn_swap = scatter_swap(grad_qkv, place)
            if step == 1 and final:
                carried, grad_attn = tie(carried, join(attn_swap))
                carried = advance(carried, "out%d" % layer)
                carried, grad_attn = settle((carried, grad_attn), "fc%d" % layer)
                waiting.append(("attn%d" % layer, scatter_sum(grad_attn)))
            if step == 2 and not final:
                carried, grad_bias, grad_attn, own_output = tie(
                    carried, grad_bias, join(attn_swap), own_output
                )
                far_output = other_tp(own_output)
                carried, grad_attn = settle((carried, grad_attn), "fc%d" % layer)
                early_share = waiting.pop(0)[1]
                waiting.append(("attn%d" % layer, scatter_sum(grad_attn)))
            if step == 2 and final:
                carried, grad_bias, waiting[1] = tie(carried, grad_bias, waiting[1][1])
                waiting[1] = ("attn%d" % layer, waiting[1])
                carried = settle(carried, "fc%d" % layer)
                share = jnp.concatenate([waiting[0][1], waiting[1][1]], axis=1)
                waiting[:] = [("last", share)]
                carried = advance(carried, "last")
            arrived = wide(carried)
            if step < reach:
                section = far_total[step * block_len : (step + 1) * block_len]
                carried = backward_step(narrow(arrived + section))
            else:
                grad_attn_in = grad_attn_in + arrived
        grad_from_attn, grad_gain_attn, grad_shift_attn = norm_backward(
            grad_attn_in, hat_attn, inv_attn, gains[0]
        )
        grad_hidden = grad_middle + grad_from_attn
        grad_bias = grad_bias.reshape(-1, 3, PAIR)
        halves = jnp.concatenate(
            [grad_bias[:, 0].reshape(-1), grad_bias[:, 2].reshape(-1), grad_fc_bias]
        )
        empty = jnp.zeros_like(halves)
        if not final:
            grad_out_bias = jnp.where(place.ctx == 0, jnp.sum(first_sum[0], axis=0), 0.0)
        small_parts[layer] = jnp.concatenate(
            [
                grad_gain_attn, grad_gain_mlp,
                grad_shift_attn, grad_proj_bias, grad_shift_mlp, grad_out_bias,
                jnp.where(place.core == 0, halves, empty),
                jnp.where(place.core == 1, halves, empty),
            ]
        )

    small = small_total(jnp.stack(small_parts), place)
    far_grad = wide(other_tp(narrow(grad_hidden)))
    token_grad = both_seqs(grad_hidden, far_grad)
    split = 6 * model_width
    norms = small[:, :split].reshape(layer_count, 6, model_width)
    norms = lax.dynamic_slice_in_dim(norms, place.shard * shard_rows, shard_rows, 2)
    halves = small[:, split:].reshape(layer_count, 2, -1)
    halves = lax.dynamic_index_in_dim(halves, place.tp, 1, False)
    split = fc_width + half_width
    attn = [sums[name][:, split:] for name in ("last", "first")]
    fc_proj = [sums[name][:, :split] for name in ("last", "first")]
    return (
        both_seqs(own_output, far_output),
        token_grad,
        norms[:, :2],
        norms[:, 2:],
        unpack_heads(*attn),
        halves[:, : 2 * half_width].reshape(layer_count, 2, half_width),
        jnp.stack([jnp.transpose(wide(v[:, fc_width:])) for v in fc_proj]),
        jnp.stack([wide(v[:, :fc_width]) for v in fc_proj]),
        halves[:, 2 * half_width :],
        jnp.stack([jnp.transpose(wide(sums["out%d" % layer])) for layer in range(layer_count)]),
    )


def solution(mesh):
    devices = mesh.devices
    devices = devices.reshape((devices.shape[0] // 2, 2) + devices.shape[1:])
    mesh = jax.sharding.Mesh(devices, ("x", "core", "ctx", "tp"))
    placed = (
        P(("x", "core"), "ctx", None),
        P(("x", "core"), "ctx", None),
        P(("x", "core"), None),
        P(None, None, ("x", "core")),
        P(None, None, ("x", "core")),
        P(None, None, ("x", "core"), "tp"),
        P(None, None, "tp"),
        P(None, "tp", ("x", "core")),
        P(None, ("x", "core"), "tp"),
        P(None, "tp"),
        P(None, "tp", ("x", "core")),
    )
    return jax.shard_map(
        per_device,
        mesh=mesh,
        in_specs=placed,
        out_specs=(
            P(("x", "core"), "ctx", None),
            P(("x", "core"), "ctx", None),
            P(None, None, ("x", "core")),
            P(None, None, ("x", "core")),
            P(None, None, ("x", "core"), "tp"),
            P(None, None, "tp"),
            P(None, "tp", ("x", "core")),
            P(None, ("x", "core"), "tp"),
            P(None, "tp"),
            P(None, "tp", ("x", "core")),
        ),
        check_vma=False,
    )
```

```python
import jax
import jax.numpy as jnp
from jax import lax
from jax.experimental import pallas as pl
from jax.experimental.pallas import tpu as pltpu
from jax.sharding import PartitionSpec as P

HD = 64
WINDOW = 1024
TILE = 256
masked_score = -1e30


def contract(left_side, right_side, left_dim, right_dim):
    return lax.dot_general(
        left_side, right_side, (((left_dim,), (right_dim,)), ((), ())),
        preferred_element_type=jnp.float32,
    )


def half_mask(shape, half):
    lane = lax.broadcasted_iota(jnp.int32, shape, 1)
    return (lane < HD) if half == 0 else (lane >= HD)


PAIR = 2 * HD


def forward_kernel(qkv_ref, low_ref, mixed_ref, total_ref):
    block_len = mixed_ref.shape[1]
    first = qkv_ref.shape[1] - block_len
    span = WINDOW + TILE
    eye = lax.broadcasted_iota(jnp.int32, (TILE, TILE), 0) == lax.broadcasted_iota(
        jnp.int32, (TILE, TILE), 1
    )
    for block in range(block_len // TILE):
        rows = pl.ds(block * TILE, TILE)
        window = pl.ds(block * TILE, span)
        queries = qkv_ref[0, pl.ds(first + block * TILE, TILE), :PAIR]
        queries = queries * jnp.asarray(HD ** (-0.5), jnp.bfloat16)
        keys = qkv_ref[0, window, PAIR : 2 * PAIR]
        values = qkv_ref[0, window, 2 * PAIR :]
        low_pos = low_ref[0, rows, :] - block * TILE
        key_pos = lax.broadcasted_iota(jnp.int32, (TILE, span), 1)
        query_pos = lax.broadcasted_iota(jnp.int32, (TILE, TILE), 0) + WINDOW
        allowed = key_pos >= low_pos
        causal = key_pos[:, WINDOW:] <= query_pos
        mixed = jnp.zeros((TILE, 2 * HD), jnp.float32)
        for half in range(2):
            scores = contract(
                jnp.where(half_mask(queries.shape, half), queries, 0), keys, 1, 1
            )
            early = jnp.where(allowed[:, :WINDOW], scores[:, :WINDOW], masked_score)
            late = jnp.where(allowed[:, WINDOW:] & causal, scores[:, WINDOW:], masked_score)
            top_score = jnp.maximum(
                jnp.max(early, axis=1, keepdims=True), jnp.max(late, axis=1, keepdims=True)
            )
            early = jnp.exp(early - top_score)
            late = jnp.exp(late - top_score)
            row_total = jnp.sum(early, axis=1, keepdims=True) + jnp.sum(
                late, axis=1, keepdims=True
            )
            part = contract(early.astype(jnp.bfloat16), values[:WINDOW], 1, 0) + contract(
                late.astype(jnp.bfloat16), values[WINDOW:], 1, 0
            )
            part = part * (1.0 / row_total)
            mixed = jnp.where(half_mask(mixed.shape, half), part, mixed)
            log_total = top_score + jnp.log(row_total)
            total_ref[0, 0, half : half + 1, rows] = jnp.sum(
                jnp.where(eye, log_total, 0.0), axis=0, keepdims=True
            )
        mixed_ref[0, rows, :] = mixed.astype(jnp.bfloat16)


def attention_forward(packed, low_pos):
    groups, key_len, width = packed.shape
    block_len = low_pos.shape[1]
    pairs = width // (3 * PAIR)
    pick = lambda seq, pair: (seq, 0, pair)
    return pl.pallas_call(
        forward_kernel,
        grid=(groups, pairs),
        in_specs=[
            pl.BlockSpec((1, key_len, 3 * PAIR), pick),
            pl.BlockSpec((1, block_len, 1), lambda seq, pair: (seq, 0, 0)),
        ],
        out_specs=[
            pl.BlockSpec((1, block_len, PAIR), pick),
            pl.BlockSpec((1, 1, 2, block_len), lambda seq, pair: (seq, pair, 0, 0)),
        ],
        out_shape=[
            jax.ShapeDtypeStruct((groups, block_len, pairs * PAIR), jnp.bfloat16),
            jax.ShapeDtypeStruct((groups, pairs, 2, block_len), jnp.float32),
        ],
        compiler_params=pltpu.CompilerParams(vmem_limit_bytes=56 << 20),
        cost_estimate=pl.CostEstimate(
            flops=block_len,
            bytes_accessed=block_len,
            transcendentals=0,
        ),
    )(packed, low_pos[:, :, None])


def backward_kernel(qkv_ref, mixed_ref, grad_ref, total_ref, low_ref, out_ref, gk_sum, gv_sum):
    block_len = mixed_ref.shape[1]
    first = qkv_ref.shape[1] - block_len
    span = WINDOW + TILE
    scale = HD ** (-0.5)
    gk_sum[...] = jnp.zeros_like(gk_sum)
    gv_sum[...] = jnp.zeros_like(gv_sum)
    eye = lax.broadcasted_iota(jnp.int32, (TILE, TILE), 0) == lax.broadcasted_iota(
        jnp.int32, (TILE, TILE), 1
    )
    for block in range(block_len // TILE):
        rows = pl.ds(block * TILE, TILE)
        window = pl.ds(block * TILE, span)
        queries = qkv_ref[0, pl.ds(first + block * TILE, TILE), :PAIR]
        queries = queries * jnp.asarray(scale, jnp.bfloat16)
        keys = qkv_ref[0, window, PAIR : 2 * PAIR]
        values = qkv_ref[0, window, 2 * PAIR :]
        grads = grad_ref[0, rows, :]
        product = grads.astype(jnp.float32) * mixed_ref[0, rows, :].astype(jnp.float32)
        low_pos = low_ref[0, :, rows] - block * TILE
        key_pos = lax.broadcasted_iota(jnp.int32, (span, TILE), 0)
        query_pos = lax.broadcasted_iota(jnp.int32, (TILE, TILE), 1) + WINDOW
        allowed = key_pos >= low_pos
        late_allowed = allowed[WINDOW:] & (key_pos[WINDOW:] <= query_pos)
        keys_t = jnp.transpose(keys)
        gq_parts = []
        for half in range(2):
            mask = half_mask(queries.shape, half)
            q_half = jnp.where(mask, queries, 0)
            g_half = jnp.where(mask, grads, 0)
            delta = jnp.sum(jnp.where(mask, product, 0.0), axis=1, keepdims=True)
            delta = jnp.sum(jnp.where(eye, delta, 0.0), axis=0, keepdims=True)
            log_total = total_ref[0, 0, half : half + 1, rows]
            scores = contract(keys, q_half, 1, 1)
            probs = jnp.concatenate(
                [
                    jnp.where(allowed[:WINDOW], jnp.exp(scores[:WINDOW] - log_total), 0.0),
                    jnp.where(late_allowed, jnp.exp(scores[WINDOW:] - log_total), 0.0),
                ]
            )
            grad_probs = contract(values, g_half, 1, 1)
            grad_scores = (probs * (grad_probs - delta)).astype(jnp.bfloat16)
            gv_sum[window, :] += contract(probs.astype(jnp.bfloat16), g_half, 1, 0)
            gk_sum[window, :] += contract(grad_scores, q_half, 1, 0)
            gq_parts.append(contract(keys_t[half * HD : (half + 1) * HD], grad_scores, 1, 0))
        gq = jnp.transpose(jnp.concatenate(gq_parts)) * scale
        out_ref[0, pl.ds(first + block * TILE, TILE), :PAIR] = gq.astype(jnp.bfloat16)
    out_ref[0, :first, :PAIR] = jnp.zeros((first, PAIR), jnp.bfloat16)
    out_ref[0, :, PAIR : 2 * PAIR] = gk_sum[...].astype(jnp.bfloat16)
    out_ref[0, :, 2 * PAIR :] = gv_sum[...].astype(jnp.bfloat16)


def attention_backward(packed, mixed, grads, log_total, low_pos):
    groups, key_len, width = packed.shape
    block_len = mixed.shape[1]
    pairs = width // (3 * PAIR)
    pick = lambda seq, pair: (seq, 0, pair)
    row_spec = pl.BlockSpec((1, block_len, PAIR), pick)
    packed_spec = pl.BlockSpec((1, key_len, 3 * PAIR), pick)
    return pl.pallas_call(
        backward_kernel,
        grid=(groups, pairs),
        in_specs=[
            packed_spec, row_spec, row_spec,
            pl.BlockSpec((1, 1, 2, block_len), lambda seq, pair: (seq, pair, 0, 0)),
            pl.BlockSpec((1, 1, block_len), lambda seq, pair: (seq, 0, 0)),
        ],
        out_specs=packed_spec,
        out_shape=jax.ShapeDtypeStruct(packed.shape, jnp.bfloat16),
        scratch_shapes=[
            pltpu.VMEM((key_len, PAIR), jnp.float32),
            pltpu.VMEM((key_len, PAIR), jnp.float32),
        ],
        compiler_params=pltpu.CompilerParams(vmem_limit_bytes=56 << 20),
        cost_estimate=pl.CostEstimate(
            flops=block_len,
            bytes_accessed=block_len,
            transcendentals=0,
        ),
    )(packed, mixed, grads, log_total, low_pos[:, None, :])


norm_eps = 1e-05


def mate(value):
    return lax.ppermute(value, "core", [(0, 1), (1, 0)])


def other_tp(value):
    return lax.ppermute(value, "tp", [(0, 1), (1, 0)])


def onward(value):
    count = lax.axis_size("ctx")
    return lax.ppermute(value, "ctx", [(i, i + 1) for i in range(count - 1)])


def backward_step(value):
    count = lax.axis_size("ctx")
    return lax.ppermute(value, "ctx", [(i + 1, i) for i in range(count - 1)])


class Place:
    def __init__(self):
        self.chips = lax.axis_size("x")
        self.core = lax.axis_index("core")
        self.shard = lax.axis_index("x") * 2 + self.core
        self.tp = lax.axis_index("tp")
        self.ctx = lax.axis_index("ctx")
        self.home = self.core == self.tp


def tie(*values):
    return lax.optimization_barrier(values)


def ordered(own, other, position, axis=0):
    return jnp.where(
        position == 0,
        jnp.stack([own, other], axis=axis),
        jnp.stack([other, own], axis=axis),
    )


def join_kernel(core_ref, *refs):
    out_ref = refs[-1]
    own = pl.program_id(1) == core_ref[0]
    at = 0
    for blocks_ref, came_ref in zip(refs[0:-1:2], refs[1:-1:2]):
        width = came_ref.shape[2]

        @pl.when(own)
        def _(at=at, width=width, blocks_ref=blocks_ref):
            out_ref[:, at : at + width] = blocks_ref[0, 0]

        @pl.when(jnp.logical_not(own))
        def _(at=at, width=width, came_ref=came_ref):
            out_ref[:, at : at + width] = came_ref[0]

        at += width


class CoreSwap:
    def __init__(self, blocks, place, column=0, width=None):
        self.place, self.blocks, self.column = place, blocks, column
        width = blocks.shape[3] if width is None else width
        other = lax.dynamic_index_in_dim(blocks, 1 - place.core, 1, False)
        self.came = mate(other[..., column * width : (column + 1) * width])


def join(*swaps):
    chips, rows = swaps[0].came.shape[:2]
    in_specs, operands, total = [], [], 0
    for swap in swaps:
        width = swap.came.shape[2]
        in_specs += [
            pl.BlockSpec(
                (1, 1, rows, width),
                lambda chip, part, core, column=swap.column: (chip, core[0], 0, column),
            ),
            pl.BlockSpec((1, rows, width), lambda chip, part, core: (chip, 0, 0)),
        ]
        operands += [swap.blocks, swap.came]
        total += width
    return pl.pallas_call(
        join_kernel,
        grid_spec=pltpu.PrefetchScalarGridSpec(
            num_scalar_prefetch=1,
            grid=(chips, 2),
            in_specs=in_specs,
            out_specs=pl.BlockSpec((rows, total), lambda chip, part, core: (chip * 2 + part, 0)),
        ),
        out_shape=jax.ShapeDtypeStruct((chips * 2 * rows, total), jnp.bfloat16),
        compiler_params=pltpu.CompilerParams(vmem_limit_bytes=24 << 20),
        cost_estimate=pl.CostEstimate(
            flops=rows, bytes_accessed=rows, transcendentals=0
        ),
    )(swaps[0].place.core.reshape(1).astype(jnp.int32), *operands)


def gather_blocks(piece, place):
    whole = lax.all_gather(piece, ("x", "tp"), axis=0, tiled=False)
    return whole.reshape((place.chips, 2) + piece.shape)


def scatter_swap(grads, place):
    return CoreSwap(grads.reshape(place.chips, 2, -1, grads.shape[1]), place)


def scatter_sum(blocks):
    return lax.psum_scatter(blocks, ("x", "tp"), scatter_dimension=0, tiled=True)


def dot_f32(left_side, right_side):
    return jnp.dot(left_side, right_side, preferred_element_type=jnp.float32)


def dot_first(left_side, right_side):
    return contract(left_side, right_side, 0, 0)


def dot_second(left_side, right_side):
    return contract(left_side, right_side, 1, 1)


def gather_small(value, place):
    if place.chips != 2:
        return lax.all_gather(value, ("x", "core"), axis=1, tiled=True)
    near = mate(value)
    pair = ordered(value, near, place.core, 1).reshape(value.shape[0], -1)
    far = lax.ppermute(pair, "x", [(0, 1), (1, 0)])
    return ordered(pair, far, lax.axis_index("x"), 1).reshape(value.shape[0], -1)


def norm_forward(hidden, norm_gain, norm_shift):
    row_mean = jnp.mean(hidden, axis=-1, keepdims=True)
    centred = hidden - row_mean
    variance = jnp.mean(centred * centred, axis=-1, keepdims=True)
    inv_std = lax.rsqrt(variance + norm_eps)
    norm_hat = centred * inv_std
    return ((norm_hat * norm_gain + norm_shift).astype(jnp.bfloat16), norm_hat, inv_std)


def norm_backward(grad_out, norm_hat, inv_std, norm_gain):
    scaled = grad_out * norm_gain
    mean_one = jnp.mean(scaled, axis=-1, keepdims=True)
    mean_two = jnp.mean(scaled * norm_hat, axis=-1, keepdims=True)
    grad_input = inv_std * (scaled - mean_one - norm_hat * mean_two)
    return (grad_input, jnp.sum(grad_out * norm_hat, axis=0), jnp.sum(grad_out, axis=0))


def wide(value):
    return value.astype(jnp.float32)


def narrow(value):
    return value.astype(jnp.bfloat16)


def pick_block(value, index, count):
    size = value.shape[0] // count
    return lax.dynamic_slice_in_dim(value, index * size, size, 0)


def small_total(value, place):
    if place.chips != 2 or lax.axis_size("ctx") != 4:
        return lax.psum(value, ("x", "core", "ctx", "tp"))
    value = value + mate(value)
    value = value + other_tp(value)
    value = value + lax.ppermute(value, "x", [(0, 1), (1, 0)])
    value = value + lax.ppermute(value, "ctx", [(0, 1), (3, 2)])
    value = value + lax.ppermute(value, "ctx", [(1, 2), (2, 1)])
    outer = (place.ctx == 0) | (place.ctx == 3)
    return jnp.where(outer, lax.ppermute(value, "ctx", [(1, 0), (2, 3)]), value)


def core_sum(own_part, mate_part):
    return own_part + wide(mate(narrow(mate_part)))


def gelu_slope(pre_act, grad_act):
    pullback = jax.vjp(lambda values: jax.nn.gelu(values, approximate=True), pre_act)[1]
    return pullback(grad_act)[0]


def pair_major(value):
    width = value.shape[-1]
    return jnp.concatenate(
        [value[kind, :, at : at + PAIR] for at in range(0, width, PAIR) for kind in range(3)],
        axis=-1,
    )


def pack_kernel(qkv_ref, proj_ref, out_ref):
    width = qkv_ref.shape[3]
    for pair in range(width // PAIR):
        for kind in range(3):
            at = (3 * pair + kind) * PAIR
            out_ref[:, at : at + PAIR] = qkv_ref[0, kind, :, pair * PAIR : (pair + 1) * PAIR]
    out_ref[:, 3 * width :] = jnp.transpose(proj_ref[0])


def attn_piece(layer, qkv_weight, proj_weight):
    rows, width = qkv_weight.shape[2:]
    return pl.pallas_call(
        pack_kernel,
        grid=(1,),
        in_specs=[
            pl.BlockSpec((1, 3, rows, width), lambda step: (layer, 0, 0, 0)),
            pl.BlockSpec((1, width, rows), lambda step: (layer, 0, 0)),
        ],
        out_specs=pl.BlockSpec((rows, 4 * width), lambda step: (0, 0)),
        out_shape=jax.ShapeDtypeStruct((rows, 4 * width), jnp.bfloat16),
        compiler_params=pltpu.CompilerParams(vmem_limit_bytes=24 << 20),
    )(qkv_weight, proj_weight)


def unpack_kernel(first_ref, second_ref, out_ref):
    kind = pl.program_id(0)
    width = out_ref.shape[3]
    for pair in range(width // PAIR):
        at = pl.multiple_of((3 * pair + kind) * PAIR, PAIR)
        for layer, ref in enumerate((first_ref, second_ref)):
            out_ref[layer, 0, :, pair * PAIR : (pair + 1) * PAIR] = ref[
                :, pl.ds(at, PAIR)
            ].astype(jnp.float32)


def unpack_heads(first, second):
    rows, width = first.shape
    width = width // 3
    block = pl.BlockSpec((rows, 3 * width), lambda kind: (0, 0))
    return pl.pallas_call(
        unpack_kernel,
        grid=(3,),
        in_specs=[block, block],
        out_specs=pl.BlockSpec((2, 1, rows, width), lambda kind: (0, kind, 0, 0)),
        out_shape=jax.ShapeDtypeStruct((2, 3, rows, width), jnp.float32),
        compiler_params=pltpu.CompilerParams(vmem_limit_bytes=24 << 20),
    )(first, second)


def per_device(
    tokens,
    cotangent,
    doc_lengths,
    norm_gains,
    norm_biases,
    qkv_weight,
    qv_bias,
    proj_weight,
    fc_weight,
    fc_bias,
    out_weight,
):
    place = Place()
    block_len, model_width = tokens.shape[1:]
    shard_rows = qkv_weight.shape[2]
    half_width = qkv_weight.shape[3]
    layer_count = qkv_weight.shape[0]
    reach = WINDOW // block_len
    key_len = (reach + 1) * block_len
    last = reach * block_len

    def my_seq(value):
        return lax.dynamic_index_in_dim(value, place.tp, 0, False)

    def both_seqs(own, other):
        return ordered(own, other, place.tp)

    own_tokens = my_seq(tokens)
    grad_hidden = wide(my_seq(cotangent))
    bias_parts = jnp.sum(grad_hidden.reshape(16, -1, model_width), axis=1)
    bias_parts = lax.psum(bias_parts, "ctx")
    attn_blocks = gather_blocks(attn_piece(0, qkv_weight, proj_weight), place)
    halo = [onward(own_tokens)]
    for _ in range(reach - 1):
        halo.insert(0, onward(halo[0]))
    vectors = jnp.concatenate([norm_gains, norm_biases], axis=1)
    vectors = gather_small(vectors.reshape(-1, vectors.shape[2]), place)
    vectors = wide(vectors).reshape(layer_count, 6, model_width)
    biases = jnp.concatenate([qv_bias.reshape(layer_count, -1), fc_bias], axis=1)
    biases = wide(jnp.where(place.home, biases, other_tp(biases)))
    lengths = my_seq(doc_lengths)
    lengths = jnp.stack([lengths, mate(lengths)])
    mlp_piece, mlp_later = [
        jnp.concatenate([fc_weight[layer], jnp.transpose(out_weight[layer])], axis=1)
        for layer in range(layer_count)
    ]
    attn_later = attn_piece(1, qkv_weight, proj_weight)
    halo[-1], mlp_piece, mlp_later, attn_later = tie(
        halo[-1], mlp_piece, mlp_later, attn_later
    )
    mlp_blocks = gather_blocks(mlp_piece, place)
    fc_width = fc_weight.shape[2]

    doc_ends = jnp.cumsum(lengths, axis=1)
    first_pos = place.ctx * block_len
    query_pos = first_pos + jnp.arange(block_len, dtype=jnp.int32)
    started = doc_ends[:, None, :] <= query_pos[None, :, None]
    doc_start = jnp.max(jnp.where(started, doc_ends[:, None, :], 0), axis=-1)
    low_pos = jnp.maximum(doc_start, query_pos[None, :] - (WINDOW - 1))
    low_pos = (low_pos - first_pos + last).astype(jnp.int32)

    hidden = wide(own_tokens)
    stash = []
    weights = []
    for layer in range(layer_count):
        gains, shifts = vectors[layer, :2], vectors[layer, 2:]
        bias_q, bias_v = biases[layer, :half_width], biases[layer, half_width : 2 * half_width]
        bias_qkv = pair_major(jnp.stack([bias_q, jnp.zeros_like(bias_q), bias_v])[:, None])
        bias_fc = biases[layer, 2 * half_width :]
        attn_in, hat_attn, inv_attn = norm_forward(hidden, gains[0], shifts[0])
        own_near = [attn_in]
        mate_near = [mate(attn_in)]
        attn_swap = CoreSwap(attn_blocks, place)
        if layer == 0:
            w_attn = join(attn_swap)
        step_value = attn_in
        for index in range(reach):
            if layer == 0:
                part = norm_forward(wide(halo[reach - 1 - index]), gains[0], shifts[0])[0]
            else:
                step_value = part = onward(step_value)
                if index == 0:
                    step_value, mlp_later = tie(step_value, mlp_later)
                    mlp_blocks = gather_blocks(mlp_later, place)
                    part = step_value
                if index == 1:
                    step_value, w_attn = tie(step_value, join(attn_swap))
                    part = step_value
            own_near.insert(0, part)
            mate_near.insert(0, mate(part))
        near = jnp.concatenate(own_near + mate_near)
        if layer == 0:
            near, bias_parts = tie(near, bias_parts)
        w_qkv, w_proj_t = w_attn[:, : 3 * half_width], w_attn[:, 3 * half_width :]
        packed = narrow(dot_f32(near, w_qkv) + bias_qkv).reshape(2, key_len, -1)
        mixed, log_total = attention_forward(packed, low_pos)
        if layer + 1 < layer_count:
            mixed, attn_later = tie(mixed, attn_later)
            attn_blocks = gather_blocks(attn_later, place)
        mate_part = dot_second(mixed[1], w_proj_t)
        own_part = dot_second(mixed[0], w_proj_t)
        middle = hidden + core_sum(own_part, mate_part) + shifts[1]
        mlp_own, hat_mlp, inv_mlp = norm_forward(middle, gains[1], shifts[2])
        mlp_in = jnp.concatenate([mlp_own, mate(mlp_own)])
        mlp_in, mlp_blocks = tie(mlp_in, mlp_blocks)
        w_fc = join(CoreSwap(mlp_blocks, place, 0, fc_width))
        out_swap = CoreSwap(mlp_blocks, place, 1, fc_width)
        pre_act = dot_f32(mlp_in, w_fc) + bias_fc
        activated = narrow(jax.nn.gelu(pre_act, approximate=True))
        w_out_t = join(out_swap)
        mate_part = dot_second(activated[block_len:], w_out_t)
        own_part = dot_second(activated[:block_len], w_out_t)
        hidden = middle + core_sum(own_part, mate_part) + shifts[3]
        weights.append((w_qkv, w_proj_t, w_fc, w_out_t))
        stash.append(
            (near, hat_attn, inv_attn, packed, mixed, log_total, hat_mlp, inv_mlp, mlp_in,
             pre_act, activated)
        )

    own_output = narrow(hidden)
    last_sum = None
    sums = {}
    waiting, latest, first_sum = [], [], []
    small_parts = [None] * layer_count

    def advance(value, name):
        nonlocal last_sum
        share = waiting.pop(0)
        assert share[0] == name
        value, share, last_sum = tie(value, share[1], last_sum)
        if latest:
            sums[latest[0]] = last_sum
        else:
            first_sum.append(last_sum)
        latest[:] = [name]
        last_sum = lax.psum(share, "ctx")
        sums[name] = last_sum
        return value

    def settle(value, name):
        assert waiting[0][0] == name
        value, share = tie(value, waiting[0][1])
        waiting[0] = (name, share)
        return value

    for layer in reversed(range(layer_count)):
        near, hat_attn, inv_attn, packed, mixed, log_total = stash[layer][:6]
        hat_mlp, inv_mlp, mlp_in, pre_act, activated = stash[layer][6:]
        gains = vectors[layer, :2]
        w_qkv, w_proj_t, w_fc, w_out_t = weights[layer]
        final = layer == 0
        grad_out_bias = jnp.sum(grad_hidden, axis=0)
        if not final:
            last_sum = bias_parts
        grad_low = narrow(grad_hidden)
        grad_low = jnp.concatenate([grad_low, mate(grad_low)])
        out_swap = scatter_swap(narrow(dot_first(grad_low, activated)), place)
        grad_pre = narrow(gelu_slope(pre_act, dot_f32(grad_low, w_out_t)))
        if not final:
            grad_pre, out_swap.came = tie(grad_pre, out_swap.came)
            waiting.append(("out%d" % layer, scatter_sum(join(out_swap))))
        grad_fc_bias = jnp.sum(wide(grad_pre), axis=0)
        mate_part = dot_second(grad_pre[block_len:], w_fc)
        own_part = dot_second(grad_pre[:block_len], w_fc)
        grad_norm_in = core_sum(own_part, mate_part)
        if final:
            grad_norm_in, grad_out = tie(grad_norm_in, join(out_swap))
            (grad_norm_in, grad_out) = settle((grad_norm_in, grad_out), "attn1")
            share = jnp.concatenate([early_share, waiting.pop(0)[1]], axis=1)
            waiting.insert(0, ("first", share))
            grad_norm_in = advance(grad_norm_in, "first")
            waiting.append(("out%d" % layer, scatter_sum(grad_out)))
        fc_swap = scatter_swap(narrow(dot_first(mlp_in, grad_pre)), place)
        grad_from_mlp, grad_gain_mlp, grad_shift_mlp = norm_backward(
            grad_norm_in, hat_mlp, inv_mlp, gains[1]
        )
        grad_middle = grad_hidden + grad_from_mlp
        grad_proj_bias = jnp.sum(grad_middle, axis=0)
        grad_low = narrow(grad_middle)
        grad_low = jnp.concatenate([grad_low, mate(grad_low)])
        grad_mixed = narrow(dot_f32(grad_low, w_proj_t)).reshape(mixed.shape)
        proj_swap = scatter_swap(
            narrow(dot_first(grad_low, mixed.reshape(2 * block_len, half_width))), place
        )
        grad_mixed, fc_swap.came, proj_swap.came = tie(grad_mixed, fc_swap.came, proj_swap.came)
        grad_mixed, grad_fc = tie(grad_mixed, join(fc_swap, proj_swap))
        grad_packed = attention_backward(packed, mixed, grad_mixed, log_total, low_pos)
        if final:
            grad_packed, far_output, grad_fc = tie(grad_packed, far_output, grad_fc)
            grad_packed, grad_fc = settle((grad_packed, grad_fc), "out%d" % layer)
        else:
            grad_packed, grad_fc = tie(grad_packed, grad_fc)
            grad_packed = advance(grad_packed, "out%d" % layer)
        waiting.append(("fc%d" % layer, scatter_sum(grad_fc)))
        mate_part = dot_second(grad_packed[1], w_qkv)
        own_part = dot_second(grad_packed[0], w_qkv)
        grad_near = core_sum(own_part, mate_part)
        far_total, grad_attn_in = grad_near[:last], grad_near[last:]
        rows = grad_packed.reshape(2 * key_len, -1)
        grad_near, rows = tie(grad_near, rows)
        if final:
            grad_near = advance(grad_near, "out%d" % layer)
        far_total, grad_attn_in = grad_near[:last], grad_near[last:]
        carried = backward_step(narrow(far_total[:block_len]))
        grad_qkv = narrow(dot_first(near, rows))
        grad_bias = jnp.sum(wide(rows), axis=0)
        if final:
            attn_swap = scatter_swap(grad_qkv, place)
        for step in range(1, reach + 1):
            if step == 1 and not final:
                carried, grad_qkv, last_sum = tie(carried, grad_qkv, last_sum)
                attn_swap = scatter_swap(grad_qkv, place)
            if step == 1 and final:
                carried, grad_attn = tie(carried, join(attn_swap))
                carried, grad_attn = settle((carried, grad_attn), "fc%d" % layer)
                waiting.append(("attn%d" % layer, scatter_sum(grad_attn)))
                carried = advance(carried, "fc%d" % layer)
            if step == 2 and not final:
                carried, grad_bias, grad_attn, own_output = tie(
                    carried, grad_bias, join(attn_swap), own_output
                )
                far_output = other_tp(own_output)
                carried, grad_attn = settle((carried, grad_attn), "fc%d" % layer)
                early_share = waiting.pop(0)[1]
                waiting.append(("attn%d" % layer, scatter_sum(grad_attn)))
            if step == 2 and final:
                carried, grad_bias = tie(carried, grad_bias)
                carried = advance(carried, "attn%d" % layer)
            arrived = wide(carried)
            if step < reach:
                section = far_total[step * block_len : (step + 1) * block_len]
                carried = backward_step(narrow(arrived + section))
            else:
                grad_attn_in = grad_attn_in + arrived
        grad_from_attn, grad_gain_attn, grad_shift_attn = norm_backward(
            grad_attn_in, hat_attn, inv_attn, gains[0]
        )
        grad_hidden = grad_middle + grad_from_attn
        grad_bias = grad_bias.reshape(-1, 3, PAIR)
        halves = jnp.concatenate(
            [grad_bias[:, 0].reshape(-1), grad_bias[:, 2].reshape(-1), grad_fc_bias]
        )
        empty = jnp.zeros_like(halves)
        if not final:
            grad_out_bias = jnp.where(place.ctx == 0, jnp.sum(first_sum[0], axis=0), 0.0)
        small_parts[layer] = jnp.concatenate(
            [
                grad_gain_attn, grad_gain_mlp,
                grad_shift_attn, grad_proj_bias, grad_shift_mlp, grad_out_bias,
                jnp.where(place.core == 0, halves, empty),
                jnp.where(place.core == 1, halves, empty),
            ]
        )

    small = small_total(jnp.stack(small_parts), place)
    far_grad = wide(other_tp(narrow(grad_hidden)))
    token_grad = both_seqs(grad_hidden, far_grad)
    split = 6 * model_width
    norms = small[:, :split].reshape(layer_count, 6, model_width)
    norms = lax.dynamic_slice_in_dim(norms, place.shard * shard_rows, shard_rows, 2)
    halves = small[:, split:].reshape(layer_count, 2, -1)
    halves = lax.dynamic_index_in_dim(halves, place.tp, 1, False)
    split = fc_width + half_width
    attn = [sums["attn0"], sums["first"][:, split:]]
    fc_proj = [sums["fc0"], sums["first"][:, :split]]
    return (
        both_seqs(own_output, far_output),
        token_grad,
        norms[:, :2],
        norms[:, 2:],
        unpack_heads(*attn),
        halves[:, : 2 * half_width].reshape(layer_count, 2, half_width),
        jnp.stack([jnp.transpose(wide(v[:, fc_width:])) for v in fc_proj]),
        jnp.stack([wide(v[:, :fc_width]) for v in fc_proj]),
        halves[:, 2 * half_width :],
        jnp.stack([jnp.transpose(wide(sums["out%d" % layer])) for layer in range(layer_count)]),
    )


def solution(mesh):
    devices = mesh.devices
    devices = devices.reshape((devices.shape[0] // 2, 2) + devices.shape[1:])
    mesh = jax.sharding.Mesh(devices, ("x", "core", "ctx", "tp"))
    placed = (
        P(("x", "core"), "ctx", None),
        P(("x", "core"), "ctx", None),
        P(("x", "core"), None),
        P(None, None, ("x", "core")),
        P(None, None, ("x", "core")),
        P(None, None, ("x", "core"), "tp"),
        P(None, None, "tp"),
        P(None, "tp", ("x", "core")),
        P(None, ("x", "core"), "tp"),
        P(None, "tp"),
        P(None, "tp", ("x", "core")),
    )
    return jax.shard_map(
        per_device,
        mesh=mesh,
        in_specs=placed,
        out_specs=(
            P(("x", "core"), "ctx", None),
            P(("x", "core"), "ctx", None),
            P(None, None, ("x", "core")),
            P(None, None, ("x", "core")),
            P(None, None, ("x", "core"), "tp"),
            P(None, None, "tp"),
            P(None, "tp", ("x", "core")),
            P(None, ("x", "core"), "tp"),
            P(None, "tp"),
            P(None, "tp", ("x", "core")),
        ),
        check_vma=False,
    )
```

```python
import jax
import jax.numpy as jnp
from jax import lax
from jax.experimental import pallas as pl
from jax.experimental.pallas import tpu as pltpu
from jax.sharding import PartitionSpec as P

HD = 64
WINDOW = 1024
TILE = 256
masked_score = -1e30


def contract(left_side, right_side, left_dim, right_dim):
    return lax.dot_general(
        left_side, right_side, (((left_dim,), (right_dim,)), ((), ())),
        preferred_element_type=jnp.float32,
    )


def half_mask(shape, half):
    lane = lax.broadcasted_iota(jnp.int32, shape, 1)
    return (lane < HD) if half == 0 else (lane >= HD)


PAIR = 2 * HD


def forward_kernel(qkv_ref, low_ref, mixed_ref, total_ref):
    block_len = mixed_ref.shape[1]
    first = qkv_ref.shape[1] - block_len
    span = WINDOW + TILE
    eye = lax.broadcasted_iota(jnp.int32, (TILE, TILE), 0) == lax.broadcasted_iota(
        jnp.int32, (TILE, TILE), 1
    )
    for block in range(block_len // TILE):
        rows = pl.ds(block * TILE, TILE)
        window = pl.ds(block * TILE, span)
        queries = qkv_ref[0, pl.ds(first + block * TILE, TILE), :PAIR]
        queries = queries * jnp.asarray(HD ** (-0.5), jnp.bfloat16)
        keys = qkv_ref[0, window, PAIR : 2 * PAIR]
        values = qkv_ref[0, window, 2 * PAIR :]
        low_pos = low_ref[0, rows, :] - block * TILE
        key_pos = lax.broadcasted_iota(jnp.int32, (TILE, span), 1)
        query_pos = lax.broadcasted_iota(jnp.int32, (TILE, TILE), 0) + WINDOW
        allowed = key_pos >= low_pos
        causal = key_pos[:, WINDOW:] <= query_pos
        mixed = jnp.zeros((TILE, 2 * HD), jnp.float32)
        for half in range(2):
            scores = contract(
                jnp.where(half_mask(queries.shape, half), queries, 0), keys, 1, 1
            )
            early = jnp.where(allowed[:, :WINDOW], scores[:, :WINDOW], masked_score)
            late = jnp.where(allowed[:, WINDOW:] & causal, scores[:, WINDOW:], masked_score)
            top_score = jnp.maximum(
                jnp.max(early, axis=1, keepdims=True), jnp.max(late, axis=1, keepdims=True)
            )
            early = jnp.exp(early - top_score)
            late = jnp.exp(late - top_score)
            row_total = jnp.sum(early, axis=1, keepdims=True) + jnp.sum(
                late, axis=1, keepdims=True
            )
            part = contract(early.astype(jnp.bfloat16), values[:WINDOW], 1, 0) + contract(
                late.astype(jnp.bfloat16), values[WINDOW:], 1, 0
            )
            part = part * (1.0 / row_total)
            mixed = jnp.where(half_mask(mixed.shape, half), part, mixed)
            log_total = top_score + jnp.log(row_total)
            total_ref[0, 0, half : half + 1, rows] = jnp.sum(
                jnp.where(eye, log_total, 0.0), axis=0, keepdims=True
            )
        mixed_ref[0, rows, :] = mixed.astype(jnp.bfloat16)


def attention_forward(packed, low_pos):
    groups, key_len, width = packed.shape
    block_len = low_pos.shape[1]
    pairs = width // (3 * PAIR)
    pick = lambda seq, pair: (seq, 0, pair)
    return pl.pallas_call(
        forward_kernel,
        grid=(groups, pairs),
        in_specs=[
            pl.BlockSpec((1, key_len, 3 * PAIR), pick),
            pl.BlockSpec((1, block_len, 1), lambda seq, pair: (seq, 0, 0)),
        ],
        out_specs=[
            pl.BlockSpec((1, block_len, PAIR), pick),
            pl.BlockSpec((1, 1, 2, block_len), lambda seq, pair: (seq, pair, 0, 0)),
        ],
        out_shape=[
            jax.ShapeDtypeStruct((groups, block_len, pairs * PAIR), jnp.bfloat16),
            jax.ShapeDtypeStruct((groups, pairs, 2, block_len), jnp.float32),
        ],
        compiler_params=pltpu.CompilerParams(vmem_limit_bytes=56 << 20),
        cost_estimate=pl.CostEstimate(
            flops=block_len,
            bytes_accessed=block_len,
            transcendentals=0,
        ),
    )(packed, low_pos[:, :, None])


def backward_kernel(qkv_ref, mixed_ref, grad_ref, total_ref, low_ref, out_ref, gk_sum, gv_sum):
    block_len = mixed_ref.shape[1]
    first = qkv_ref.shape[1] - block_len
    span = WINDOW + TILE
    scale = HD ** (-0.5)
    gk_sum[...] = jnp.zeros_like(gk_sum)
    gv_sum[...] = jnp.zeros_like(gv_sum)
    eye = lax.broadcasted_iota(jnp.int32, (TILE, TILE), 0) == lax.broadcasted_iota(
        jnp.int32, (TILE, TILE), 1
    )
    for block in range(block_len // TILE):
        rows = pl.ds(block * TILE, TILE)
        window = pl.ds(block * TILE, span)
        queries = qkv_ref[0, pl.ds(first + block * TILE, TILE), :PAIR]
        queries = queries * jnp.asarray(scale, jnp.bfloat16)
        keys = qkv_ref[0, window, PAIR : 2 * PAIR]
        values = qkv_ref[0, window, 2 * PAIR :]
        grads = grad_ref[0, rows, :]
        product = grads.astype(jnp.float32) * mixed_ref[0, rows, :].astype(jnp.float32)
        low_pos = low_ref[0, :, rows] - block * TILE
        key_pos = lax.broadcasted_iota(jnp.int32, (span, TILE), 0)
        query_pos = lax.broadcasted_iota(jnp.int32, (TILE, TILE), 1) + WINDOW
        allowed = key_pos >= low_pos
        late_allowed = allowed[WINDOW:] & (key_pos[WINDOW:] <= query_pos)
        keys_t = jnp.transpose(keys)
        gq_parts = []
        for half in range(2):
            mask = half_mask(queries.shape, half)
            q_half = jnp.where(mask, queries, 0)
            g_half = jnp.where(mask, grads, 0)
            delta = jnp.sum(jnp.where(mask, product, 0.0), axis=1, keepdims=True)
            delta = jnp.sum(jnp.where(eye, delta, 0.0), axis=0, keepdims=True)
            log_total = total_ref[0, 0, half : half + 1, rows]
            scores = contract(keys, q_half, 1, 1)
            probs = jnp.concatenate(
                [
                    jnp.where(allowed[:WINDOW], jnp.exp(scores[:WINDOW] - log_total), 0.0),
                    jnp.where(late_allowed, jnp.exp(scores[WINDOW:] - log_total), 0.0),
                ]
            )
            grad_probs = contract(values, g_half, 1, 1)
            grad_scores = (probs * (grad_probs - delta)).astype(jnp.bfloat16)
            gv_sum[window, :] += contract(probs.astype(jnp.bfloat16), g_half, 1, 0)
            gk_sum[window, :] += contract(grad_scores, q_half, 1, 0)
            gq_parts.append(contract(keys_t[half * HD : (half + 1) * HD], grad_scores, 1, 0))
        gq = jnp.transpose(jnp.concatenate(gq_parts)) * scale
        out_ref[0, pl.ds(first + block * TILE, TILE), :PAIR] = gq.astype(jnp.bfloat16)
    out_ref[0, :first, :PAIR] = jnp.zeros((first, PAIR), jnp.bfloat16)
    out_ref[0, :, PAIR : 2 * PAIR] = gk_sum[...].astype(jnp.bfloat16)
    out_ref[0, :, 2 * PAIR :] = gv_sum[...].astype(jnp.bfloat16)


def attention_backward(packed, mixed, grads, log_total, low_pos):
    groups, key_len, width = packed.shape
    block_len = mixed.shape[1]
    pairs = width // (3 * PAIR)
    pick = lambda seq, pair: (seq, 0, pair)
    row_spec = pl.BlockSpec((1, block_len, PAIR), pick)
    packed_spec = pl.BlockSpec((1, key_len, 3 * PAIR), pick)
    return pl.pallas_call(
        backward_kernel,
        grid=(groups, pairs),
        in_specs=[
            packed_spec, row_spec, row_spec,
            pl.BlockSpec((1, 1, 2, block_len), lambda seq, pair: (seq, pair, 0, 0)),
            pl.BlockSpec((1, 1, block_len), lambda seq, pair: (seq, 0, 0)),
        ],
        out_specs=packed_spec,
        out_shape=jax.ShapeDtypeStruct(packed.shape, jnp.bfloat16),
        scratch_shapes=[
            pltpu.VMEM((key_len, PAIR), jnp.float32),
            pltpu.VMEM((key_len, PAIR), jnp.float32),
        ],
        compiler_params=pltpu.CompilerParams(vmem_limit_bytes=56 << 20),
        cost_estimate=pl.CostEstimate(
            flops=block_len,
            bytes_accessed=block_len,
            transcendentals=0,
        ),
    )(packed, mixed, grads, log_total, low_pos[:, None, :])


norm_eps = 1e-05


def mate(value):
    return lax.ppermute(value, "core", [(0, 1), (1, 0)])


def other_tp(value):
    return lax.ppermute(value, "tp", [(0, 1), (1, 0)])


def onward(value):
    count = lax.axis_size("ctx")
    return lax.ppermute(value, "ctx", [(i, i + 1) for i in range(count - 1)])


def backward_step(value):
    count = lax.axis_size("ctx")
    return lax.ppermute(value, "ctx", [(i + 1, i) for i in range(count - 1)])


class Place:
    def __init__(self):
        self.chips = lax.axis_size("x")
        self.core = lax.axis_index("core")
        self.shard = lax.axis_index("x") * 2 + self.core
        self.tp = lax.axis_index("tp")
        self.ctx = lax.axis_index("ctx")
        self.home = self.core == self.tp


def tie(*values):
    return lax.optimization_barrier(values)


def ordered(own, other, position, axis=0):
    return jnp.where(
        position == 0,
        jnp.stack([own, other], axis=axis),
        jnp.stack([other, own], axis=axis),
    )


def join_kernel(core_ref, *refs):
    out_ref = refs[-1]
    own = pl.program_id(1) == core_ref[0]
    at = 0
    for blocks_ref, came_ref in zip(refs[0:-1:2], refs[1:-1:2]):
        width = came_ref.shape[2]

        @pl.when(own)
        def _(at=at, width=width, blocks_ref=blocks_ref):
            out_ref[:, at : at + width] = blocks_ref[0, 0]

        @pl.when(jnp.logical_not(own))
        def _(at=at, width=width, came_ref=came_ref):
            out_ref[:, at : at + width] = came_ref[0]

        at += width


class CoreSwap:
    def __init__(self, blocks, place, column=0, width=None):
        self.place, self.blocks, self.column = place, blocks, column
        width = blocks.shape[3] if width is None else width
        other = lax.dynamic_index_in_dim(blocks, 1 - place.core, 1, False)
        self.came = mate(other[..., column * width : (column + 1) * width])


def join(*swaps):
    chips, rows = swaps[0].came.shape[:2]
    in_specs, operands, total = [], [], 0
    for swap in swaps:
        width = swap.came.shape[2]
        in_specs += [
            pl.BlockSpec(
                (1, 1, rows, width),
                lambda chip, part, core, column=swap.column: (chip, core[0], 0, column),
            ),
            pl.BlockSpec((1, rows, width), lambda chip, part, core: (chip, 0, 0)),
        ]
        operands += [swap.blocks, swap.came]
        total += width
    return pl.pallas_call(
        join_kernel,
        grid_spec=pltpu.PrefetchScalarGridSpec(
            num_scalar_prefetch=1,
            grid=(chips, 2),
            in_specs=in_specs,
            out_specs=pl.BlockSpec((rows, total), lambda chip, part, core: (chip * 2 + part, 0)),
        ),
        out_shape=jax.ShapeDtypeStruct((chips * 2 * rows, total), jnp.bfloat16),
        compiler_params=pltpu.CompilerParams(vmem_limit_bytes=24 << 20),
        cost_estimate=pl.CostEstimate(
            flops=rows, bytes_accessed=rows, transcendentals=0
        ),
    )(swaps[0].place.core.reshape(1).astype(jnp.int32), *operands)


def gather_blocks(piece, place):
    whole = lax.all_gather(piece, ("x", "tp"), axis=0, tiled=False)
    return whole.reshape((place.chips, 2) + piece.shape)


def scatter_swap(grads, place):
    return CoreSwap(grads.reshape(place.chips, 2, -1, grads.shape[1]), place)


def scatter_sum(blocks):
    return lax.psum_scatter(blocks, ("x", "tp"), scatter_dimension=0, tiled=True)


def dot_f32(left_side, right_side):
    return jnp.dot(left_side, right_side, preferred_element_type=jnp.float32)


def dot_first(left_side, right_side):
    return contract(left_side, right_side, 0, 0)


def dot_second(left_side, right_side):
    return contract(left_side, right_side, 1, 1)


def gather_small(value, place):
    if place.chips != 2:
        return lax.all_gather(value, ("x", "core"), axis=1, tiled=True)
    near = mate(value)
    pair = ordered(value, near, place.core, 1).reshape(value.shape[0], -1)
    far = lax.ppermute(pair, "x", [(0, 1), (1, 0)])
    return ordered(pair, far, lax.axis_index("x"), 1).reshape(value.shape[0], -1)


def norm_forward(hidden, norm_gain, norm_shift):
    row_mean = jnp.mean(hidden, axis=-1, keepdims=True)
    centred = hidden - row_mean
    variance = jnp.mean(centred * centred, axis=-1, keepdims=True)
    inv_std = lax.rsqrt(variance + norm_eps)
    norm_hat = centred * inv_std
    return ((norm_hat * norm_gain + norm_shift).astype(jnp.bfloat16), norm_hat, inv_std)


def norm_backward(grad_out, norm_hat, inv_std, norm_gain):
    scaled = grad_out * norm_gain
    mean_one = jnp.mean(scaled, axis=-1, keepdims=True)
    mean_two = jnp.mean(scaled * norm_hat, axis=-1, keepdims=True)
    grad_input = inv_std * (scaled - mean_one - norm_hat * mean_two)
    return (grad_input, jnp.sum(grad_out * norm_hat, axis=0), jnp.sum(grad_out, axis=0))


def wide(value):
    return value.astype(jnp.float32)


def narrow(value):
    return value.astype(jnp.bfloat16)


def pick_block(value, index, count):
    size = value.shape[0] // count
    return lax.dynamic_slice_in_dim(value, index * size, size, 0)


def small_total(value, place):
    if place.chips != 2 or lax.axis_size("ctx") != 4:
        return lax.psum(value, ("x", "core", "ctx", "tp"))
    value = value + mate(value)
    value = value + other_tp(value)
    value = value + lax.ppermute(value, "x", [(0, 1), (1, 0)])
    value = value + lax.ppermute(value, "ctx", [(0, 1), (3, 2)])
    value = value + lax.ppermute(value, "ctx", [(1, 2), (2, 1)])
    outer = (place.ctx == 0) | (place.ctx == 3)
    return jnp.where(outer, lax.ppermute(value, "ctx", [(1, 0), (2, 3)]), value)


def core_sum(own_part, mate_part):
    return own_part + wide(mate(narrow(mate_part)))


def gelu_slope(pre_act, grad_act):
    pullback = jax.vjp(lambda values: jax.nn.gelu(values, approximate=True), pre_act)[1]
    return pullback(grad_act)[0]


def pair_major(value):
    width = value.shape[-1]
    return jnp.concatenate(
        [value[kind, :, at : at + PAIR] for at in range(0, width, PAIR) for kind in range(3)],
        axis=-1,
    )


def pack_kernel(qkv_ref, proj_ref, out_ref):
    width = qkv_ref.shape[3]
    for pair in range(width // PAIR):
        for kind in range(3):
            at = (3 * pair + kind) * PAIR
            out_ref[:, at : at + PAIR] = qkv_ref[0, kind, :, pair * PAIR : (pair + 1) * PAIR]
    out_ref[:, 3 * width :] = jnp.transpose(proj_ref[0])


def attn_piece(layer, qkv_weight, proj_weight):
    rows, width = qkv_weight.shape[2:]
    return pl.pallas_call(
        pack_kernel,
        grid=(1,),
        in_specs=[
            pl.BlockSpec((1, 3, rows, width), lambda step: (layer, 0, 0, 0)),
            pl.BlockSpec((1, width, rows), lambda step: (layer, 0, 0)),
        ],
        out_specs=pl.BlockSpec((rows, 4 * width), lambda step: (0, 0)),
        out_shape=jax.ShapeDtypeStruct((rows, 4 * width), jnp.bfloat16),
        compiler_params=pltpu.CompilerParams(vmem_limit_bytes=24 << 20),
    )(qkv_weight, proj_weight)


def unpack_kernel(first_ref, second_ref, out_ref):
    kind = pl.program_id(0)
    width = out_ref.shape[3]
    for pair in range(width // PAIR):
        at = pl.multiple_of((3 * pair + kind) * PAIR, PAIR)
        for layer, ref in enumerate((first_ref, second_ref)):
            out_ref[layer, 0, :, pair * PAIR : (pair + 1) * PAIR] = ref[
                :, pl.ds(at, PAIR)
            ].astype(jnp.float32)


def unpack_heads(first, second):
    rows, width = first.shape
    width = width // 3
    block = pl.BlockSpec((rows, 3 * width), lambda kind: (0, 0))
    return pl.pallas_call(
        unpack_kernel,
        grid=(3,),
        in_specs=[block, block],
        out_specs=pl.BlockSpec((2, 1, rows, width), lambda kind: (0, kind, 0, 0)),
        out_shape=jax.ShapeDtypeStruct((2, 3, rows, width), jnp.float32),
        compiler_params=pltpu.CompilerParams(vmem_limit_bytes=24 << 20),
    )(first, second)


def per_device(
    tokens,
    cotangent,
    doc_lengths,
    norm_gains,
    norm_biases,
    qkv_weight,
    qv_bias,
    proj_weight,
    fc_weight,
    fc_bias,
    out_weight,
):
    place = Place()
    block_len, model_width = tokens.shape[1:]
    shard_rows = qkv_weight.shape[2]
    half_width = qkv_weight.shape[3]
    layer_count = qkv_weight.shape[0]
    reach = WINDOW // block_len
    key_len = (reach + 1) * block_len
    last = reach * block_len

    def my_seq(value):
        return lax.dynamic_index_in_dim(value, place.tp, 0, False)

    def both_seqs(own, other):
        return ordered(own, other, place.tp)

    own_tokens = my_seq(tokens)
    grad_hidden = wide(my_seq(cotangent))
    bias_parts = jnp.sum(grad_hidden.reshape(16, -1, model_width), axis=1)
    bias_parts = lax.psum(bias_parts, "ctx")
    attn_blocks = gather_blocks(attn_piece(0, qkv_weight, proj_weight), place)
    halo = [onward(own_tokens)]
    for _ in range(reach - 1):
        halo.insert(0, onward(halo[0]))
    vectors = jnp.concatenate([norm_gains, norm_biases], axis=1)
    vectors = gather_small(vectors.reshape(-1, vectors.shape[2]), place)
    vectors = wide(vectors).reshape(layer_count, 6, model_width)
    biases = jnp.concatenate([qv_bias.reshape(layer_count, -1), fc_bias], axis=1)
    biases = wide(jnp.where(place.home, biases, other_tp(biases)))
    lengths = my_seq(doc_lengths)
    lengths = jnp.stack([lengths, mate(lengths)])
    mlp_piece, mlp_later = [
        jnp.concatenate([fc_weight[layer], jnp.transpose(out_weight[layer])], axis=1)
        for layer in range(layer_count)
    ]
    attn_later = attn_piece(1, qkv_weight, proj_weight)
    halo[-1], mlp_piece, mlp_later, attn_later = tie(
        halo[-1], mlp_piece, mlp_later, attn_later
    )
    mlp_blocks = gather_blocks(mlp_piece, place)
    fc_width = fc_weight.shape[2]

    doc_ends = jnp.cumsum(lengths, axis=1)
    first_pos = place.ctx * block_len
    query_pos = first_pos + jnp.arange(block_len, dtype=jnp.int32)
    started = doc_ends[:, None, :] <= query_pos[None, :, None]
    doc_start = jnp.max(jnp.where(started, doc_ends[:, None, :], 0), axis=-1)
    low_pos = jnp.maximum(doc_start, query_pos[None, :] - (WINDOW - 1))
    low_pos = (low_pos - first_pos + last).astype(jnp.int32)

    hidden = wide(own_tokens)
    stash = []
    weights = []
    for layer in range(layer_count):
        gains, shifts = vectors[layer, :2], vectors[layer, 2:]
        bias_q, bias_v = biases[layer, :half_width], biases[layer, half_width : 2 * half_width]
        bias_qkv = pair_major(jnp.stack([bias_q, jnp.zeros_like(bias_q), bias_v])[:, None])
        bias_fc = biases[layer, 2 * half_width :]
        attn_in, hat_attn, inv_attn = norm_forward(hidden, gains[0], shifts[0])
        own_near = [attn_in]
        mate_near = [mate(attn_in)]
        attn_swap = CoreSwap(attn_blocks, place)
        if layer == 0:
            w_attn = join(attn_swap)
        step_value = attn_in
        for index in range(reach):
            if layer == 0:
                part = norm_forward(wide(halo[reach - 1 - index]), gains[0], shifts[0])[0]
            else:
                step_value = part = onward(step_value)
                if index == 0:
                    step_value, mlp_later = tie(step_value, mlp_later)
                    mlp_blocks = gather_blocks(mlp_later, place)
                    part = step_value
                if index == 1:
                    step_value, w_attn = tie(step_value, join(attn_swap))
                    part = step_value
            own_near.insert(0, part)
            mate_near.insert(0, mate(part))
        near = jnp.concatenate(own_near + mate_near)
        if layer == 0:
            near, bias_parts = tie(near, bias_parts)
        w_qkv, w_proj_t = w_attn[:, : 3 * half_width], w_attn[:, 3 * half_width :]
        packed = narrow(dot_f32(near, w_qkv) + bias_qkv).reshape(2, key_len, -1)
        mixed, log_total = attention_forward(packed, low_pos)
        if layer + 1 < layer_count:
            mixed, attn_later = tie(mixed, attn_later)
            attn_blocks = gather_blocks(attn_later, place)
        mate_part = dot_second(mixed[1], w_proj_t)
        own_part = dot_second(mixed[0], w_proj_t)
        middle = hidden + core_sum(own_part, mate_part) + shifts[1]
        mlp_own, hat_mlp, inv_mlp = norm_forward(middle, gains[1], shifts[2])
        mlp_in = jnp.concatenate([mlp_own, mate(mlp_own)])
        mlp_in, mlp_blocks = tie(mlp_in, mlp_blocks)
        w_fc = join(CoreSwap(mlp_blocks, place, 0, fc_width))
        out_swap = CoreSwap(mlp_blocks, place, 1, fc_width)
        pre_act = dot_f32(mlp_in, w_fc) + bias_fc
        activated = narrow(jax.nn.gelu(pre_act, approximate=True))
        w_out_t = join(out_swap)
        mate_part = dot_second(activated[block_len:], w_out_t)
        own_part = dot_second(activated[:block_len], w_out_t)
        hidden = middle + core_sum(own_part, mate_part) + shifts[3]
        weights.append((w_qkv, w_proj_t, w_fc, w_out_t))
        stash.append(
            (near, hat_attn, inv_attn, packed, mixed, log_total, hat_mlp, inv_mlp, mlp_in,
             pre_act, activated)
        )

    own_output = narrow(hidden)
    last_sum = None
    sums = {}
    waiting, latest, first_sum = [], [], []
    small_parts = [None] * layer_count

    def advance(value, name):
        nonlocal last_sum
        share = waiting.pop(0)
        assert share[0] == name
        value, share, last_sum = tie(value, share[1], last_sum)
        if latest:
            sums[latest[0]] = last_sum
        else:
            first_sum.append(last_sum)
        latest[:] = [name]
        last_sum = lax.psum(share, "ctx")
        sums[name] = last_sum
        return value

    def settle(value, name):
        assert waiting[0][0] == name
        value, share = tie(value, waiting[0][1])
        waiting[0] = (name, share)
        return value

    for layer in reversed(range(layer_count)):
        near, hat_attn, inv_attn, packed, mixed, log_total = stash[layer][:6]
        hat_mlp, inv_mlp, mlp_in, pre_act, activated = stash[layer][6:]
        gains = vectors[layer, :2]
        w_qkv, w_proj_t, w_fc, w_out_t = weights[layer]
        final = layer == 0
        grad_out_bias = jnp.sum(grad_hidden, axis=0)
        if not final:
            last_sum = bias_parts
        grad_low = narrow(grad_hidden)
        grad_low = jnp.concatenate([grad_low, mate(grad_low)])
        out_swap = scatter_swap(narrow(dot_first(grad_low, activated)), place)
        grad_act_in = grad_low
        if not final:
            grad_act_in, grad_out = tie(grad_low, join(out_swap))
            waiting.append(("out%d" % layer, scatter_sum(grad_out)))
        grad_pre = narrow(gelu_slope(pre_act, dot_f32(grad_act_in, w_out_t)))
        grad_fc_bias = jnp.sum(wide(grad_pre), axis=0)
        mate_part = dot_second(grad_pre[block_len:], w_fc)
        own_part = dot_second(grad_pre[:block_len], w_fc)
        grad_norm_in = core_sum(own_part, mate_part)
        if final:
            grad_norm_in, grad_out = tie(grad_norm_in, join(out_swap))
            (grad_norm_in, grad_out) = settle((grad_norm_in, grad_out), "attn1")
            share = jnp.concatenate([early_share, waiting.pop(0)[1]], axis=1)
            waiting.insert(0, ("first", share))
            grad_norm_in = advance(grad_norm_in, "first")
            waiting.append(("out%d" % layer, scatter_sum(grad_out)))
        fc_swap = scatter_swap(narrow(dot_first(mlp_in, grad_pre)), place)
        grad_from_mlp, grad_gain_mlp, grad_shift_mlp = norm_backward(
            grad_norm_in, hat_mlp, inv_mlp, gains[1]
        )
        grad_middle = grad_hidden + grad_from_mlp
        grad_proj_bias = jnp.sum(grad_middle, axis=0)
        grad_low = narrow(grad_middle)
        grad_low = jnp.concatenate([grad_low, mate(grad_low)])
        grad_mixed = narrow(dot_f32(grad_low, w_proj_t)).reshape(mixed.shape)
        proj_swap = scatter_swap(
            narrow(dot_first(grad_low, mixed.reshape(2 * block_len, half_width))), place
        )
        grad_mixed, fc_swap.came, proj_swap.came = tie(grad_mixed, fc_swap.came, proj_swap.came)
        grad_mixed, grad_fc = tie(grad_mixed, join(fc_swap, proj_swap))
        if not final:
            grad_mixed = advance(grad_mixed, "out%d" % layer)
        grad_packed = attention_backward(packed, mixed, grad_mixed, log_total, low_pos)
        if final:
            grad_packed, far_output, grad_fc = tie(grad_packed, far_output, grad_fc)
            grad_packed, grad_fc = settle((grad_packed, grad_fc), "out%d" % layer)
        else:
            grad_mixed, grad_fc = tie(grad_mixed, grad_fc)
        waiting.append(("fc%d" % layer, scatter_sum(grad_fc)))
        mate_part = dot_second(grad_packed[1], w_qkv)
        own_part = dot_second(grad_packed[0], w_qkv)
        grad_near = core_sum(own_part, mate_part)
        far_total, grad_attn_in = grad_near[:last], grad_near[last:]
        rows = grad_packed.reshape(2 * key_len, -1)
        grad_near, rows = tie(grad_near, rows)
        if final:
            grad_near = advance(grad_near, "out%d" % layer)
        far_total, grad_attn_in = grad_near[:last], grad_near[last:]
        carried = backward_step(narrow(far_total[:block_len]))
        grad_qkv = narrow(dot_first(near, rows))
        grad_bias = jnp.sum(wide(rows), axis=0)
        if final:
            attn_swap = scatter_swap(grad_qkv, place)
        for step in range(1, reach + 1):
            if step == 1 and not final:
                carried, grad_qkv, last_sum = tie(carried, grad_qkv, last_sum)
                attn_swap = scatter_swap(grad_qkv, place)
            if step == 1 and final:
                carried, grad_attn = tie(carried, join(attn_swap))
                carried, grad_attn = settle((carried, grad_attn), "fc%d" % layer)
                waiting.append(("attn%d" % layer, scatter_sum(grad_attn)))
                carried = advance(carried, "fc%d" % layer)
            if step == 2 and not final:
                carried, grad_bias, grad_attn, own_output = tie(
                    carried, grad_bias, join(attn_swap), own_output
                )
                far_output = other_tp(own_output)
                carried, grad_attn = settle((carried, grad_attn), "fc%d" % layer)
                early_share = waiting.pop(0)[1]
                waiting.append(("attn%d" % layer, scatter_sum(grad_attn)))
            if step == 2 and final:
                carried, grad_bias = tie(carried, grad_bias)
                carried = advance(carried, "attn%d" % layer)
            arrived = wide(carried)
            if step < reach:
                section = far_total[step * block_len : (step + 1) * block_len]
                carried = backward_step(narrow(arrived + section))
            else:
                grad_attn_in = grad_attn_in + arrived
        grad_from_attn, grad_gain_attn, grad_shift_attn = norm_backward(
            grad_attn_in, hat_attn, inv_attn, gains[0]
        )
        grad_hidden = grad_middle + grad_from_attn
        grad_bias = grad_bias.reshape(-1, 3, PAIR)
        halves = jnp.concatenate(
            [grad_bias[:, 0].reshape(-1), grad_bias[:, 2].reshape(-1), grad_fc_bias]
        )
        empty = jnp.zeros_like(halves)
        if not final:
            grad_out_bias = jnp.where(place.ctx == 0, jnp.sum(first_sum[0], axis=0), 0.0)
        small_parts[layer] = jnp.concatenate(
            [
                grad_gain_attn, grad_gain_mlp,
                grad_shift_attn, grad_proj_bias, grad_shift_mlp, grad_out_bias,
                jnp.where(place.core == 0, halves, empty),
                jnp.where(place.core == 1, halves, empty),
            ]
        )

    small = small_total(jnp.stack(small_parts), place)
    far_grad = wide(other_tp(narrow(grad_hidden)))
    token_grad = both_seqs(grad_hidden, far_grad)
    split = 6 * model_width
    norms = small[:, :split].reshape(layer_count, 6, model_width)
    norms = lax.dynamic_slice_in_dim(norms, place.shard * shard_rows, shard_rows, 2)
    halves = small[:, split:].reshape(layer_count, 2, -1)
    halves = lax.dynamic_index_in_dim(halves, place.tp, 1, False)
    split = fc_width + half_width
    attn = [sums["attn0"], sums["first"][:, split:]]
    fc_proj = [sums["fc0"], sums["first"][:, :split]]
    return (
        both_seqs(own_output, far_output),
        token_grad,
        norms[:, :2],
        norms[:, 2:],
        unpack_heads(*attn),
        halves[:, : 2 * half_width].reshape(layer_count, 2, half_width),
        jnp.stack([jnp.transpose(wide(v[:, fc_width:])) for v in fc_proj]),
        jnp.stack([wide(v[:, :fc_width]) for v in fc_proj]),
        halves[:, 2 * half_width :],
        jnp.stack([jnp.transpose(wide(sums["out%d" % layer])) for layer in range(layer_count)]),
    )


def solution(mesh):
    devices = mesh.devices
    devices = devices.reshape((devices.shape[0] // 2, 2) + devices.shape[1:])
    mesh = jax.sharding.Mesh(devices, ("x", "core", "ctx", "tp"))
    placed = (
        P(("x", "core"), "ctx", None),
        P(("x", "core"), "ctx", None),
        P(("x", "core"), None),
        P(None, None, ("x", "core")),
        P(None, None, ("x", "core")),
        P(None, None, ("x", "core"), "tp"),
        P(None, None, "tp"),
        P(None, "tp", ("x", "core")),
        P(None, ("x", "core"), "tp"),
        P(None, "tp"),
        P(None, "tp", ("x", "core")),
    )
    return jax.shard_map(
        per_device,
        mesh=mesh,
        in_specs=placed,
        out_specs=(
            P(("x", "core"), "ctx", None),
            P(("x", "core"), "ctx", None),
            P(None, None, ("x", "core")),
            P(None, None, ("x", "core")),
            P(None, None, ("x", "core"), "tp"),
            P(None, None, "tp"),
            P(None, "tp", ("x", "core")),
            P(None, ("x", "core"), "tp"),
            P(None, "tp"),
            P(None, "tp", ("x", "core")),
        ),
        check_vma=False,
    )
```

```python
import jax
import jax.numpy as jnp
from jax import lax
from jax.experimental import pallas as pl
from jax.experimental.pallas import tpu as pltpu
from jax.sharding import PartitionSpec as P

HD = 64
WINDOW = 1024
TILE = 256
masked_score = -1e30


def contract(left_side, right_side, left_dim, right_dim):
    return lax.dot_general(
        left_side, right_side, (((left_dim,), (right_dim,)), ((), ())),
        preferred_element_type=jnp.float32,
    )


def half_mask(shape, half):
    lane = lax.broadcasted_iota(jnp.int32, shape, 1)
    return (lane < HD) if half == 0 else (lane >= HD)


PAIR = 2 * HD


def forward_kernel(qkv_ref, low_ref, mixed_ref, total_ref):
    block_len = mixed_ref.shape[1]
    first = qkv_ref.shape[1] - block_len
    span = WINDOW + TILE
    eye = lax.broadcasted_iota(jnp.int32, (TILE, TILE), 0) == lax.broadcasted_iota(
        jnp.int32, (TILE, TILE), 1
    )
    for block in range(block_len // TILE):
        rows = pl.ds(block * TILE, TILE)
        window = pl.ds(block * TILE, span)
        queries = qkv_ref[0, pl.ds(first + block * TILE, TILE), :PAIR]
        queries = queries * jnp.asarray(HD ** (-0.5), jnp.bfloat16)
        keys = qkv_ref[0, window, PAIR : 2 * PAIR]
        values = qkv_ref[0, window, 2 * PAIR :]
        low_pos = low_ref[0, rows, :] - block * TILE
        key_pos = lax.broadcasted_iota(jnp.int32, (TILE, span), 1)
        query_pos = lax.broadcasted_iota(jnp.int32, (TILE, TILE), 0) + WINDOW
        allowed = key_pos >= low_pos
        causal = key_pos[:, WINDOW:] <= query_pos
        mixed = jnp.zeros((TILE, 2 * HD), jnp.float32)
        for half in range(2):
            scores = contract(
                jnp.where(half_mask(queries.shape, half), queries, 0), keys, 1, 1
            )
            early = jnp.where(allowed[:, :WINDOW], scores[:, :WINDOW], masked_score)
            late = jnp.where(allowed[:, WINDOW:] & causal, scores[:, WINDOW:], masked_score)
            top_score = jnp.maximum(
                jnp.max(early, axis=1, keepdims=True), jnp.max(late, axis=1, keepdims=True)
            )
            early = jnp.exp(early - top_score)
            late = jnp.exp(late - top_score)
            row_total = jnp.sum(early, axis=1, keepdims=True) + jnp.sum(
                late, axis=1, keepdims=True
            )
            part = contract(early.astype(jnp.bfloat16), values[:WINDOW], 1, 0) + contract(
                late.astype(jnp.bfloat16), values[WINDOW:], 1, 0
            )
            part = part * (1.0 / row_total)
            mixed = jnp.where(half_mask(mixed.shape, half), part, mixed)
            log_total = top_score + jnp.log(row_total)
            total_ref[0, 0, half : half + 1, rows] = jnp.sum(
                jnp.where(eye, log_total, 0.0), axis=0, keepdims=True
            )
        mixed_ref[0, rows, :] = mixed.astype(jnp.bfloat16)


def attention_forward(packed, low_pos):
    groups, key_len, width = packed.shape
    block_len = low_pos.shape[1]
    pairs = width // (3 * PAIR)
    pick = lambda seq, pair: (seq, 0, pair)
    return pl.pallas_call(
        forward_kernel,
        grid=(groups, pairs),
        in_specs=[
            pl.BlockSpec((1, key_len, 3 * PAIR), pick),
            pl.BlockSpec((1, block_len, 1), lambda seq, pair: (seq, 0, 0)),
        ],
        out_specs=[
            pl.BlockSpec((1, block_len, PAIR), pick),
            pl.BlockSpec((1, 1, 2, block_len), lambda seq, pair: (seq, pair, 0, 0)),
        ],
        out_shape=[
            jax.ShapeDtypeStruct((groups, block_len, pairs * PAIR), jnp.bfloat16),
            jax.ShapeDtypeStruct((groups, pairs, 2, block_len), jnp.float32),
        ],
        compiler_params=pltpu.CompilerParams(vmem_limit_bytes=56 << 20),
        cost_estimate=pl.CostEstimate(
            flops=block_len,
            bytes_accessed=block_len,
            transcendentals=0,
        ),
    )(packed, low_pos[:, :, None])


def backward_kernel(qkv_ref, mixed_ref, grad_ref, total_ref, low_ref, out_ref, gk_sum, gv_sum):
    block_len = mixed_ref.shape[1]
    first = qkv_ref.shape[1] - block_len
    span = WINDOW + TILE
    scale = HD ** (-0.5)
    gk_sum[...] = jnp.zeros_like(gk_sum)
    gv_sum[...] = jnp.zeros_like(gv_sum)
    eye = lax.broadcasted_iota(jnp.int32, (TILE, TILE), 0) == lax.broadcasted_iota(
        jnp.int32, (TILE, TILE), 1
    )
    for block in range(block_len // TILE):
        rows = pl.ds(block * TILE, TILE)
        window = pl.ds(block * TILE, span)
        queries = qkv_ref[0, pl.ds(first + block * TILE, TILE), :PAIR]
        queries = queries * jnp.asarray(scale, jnp.bfloat16)
        keys = qkv_ref[0, window, PAIR : 2 * PAIR]
        values = qkv_ref[0, window, 2 * PAIR :]
        grads = grad_ref[0, rows, :]
        product = grads.astype(jnp.float32) * mixed_ref[0, rows, :].astype(jnp.float32)
        low_pos = low_ref[0, :, rows] - block * TILE
        key_pos = lax.broadcasted_iota(jnp.int32, (span, TILE), 0)
        query_pos = lax.broadcasted_iota(jnp.int32, (TILE, TILE), 1) + WINDOW
        allowed = key_pos >= low_pos
        late_allowed = allowed[WINDOW:] & (key_pos[WINDOW:] <= query_pos)
        keys_t = jnp.transpose(keys)
        gq_parts = []
        for half in range(2):
            mask = half_mask(queries.shape, half)
            q_half = jnp.where(mask, queries, 0)
            g_half = jnp.where(mask, grads, 0)
            delta = jnp.sum(jnp.where(mask, product, 0.0), axis=1, keepdims=True)
            delta = jnp.sum(jnp.where(eye, delta, 0.0), axis=0, keepdims=True)
            log_total = total_ref[0, 0, half : half + 1, rows]
            scores = contract(keys, q_half, 1, 1)
            probs = jnp.concatenate(
                [
                    jnp.where(allowed[:WINDOW], jnp.exp(scores[:WINDOW] - log_total), 0.0),
                    jnp.where(late_allowed, jnp.exp(scores[WINDOW:] - log_total), 0.0),
                ]
            )
            grad_probs = contract(values, g_half, 1, 1)
            grad_scores = (probs * (grad_probs - delta)).astype(jnp.bfloat16)
            gv_sum[window, :] += contract(probs.astype(jnp.bfloat16), g_half, 1, 0)
            gk_sum[window, :] += contract(grad_scores, q_half, 1, 0)
            gq_parts.append(contract(keys_t[half * HD : (half + 1) * HD], grad_scores, 1, 0))
        gq = jnp.transpose(jnp.concatenate(gq_parts)) * scale
        out_ref[0, pl.ds(first + block * TILE, TILE), :PAIR] = gq.astype(jnp.bfloat16)
    out_ref[0, :first, :PAIR] = jnp.zeros((first, PAIR), jnp.bfloat16)
    out_ref[0, :, PAIR : 2 * PAIR] = gk_sum[...].astype(jnp.bfloat16)
    out_ref[0, :, 2 * PAIR :] = gv_sum[...].astype(jnp.bfloat16)


def attention_backward(packed, mixed, grads, log_total, low_pos):
    groups, key_len, width = packed.shape
    block_len = mixed.shape[1]
    pairs = width // (3 * PAIR)
    pick = lambda seq, pair: (seq, 0, pair)
    row_spec = pl.BlockSpec((1, block_len, PAIR), pick)
    packed_spec = pl.BlockSpec((1, key_len, 3 * PAIR), pick)
    return pl.pallas_call(
        backward_kernel,
        grid=(groups, pairs),
        in_specs=[
            packed_spec, row_spec, row_spec,
            pl.BlockSpec((1, 1, 2, block_len), lambda seq, pair: (seq, pair, 0, 0)),
            pl.BlockSpec((1, 1, block_len), lambda seq, pair: (seq, 0, 0)),
        ],
        out_specs=packed_spec,
        out_shape=jax.ShapeDtypeStruct(packed.shape, jnp.bfloat16),
        scratch_shapes=[
            pltpu.VMEM((key_len, PAIR), jnp.float32),
            pltpu.VMEM((key_len, PAIR), jnp.float32),
        ],
        compiler_params=pltpu.CompilerParams(vmem_limit_bytes=56 << 20),
        cost_estimate=pl.CostEstimate(
            flops=block_len,
            bytes_accessed=block_len,
            transcendentals=0,
        ),
    )(packed, mixed, grads, log_total, low_pos[:, None, :])


norm_eps = 1e-05


def mate(value):
    return lax.ppermute(value, "core", [(0, 1), (1, 0)])


def other_tp(value):
    return lax.ppermute(value, "tp", [(0, 1), (1, 0)])


def onward(value):
    count = lax.axis_size("ctx")
    return lax.ppermute(value, "ctx", [(i, i + 1) for i in range(count - 1)])


def backward_step(value):
    count = lax.axis_size("ctx")
    return lax.ppermute(value, "ctx", [(i + 1, i) for i in range(count - 1)])


class Place:
    def __init__(self):
        self.chips = lax.axis_size("x")
        self.core = lax.axis_index("core")
        self.shard = lax.axis_index("x") * 2 + self.core
        self.tp = lax.axis_index("tp")
        self.ctx = lax.axis_index("ctx")
        self.home = self.core == self.tp


def tie(*values):
    return lax.optimization_barrier(values)


def ordered(own, other, position, axis=0):
    return jnp.where(
        position == 0,
        jnp.stack([own, other], axis=axis),
        jnp.stack([other, own], axis=axis),
    )


def join_kernel(core_ref, *refs):
    out_ref = refs[-1]
    own = pl.program_id(1) == core_ref[0]
    at = 0
    for blocks_ref, came_ref in zip(refs[0:-1:2], refs[1:-1:2]):
        width = came_ref.shape[2]

        @pl.when(own)
        def _(at=at, width=width, blocks_ref=blocks_ref):
            out_ref[:, at : at + width] = blocks_ref[0, 0]

        @pl.when(jnp.logical_not(own))
        def _(at=at, width=width, came_ref=came_ref):
            out_ref[:, at : at + width] = came_ref[0]

        at += width


class CoreSwap:
    def __init__(self, blocks, place, column=0, width=None):
        self.place, self.blocks, self.column = place, blocks, column
        width = blocks.shape[3] if width is None else width
        zero = jnp.int32(0)
        other = lax.dynamic_slice(
            blocks,
            (zero, (1 - place.core).astype(jnp.int32), zero, jnp.int32(column * width)),
            (blocks.shape[0], 1, blocks.shape[2], width),
        )
        self.came = mate(other[:, 0])


def join(*swaps):
    chips, rows = swaps[0].came.shape[:2]
    in_specs, operands, total = [], [], 0
    for swap in swaps:
        width = swap.came.shape[2]
        in_specs += [
            pl.BlockSpec(
                (1, 1, rows, width),
                lambda chip, part, core, column=swap.column: (chip, core[0], 0, column),
            ),
            pl.BlockSpec((1, rows, width), lambda chip, part, core: (chip, 0, 0)),
        ]
        operands += [swap.blocks, swap.came]
        total += width
    return pl.pallas_call(
        join_kernel,
        grid_spec=pltpu.PrefetchScalarGridSpec(
            num_scalar_prefetch=1,
            grid=(chips, 2),
            in_specs=in_specs,
            out_specs=pl.BlockSpec((rows, total), lambda chip, part, core: (chip * 2 + part, 0)),
        ),
        out_shape=jax.ShapeDtypeStruct((chips * 2 * rows, total), jnp.bfloat16),
        compiler_params=pltpu.CompilerParams(vmem_limit_bytes=24 << 20),
        cost_estimate=pl.CostEstimate(
            flops=rows, bytes_accessed=rows, transcendentals=0
        ),
    )(swaps[0].place.core.reshape(1).astype(jnp.int32), *operands)


def gather_blocks(piece, place):
    whole = lax.all_gather(piece, ("x", "tp"), axis=0, tiled=False)
    return whole.reshape((place.chips, 2) + piece.shape)


def scatter_swap(grads, place):
    return CoreSwap(grads.reshape(place.chips, 2, -1, grads.shape[1]), place)


def scatter_sum(blocks):
    return lax.psum_scatter(blocks, ("x", "tp"), scatter_dimension=0, tiled=True)


def dot_f32(left_side, right_side):
    return jnp.dot(left_side, right_side, preferred_element_type=jnp.float32)


def dot_first(left_side, right_side):
    return contract(left_side, right_side, 0, 0)


def dot_second(left_side, right_side):
    return contract(left_side, right_side, 1, 1)


def gather_small(value, place):
    if place.chips != 2:
        return lax.all_gather(value, ("x", "core"), axis=1, tiled=True)
    near = mate(value)
    pair = ordered(value, near, place.core, 1).reshape(value.shape[0], -1)
    far = lax.ppermute(pair, "x", [(0, 1), (1, 0)])
    return ordered(pair, far, lax.axis_index("x"), 1).reshape(value.shape[0], -1)


def norm_forward(hidden, norm_gain, norm_shift):
    row_mean = jnp.mean(hidden, axis=-1, keepdims=True)
    centred = hidden - row_mean
    variance = jnp.mean(centred * centred, axis=-1, keepdims=True)
    inv_std = lax.rsqrt(variance + norm_eps)
    norm_hat = centred * inv_std
    return ((norm_hat * norm_gain + norm_shift).astype(jnp.bfloat16), norm_hat, inv_std)


def norm_backward(grad_out, norm_hat, inv_std, norm_gain):
    scaled = grad_out * norm_gain
    mean_one = jnp.mean(scaled, axis=-1, keepdims=True)
    mean_two = jnp.mean(scaled * norm_hat, axis=-1, keepdims=True)
    grad_input = inv_std * (scaled - mean_one - norm_hat * mean_two)
    return (grad_input, jnp.sum(grad_out * norm_hat, axis=0), jnp.sum(grad_out, axis=0))


def wide(value):
    return value.astype(jnp.float32)


def narrow(value):
    return value.astype(jnp.bfloat16)


def pick_block(value, index, count):
    size = value.shape[0] // count
    return lax.dynamic_slice_in_dim(value, index * size, size, 0)


def small_total(value, place):
    if place.chips != 2 or lax.axis_size("ctx") != 4:
        return lax.psum(value, ("x", "core", "ctx", "tp"))
    value = value + mate(value)
    value = value + other_tp(value)
    value = value + lax.ppermute(value, "x", [(0, 1), (1, 0)])
    value = value + lax.ppermute(value, "ctx", [(0, 1), (3, 2)])
    value = value + lax.ppermute(value, "ctx", [(1, 2), (2, 1)])
    outer = (place.ctx == 0) | (place.ctx == 3)
    return jnp.where(outer, lax.ppermute(value, "ctx", [(1, 0), (2, 3)]), value)


def core_sum(own_part, mate_part):
    return own_part + wide(mate(narrow(mate_part)))


def gelu_slope(pre_act, grad_act):
    pullback = jax.vjp(lambda values: jax.nn.gelu(values, approximate=True), pre_act)[1]
    return pullback(grad_act)[0]


def pair_major(value):
    width = value.shape[-1]
    return jnp.concatenate(
        [value[kind, :, at : at + PAIR] for at in range(0, width, PAIR) for kind in range(3)],
        axis=-1,
    )


def pack_kernel(qkv_ref, proj_ref, out_ref):
    width = qkv_ref.shape[3]
    for pair in range(width // PAIR):
        for kind in range(3):
            at = (3 * pair + kind) * PAIR
            out_ref[:, at : at + PAIR] = qkv_ref[0, kind, :, pair * PAIR : (pair + 1) * PAIR]
    out_ref[:, 3 * width :] = jnp.transpose(proj_ref[0])


def attn_piece(layer, qkv_weight, proj_weight):
    rows, width = qkv_weight.shape[2:]
    return pl.pallas_call(
        pack_kernel,
        grid=(1,),
        in_specs=[
            pl.BlockSpec((1, 3, rows, width), lambda step: (layer, 0, 0, 0)),
            pl.BlockSpec((1, width, rows), lambda step: (layer, 0, 0)),
        ],
        out_specs=pl.BlockSpec((rows, 4 * width), lambda step: (0, 0)),
        out_shape=jax.ShapeDtypeStruct((rows, 4 * width), jnp.bfloat16),
        compiler_params=pltpu.CompilerParams(vmem_limit_bytes=24 << 20),
    )(qkv_weight, proj_weight)


def unpack_kernel(first_ref, second_ref, out_ref):
    kind = pl.program_id(0)
    width = out_ref.shape[3]
    for pair in range(width // PAIR):
        at = pl.multiple_of((3 * pair + kind) * PAIR, PAIR)
        for layer, ref in enumerate((first_ref, second_ref)):
            out_ref[layer, 0, :, pair * PAIR : (pair + 1) * PAIR] = ref[
                :, pl.ds(at, PAIR)
            ].astype(jnp.float32)


def unpack_heads(first, second):
    rows, width = first.shape
    width = width // 3
    block = pl.BlockSpec((rows, 3 * width), lambda kind: (0, 0))
    return pl.pallas_call(
        unpack_kernel,
        grid=(3,),
        in_specs=[block, block],
        out_specs=pl.BlockSpec((2, 1, rows, width), lambda kind: (0, kind, 0, 0)),
        out_shape=jax.ShapeDtypeStruct((2, 3, rows, width), jnp.float32),
        compiler_params=pltpu.CompilerParams(vmem_limit_bytes=24 << 20),
    )(first, second)


def per_device(
    tokens,
    cotangent,
    doc_lengths,
    norm_gains,
    norm_biases,
    qkv_weight,
    qv_bias,
    proj_weight,
    fc_weight,
    fc_bias,
    out_weight,
):
    place = Place()
    block_len, model_width = tokens.shape[1:]
    shard_rows = qkv_weight.shape[2]
    half_width = qkv_weight.shape[3]
    layer_count = qkv_weight.shape[0]
    reach = WINDOW // block_len
    key_len = (reach + 1) * block_len
    last = reach * block_len

    def my_seq(value):
        return lax.dynamic_index_in_dim(value, place.tp, 0, False)

    def both_seqs(own, other):
        return ordered(own, other, place.tp)

    own_tokens = my_seq(tokens)
    grad_hidden = wide(my_seq(cotangent))
    bias_parts = jnp.sum(grad_hidden.reshape(16, -1, model_width), axis=1)
    bias_parts = lax.psum(bias_parts, "ctx")
    attn_blocks = gather_blocks(attn_piece(0, qkv_weight, proj_weight), place)
    halo = [onward(own_tokens)]
    for _ in range(reach - 1):
        halo.insert(0, onward(halo[0]))
    vectors = jnp.concatenate([norm_gains, norm_biases], axis=1)
    vectors = gather_small(vectors.reshape(-1, vectors.shape[2]), place)
    vectors = wide(vectors).reshape(layer_count, 6, model_width)
    biases = jnp.concatenate([qv_bias.reshape(layer_count, -1), fc_bias], axis=1)
    biases = wide(jnp.where(place.home, biases, other_tp(biases)))
    lengths = my_seq(doc_lengths)
    lengths = jnp.stack([lengths, mate(lengths)])
    mlp_piece, mlp_later = [
        jnp.concatenate([fc_weight[layer], jnp.transpose(out_weight[layer])], axis=1)
        for layer in range(layer_count)
    ]
    attn_later = attn_piece(1, qkv_weight, proj_weight)
    halo[-1], mlp_piece, mlp_later, attn_later = tie(
        halo[-1], mlp_piece, mlp_later, attn_later
    )
    mlp_blocks = gather_blocks(mlp_piece, place)
    fc_width = fc_weight.shape[2]

    doc_ends = jnp.cumsum(lengths, axis=1)
    first_pos = place.ctx * block_len
    query_pos = first_pos + jnp.arange(block_len, dtype=jnp.int32)
    started = doc_ends[:, None, :] <= query_pos[None, :, None]
    doc_start = jnp.max(jnp.where(started, doc_ends[:, None, :], 0), axis=-1)
    low_pos = jnp.maximum(doc_start, query_pos[None, :] - (WINDOW - 1))
    low_pos = (low_pos - first_pos + last).astype(jnp.int32)

    hidden = wide(own_tokens)
    stash = []
    weights = []
    for layer in range(layer_count):
        gains, shifts = vectors[layer, :2], vectors[layer, 2:]
        bias_q, bias_v = biases[layer, :half_width], biases[layer, half_width : 2 * half_width]
        bias_qkv = pair_major(jnp.stack([bias_q, jnp.zeros_like(bias_q), bias_v])[:, None])
        bias_fc = biases[layer, 2 * half_width :]
        attn_in, hat_attn, inv_attn = norm_forward(hidden, gains[0], shifts[0])
        own_near = [attn_in]
        mate_near = [mate(attn_in)]
        attn_swap = CoreSwap(attn_blocks, place)
        if layer == 0:
            w_attn = join(attn_swap)
        step_value = attn_in
        for index in range(reach):
            if layer == 0:
                part = norm_forward(wide(halo[reach - 1 - index]), gains[0], shifts[0])[0]
            else:
                step_value = part = onward(step_value)
                if index == 0:
                    step_value, mlp_later = tie(step_value, mlp_later)
                    mlp_blocks = gather_blocks(mlp_later, place)
                    part = step_value
                if index == 1:
                    step_value, w_attn = tie(step_value, join(attn_swap))
                    part = step_value
            own_near.insert(0, part)
            mate_near.insert(0, mate(part))
        near = jnp.concatenate(own_near + mate_near)
        if layer == 0:
            near, bias_parts = tie(near, bias_parts)
        w_qkv, w_proj_t = w_attn[:, : 3 * half_width], w_attn[:, 3 * half_width :]
        packed = narrow(dot_f32(near, w_qkv) + bias_qkv).reshape(2, key_len, -1)
        mixed, log_total = attention_forward(packed, low_pos)
        if layer + 1 < layer_count:
            mixed, attn_later = tie(mixed, attn_later)
            attn_blocks = gather_blocks(attn_later, place)
        mate_part = dot_second(mixed[1], w_proj_t)
        own_part = dot_second(mixed[0], w_proj_t)
        middle = hidden + core_sum(own_part, mate_part) + shifts[1]
        mlp_own, hat_mlp, inv_mlp = norm_forward(middle, gains[1], shifts[2])
        mlp_in = jnp.concatenate([mlp_own, mate(mlp_own)])
        mlp_in, mlp_blocks = tie(mlp_in, mlp_blocks)
        w_fc = join(CoreSwap(mlp_blocks, place, 0, fc_width))
        out_swap = CoreSwap(mlp_blocks, place, 1, fc_width)
        pre_act = dot_f32(mlp_in, w_fc) + bias_fc
        activated = narrow(jax.nn.gelu(pre_act, approximate=True))
        w_out_t = join(out_swap)
        mate_part = dot_second(activated[block_len:], w_out_t)
        own_part = dot_second(activated[:block_len], w_out_t)
        hidden = middle + core_sum(own_part, mate_part) + shifts[3]
        weights.append((w_qkv, w_proj_t, w_fc, w_out_t))
        stash.append(
            (near, hat_attn, inv_attn, packed, mixed, log_total, hat_mlp, inv_mlp, mlp_in,
             pre_act, activated)
        )

    own_output = narrow(hidden)
    last_sum = None
    sums = {}
    waiting, latest, first_sum = [], [], []
    small_parts = [None] * layer_count

    def advance(value, name):
        nonlocal last_sum
        share = waiting.pop(0)
        assert share[0] == name
        value, share, last_sum = tie(value, share[1], last_sum)
        if latest:
            sums[latest[0]] = last_sum
        else:
            first_sum.append(last_sum)
        latest[:] = [name]
        last_sum = lax.psum(share, "ctx")
        sums[name] = last_sum
        return value

    def settle(value, name):
        assert waiting[0][0] == name
        value, share = tie(value, waiting[0][1])
        waiting[0] = (name, share)
        return value

    for layer in reversed(range(layer_count)):
        near, hat_attn, inv_attn, packed, mixed, log_total = stash[layer][:6]
        hat_mlp, inv_mlp, mlp_in, pre_act, activated = stash[layer][6:]
        gains = vectors[layer, :2]
        w_qkv, w_proj_t, w_fc, w_out_t = weights[layer]
        final = layer == 0
        grad_out_bias = jnp.sum(grad_hidden, axis=0)
        if not final:
            last_sum = bias_parts
        grad_low = narrow(grad_hidden)
        grad_low = jnp.concatenate([grad_low, mate(grad_low)])
        out_swap = scatter_swap(narrow(dot_first(grad_low, activated)), place)
        grad_act_in = grad_low
        if not final:
            grad_act_in, grad_out = tie(grad_low, join(out_swap))
            waiting.append(("out%d" % layer, scatter_sum(grad_out)))
        grad_pre = narrow(gelu_slope(pre_act, dot_f32(grad_act_in, w_out_t)))
        grad_fc_bias = jnp.sum(wide(grad_pre), axis=0)
        mate_part = dot_second(grad_pre[block_len:], w_fc)
        own_part = dot_second(grad_pre[:block_len], w_fc)
        grad_norm_in = core_sum(own_part, mate_part)
        if final:
            grad_norm_in, grad_out = tie(grad_norm_in, join(out_swap))
            (grad_norm_in, grad_out) = settle((grad_norm_in, grad_out), "attn1")
            share = jnp.concatenate([early_share, waiting.pop(0)[1]], axis=1)
            waiting.insert(0, ("first", share))
            grad_norm_in = advance(grad_norm_in, "first")
            waiting.append(("out%d" % layer, scatter_sum(grad_out)))
        fc_swap = scatter_swap(narrow(dot_first(mlp_in, grad_pre)), place)
        grad_from_mlp, grad_gain_mlp, grad_shift_mlp = norm_backward(
            grad_norm_in, hat_mlp, inv_mlp, gains[1]
        )
        grad_middle = grad_hidden + grad_from_mlp
        grad_proj_bias = jnp.sum(grad_middle, axis=0)
        grad_low = narrow(grad_middle)
        grad_low = jnp.concatenate([grad_low, mate(grad_low)])
        grad_mixed = narrow(dot_f32(grad_low, w_proj_t)).reshape(mixed.shape)
        proj_swap = scatter_swap(
            narrow(dot_first(grad_low, mixed.reshape(2 * block_len, half_width))), place
        )
        grad_mixed, fc_swap.came, proj_swap.came = tie(grad_mixed, fc_swap.came, proj_swap.came)
        grad_mixed, grad_fc = tie(grad_mixed, join(fc_swap, proj_swap))
        if not final:
            grad_mixed = advance(grad_mixed, "out%d" % layer)
        grad_packed = attention_backward(packed, mixed, grad_mixed, log_total, low_pos)
        if final:
            grad_packed, far_output, grad_fc = tie(grad_packed, far_output, grad_fc)
            grad_packed, grad_fc = settle((grad_packed, grad_fc), "out%d" % layer)
        else:
            grad_mixed, grad_fc = tie(grad_mixed, grad_fc)
        waiting.append(("fc%d" % layer, scatter_sum(grad_fc)))
        mate_part = dot_second(grad_packed[1], w_qkv)
        own_part = dot_second(grad_packed[0], w_qkv)
        grad_near = core_sum(own_part, mate_part)
        far_total, grad_attn_in = grad_near[:last], grad_near[last:]
        rows = grad_packed.reshape(2 * key_len, -1)
        grad_near, rows = tie(grad_near, rows)
        if final:
            grad_near = advance(grad_near, "out%d" % layer)
        far_total, grad_attn_in = grad_near[:last], grad_near[last:]
        carried = backward_step(narrow(far_total[:block_len]))
        grad_qkv = narrow(dot_first(near, rows))
        grad_bias = jnp.sum(wide(rows), axis=0)
        if final:
            attn_swap = scatter_swap(grad_qkv, place)
        for step in range(1, reach + 1):
            if step == 1 and not final:
                carried, grad_qkv, last_sum = tie(carried, grad_qkv, last_sum)
                attn_swap = scatter_swap(grad_qkv, place)
            if step == 1 and final:
                carried, grad_attn = tie(carried, join(attn_swap))
                carried, grad_attn = settle((carried, grad_attn), "fc%d" % layer)
                waiting.append(("attn%d" % layer, scatter_sum(grad_attn)))
                carried = advance(carried, "fc%d" % layer)
            if step == 2 and not final:
                carried, grad_bias, grad_attn, own_output = tie(
                    carried, grad_bias, join(attn_swap), own_output
                )
                far_output = other_tp(own_output)
                carried, grad_attn = settle((carried, grad_attn), "fc%d" % layer)
                early_share = waiting.pop(0)[1]
                waiting.append(("attn%d" % layer, scatter_sum(grad_attn)))
            if step == 2 and final:
                carried, grad_bias = tie(carried, grad_bias)
                carried = advance(carried, "attn%d" % layer)
            arrived = wide(carried)
            if step < reach:
                section = far_total[step * block_len : (step + 1) * block_len]
                carried = backward_step(narrow(arrived + section))
            else:
                grad_attn_in = grad_attn_in + arrived
        grad_from_attn, grad_gain_attn, grad_shift_attn = norm_backward(
            grad_attn_in, hat_attn, inv_attn, gains[0]
        )
        grad_hidden = grad_middle + grad_from_attn
        grad_bias = grad_bias.reshape(-1, 3, PAIR)
        halves = jnp.concatenate(
            [grad_bias[:, 0].reshape(-1), grad_bias[:, 2].reshape(-1), grad_fc_bias]
        )
        empty = jnp.zeros_like(halves)
        if not final:
            grad_out_bias = jnp.where(place.ctx == 0, jnp.sum(first_sum[0], axis=0), 0.0)
        small_parts[layer] = jnp.concatenate(
            [
                grad_gain_attn, grad_gain_mlp,
                grad_shift_attn, grad_proj_bias, grad_shift_mlp, grad_out_bias,
                jnp.where(place.core == 0, halves, empty),
                jnp.where(place.core == 1, halves, empty),
            ]
        )

    small = small_total(jnp.stack(small_parts), place)
    far_grad = wide(other_tp(narrow(grad_hidden)))
    token_grad = both_seqs(grad_hidden, far_grad)
    split = 6 * model_width
    norms = small[:, :split].reshape(layer_count, 6, model_width)
    norms = lax.dynamic_slice_in_dim(norms, place.shard * shard_rows, shard_rows, 2)
    halves = small[:, split:].reshape(layer_count, 2, -1)
    halves = lax.dynamic_index_in_dim(halves, place.tp, 1, False)
    split = fc_width + half_width
    attn = [sums["attn0"], sums["first"][:, split:]]
    fc_proj = [sums["fc0"], sums["first"][:, :split]]
    return (
        both_seqs(own_output, far_output),
        token_grad,
        norms[:, :2],
        norms[:, 2:],
        unpack_heads(*attn),
        halves[:, : 2 * half_width].reshape(layer_count, 2, half_width),
        jnp.stack([jnp.transpose(wide(v[:, fc_width:])) for v in fc_proj]),
        jnp.stack([wide(v[:, :fc_width]) for v in fc_proj]),
        halves[:, 2 * half_width :],
        jnp.stack([jnp.transpose(wide(sums["out%d" % layer])) for layer in range(layer_count)]),
    )


def solution(mesh):
    devices = mesh.devices
    devices = devices.reshape((devices.shape[0] // 2, 2) + devices.shape[1:])
    mesh = jax.sharding.Mesh(devices, ("x", "core", "ctx", "tp"))
    placed = (
        P(("x", "core"), "ctx", None),
        P(("x", "core"), "ctx", None),
        P(("x", "core"), None),
        P(None, None, ("x", "core")),
        P(None, None, ("x", "core")),
        P(None, None, ("x", "core"), "tp"),
        P(None, None, "tp"),
        P(None, "tp", ("x", "core")),
        P(None, ("x", "core"), "tp"),
        P(None, "tp"),
        P(None, "tp", ("x", "core")),
    )
    return jax.shard_map(
        per_device,
        mesh=mesh,
        in_specs=placed,
        out_specs=(
            P(("x", "core"), "ctx", None),
            P(("x", "core"), "ctx", None),
            P(None, None, ("x", "core")),
            P(None, None, ("x", "core")),
            P(None, None, ("x", "core"), "tp"),
            P(None, None, "tp"),
            P(None, "tp", ("x", "core")),
            P(None, ("x", "core"), "tp"),
            P(None, "tp"),
            P(None, "tp", ("x", "core")),
        ),
        check_vma=False,
    )
```
